256 devices in a mesh: lat: 16 (over x, y_hi, core), lon: 16 (over y_lo, z).
Axes of the slice: x: 4, y: 4 (y_hi: 2, y_lo: 2; y = y_hi * 2 + y_lo), z: 8, core: 2. Of those that a mesh axis runs over, the one named last changes fastest.
Arguments:
- tokens: bfloat16 [4, 192, 192, 192], P(None, 'lat', 'lon'), may hold values from -6 to 6
- cotangent: bfloat16 [4, 192, 192, 192], P(None, 'lat', 'lon'), may hold values from -6 to 6
- w_qkv: bfloat16 [2, 192, 576], replicated, may hold values from -0.4375 to 0.4375
- w_proj: bfloat16 [2, 192, 192], replicated, may hold values from -0.4375 to 0.4375
- w_in: bfloat16 [2, 192, 768], replicated, may hold values from -0.4375 to 0.4375
- w_out: bfloat16 [2, 768, 192], replicated, may hold values from -0.21875 to 0.21875
- earth_bias: bfloat16 [2, 2, 32, 6, 20736], P(None, None, 'lat'), may hold values from -4 to 4
Outputs:
- d_tokens: bfloat16 [4, 192, 192, 192], P(None, 'lat', 'lon')
- d_qkv: float32 [2, 192, 576], replicated
- d_proj: float32 [2, 192, 192], replicated
- d_bias: float32 [2, 2, 32, 6, 20736], P(None, None, 'lat')
The draws below stay inside these ranges and needn't reach their ends.
All inputs are finite; a program needn't handle non-finite values.
Results may differ from the reference program's by a relative error of at most 0.028.
Values may be sent and summed in bfloat16 or wider, within the bound.
A program may use at most 128 MiB of HBM per device.

```python
import jax
import jax.numpy as jnp
from jax import lax

C = 192
HEADS = 6
FF = 768
WZ = 2
WLAT = 6
WLON = 12
LEVELS = 4
WIN = 144
LAT = 192
LON = 192
ZWIN = 2
LATWIN = 32


def shard_levels(key, extent, shards, least, top_value):
    level = 1.0
    for position, shards_of in shards:
        steps = jax.random.uniform(jax.random.fold_in(jax.random.fold_in(key, 6), position), (shards_of,), jnp.float32, least / len(shards), top_value / len(shards))
        level = level * jnp.repeat(jnp.exp(steps), extent[position] // shards_of).reshape((-1,) + (1,) * (len(extent) - 1 - position))
    return level


def bell_draw(rng, shape, scale, limit, split=(), kind=jnp.bfloat16):
    drawn = jax.random.normal(rng, shape, jnp.float32) * scale
    if len(split) > 0:
        drawn = shard_levels(rng, shape, split, -0.22, 0.18) * drawn
    return jnp.clip(drawn, min=-limit, max=limit).astype(kind)


def setup_inputs(seed: int = 0) -> dict:
    key_of = jax.random.split(jax.random.key(seed), 8)
    tokens = bell_draw(key_of[0], (LEVELS, LAT, LON, C), 1.0, 6.0, ((1, 16), (2, 16)))
    cotangent = bell_draw(key_of[1], (LEVELS, LAT, LON, C), 1.0, 6.0, ((1, 16), (2, 16)))
    w_qkv = bell_draw(key_of[2], (2, C, 3 * C), C ** -0.5, 0.4375)
    w_proj = bell_draw(key_of[3], (2, C, C), C ** -0.5, 0.4375)
    w_in = bell_draw(key_of[4], (2, C, FF), C ** -0.5, 0.4375)
    w_out = bell_draw(key_of[5], (2, FF, C), FF ** -0.5, 0.21875)
    earth_bias = bell_draw(key_of[6], (2, ZWIN, LATWIN, HEADS, WIN * WIN), 1.0, 4.0, ((2, 16),))
    return dict(tokens=tokens, cotangent=cotangent, w_qkv=w_qkv, w_proj=w_proj, w_in=w_in, w_out=w_out, earth_bias=earth_bias)


EPSILON = 1e-05

def layer_norm(values):
    center = lax.optimization_barrier(jnp.mean(values, axis=-1, keepdims=True))
    offset = values - center
    spread = lax.optimization_barrier(jnp.mean(offset * offset, axis=-1, keepdims=True))
    return offset * lax.rsqrt(spread + EPSILON)

def norm_back(inputs, upstream):
    return jax.vjp(layer_norm, inputs.astype(jnp.float32))[1](upstream)[0]

def exact_gelu(values):
    return jax.nn.gelu(values, approximate=False)

def project(grid_in, matrix):
    flat_in = grid_in.reshape(-1, grid_in.shape[-1])
    result = jnp.dot(flat_in, matrix, preferred_element_type=jnp.float32)
    return result.reshape(grid_in.shape[:-1] + (matrix.shape[1],))

def to_windows(grid_in):
    levels, lat_rows, lon_cols, feature_dim = grid_in.shape
    parted = grid_in.reshape(levels // WZ, WZ, lat_rows // WLAT, WLAT, lon_cols // WLON, WLON, feature_dim)
    parted = parted.transpose(0, 2, 4, 1, 3, 5, 6)
    return parted.reshape(levels // WZ, lat_rows // WLAT, lon_cols // WLON, WZ * WLAT * WLON, feature_dim)

def from_windows(windows):
    level_win, lat_win, lon_win, win_tokens, feature_dim = windows.shape
    parted = windows.reshape(level_win, lat_win, lon_win, WZ, WLAT, WLON, feature_dim)
    parted = parted.transpose(0, 3, 1, 4, 2, 5, 6)
    return parted.reshape(level_win * WZ, lat_win * WLAT, lon_win * WLON, feature_dim)

def shift_mask(lat_start, lat_windows, total_lat):
    token_ids = jnp.arange(WZ * WLAT * WLON, dtype=jnp.int32)
    level_pos = token_ids // (WLAT * WLON)
    row_pos = token_ids // WLON % WLAT
    level_win = jnp.arange(LEVELS // WZ, dtype=jnp.int32)[:, None, None]
    lat_win = jnp.arange(lat_windows, dtype=jnp.int32)[None, :, None]
    level_orig = (level_win * WZ + level_pos + WZ // 2) % LEVELS
    level_first = (level_win * WZ + WZ // 2) % LEVELS
    lat_orig = (lat_start + lat_win * WLAT + row_pos + WLAT // 2) % total_lat
    lat_first = (lat_start + lat_win * WLAT + WLAT // 2) % total_lat
    region = (level_orig < level_first).astype(jnp.int32) * 2 + (lat_orig < lat_first).astype(jnp.int32)
    return (region[..., :, None] == region[..., None, :]).astype(jnp.float32)

def split_heads(windows):
    leading = windows.shape[:-2]
    win_tokens = windows.shape[-2]
    model_dim = windows.shape[-1] // 3
    head_dim = model_dim // HEADS
    split_qkv = windows.astype(jnp.float32).reshape(leading + (win_tokens, 3, HEADS, head_dim))
    return (split_qkv[..., 0, :, :], split_qkv[..., 1, :, :], split_qkv[..., 2, :, :], head_dim ** (-0.5))

def attend(windows, bias_table, region_mask):
    query_part, key_part, value_part, score_scale = split_heads(windows)
    scores = jnp.einsum('...qhd,...khd->...hqk', query_part, key_part) * score_scale + bias_table
    weights = jnp.exp(scores)
    if region_mask is not None:
        weights = weights * region_mask
    probabilities = weights / lax.optimization_barrier(jnp.sum(weights, axis=-1, keepdims=True))
    rounded = lax.optimization_barrier(probabilities.astype(jnp.bfloat16)).astype(jnp.float32)
    mixed_out = jnp.einsum('...hqk,...khd->...qhd', rounded, value_part)
    shape_out = windows.shape[:-1] + (windows.shape[-1] // 3,)
    return (probabilities, mixed_out.reshape(shape_out).astype(jnp.bfloat16))

def attend_back(windows, probabilities, mixed_grad):
    query_part, key_part, value_part, score_scale = split_heads(windows)
    grad_heads = mixed_grad.astype(jnp.float32).reshape(query_part.shape)
    rounded = lax.optimization_barrier(probabilities.astype(jnp.bfloat16)).astype(jnp.float32)
    prob_grad = jnp.einsum('...qhd,...khd->...hqk', grad_heads, value_part)
    value_grad = jnp.einsum('...hqk,...qhd->...khd', rounded, grad_heads)
    score_grad = probabilities * (prob_grad - lax.optimization_barrier(jnp.sum(prob_grad * probabilities, axis=-1, keepdims=True)))
    score_round = lax.optimization_barrier(score_grad.astype(jnp.bfloat16)).astype(jnp.float32)
    query_grad = jnp.einsum('...hqk,...khd->...qhd', score_round, key_part) * score_scale
    key_grad = jnp.einsum('...hqk,...qhd->...khd', score_round, query_part) * score_scale
    stacked = jnp.stack([query_grad, key_grad, value_grad], axis=-3)
    return (stacked.reshape(windows.shape).astype(jnp.bfloat16), score_grad)

def mlp_forward(middle, w_in_b, w_out_b):
    normed = layer_norm(middle.astype(jnp.float32)).astype(jnp.bfloat16)
    hidden = exact_gelu(project(normed, w_in_b)).astype(jnp.bfloat16)
    return (middle.astype(jnp.float32) + project(hidden, w_out_b)).astype(jnp.bfloat16)

def mlp_back(middle, upstream, w_in_b, w_out_b):
    normed = layer_norm(middle.astype(jnp.float32)).astype(jnp.bfloat16)
    pre_act = project(normed, w_in_b)
    act_grad = project(upstream, w_out_b.T)
    pre_grad = jax.vjp(exact_gelu, pre_act)[1](act_grad)[0].astype(jnp.bfloat16)
    normed_grad = project(pre_grad, w_in_b.T)
    return (upstream.astype(jnp.float32) + norm_back(middle, normed_grad)).astype(jnp.bfloat16)

def split_rows(grid_in):
    levels, lat_rows, lon_cols, feature_dim = grid_in.shape
    return grid_in.reshape(levels, lat_rows // WLAT, WLAT, lon_cols, feature_dim).transpose(1, 0, 2, 3, 4)

def join_rows(stacked):
    blocks, levels, band_rows, lon_cols, feature_dim = stacked.shape
    return stacked.transpose(1, 0, 2, 3, 4).reshape(levels, blocks * band_rows, lon_cols, feature_dim)

def by_rows(function, *arrays_in):
    pieces = tuple((split_rows(array_in) for array_in in arrays_in))
    return join_rows(lax.map(lambda item_set: function(*item_set), pieces))

def mix_rows(source_rows, bias_row, row_index, w_qkv_b, region_on):
    qkv = project(source_rows, w_qkv_b).astype(jnp.bfloat16)
    windows = to_windows(qkv)[:, 0]
    region_mask = None
    if region_on:
        region_mask = shift_mask(row_index * WLAT, 1, LAT)[:, 0][:, None, None]
    probabilities, mixed_out = attend(windows, bias_row[:, None], region_mask)
    return (windows, probabilities, from_windows(mixed_out[:, None]))

def reference(tokens, cotangent, w_qkv, w_proj, w_in, w_out, earth_bias):
    rolls = (-(WZ // 2), -(WLAT // 2), -(WLON // 2))
    unrolls = (WZ // 2, WLAT // 2, WLON // 2)
    bias_square = earth_bias.astype(jnp.float32).reshape(2, ZWIN, LATWIN, HEADS, WIN, WIN)
    bias_rows = bias_square.transpose(0, 2, 1, 3, 4, 5)
    row_ids = jnp.arange(LAT // WLAT, dtype=jnp.int32)

    def attention_out(source, layer, region_on):

        def step(item_set):
            source_rows, bias_row, row_index = item_set
            windows, probabilities, mixed_rows = mix_rows(source_rows, bias_row, row_index, w_qkv[layer], region_on)
            return project(mixed_rows, w_proj[layer]).astype(jnp.bfloat16)
        return join_rows(lax.map(step, (split_rows(source), bias_rows[layer], row_ids)))

    def block_forward(inputs, layer, region_on):
        normed = layer_norm(inputs.astype(jnp.float32)).astype(jnp.bfloat16)
        source = jnp.roll(normed, rolls, (0, 1, 2)) if region_on else normed
        attended = attention_out(source, layer, region_on)
        if region_on:
            attended = jnp.roll(attended, unrolls, (0, 1, 2))
        return (inputs.astype(jnp.float32) + attended.astype(jnp.float32)).astype(jnp.bfloat16)

    def block_backward(inputs, middle, upstream, layer, region_on):
        middle_grad = by_rows(lambda mid_rows, up_rows: mlp_back(mid_rows, up_rows, w_in[layer], w_out[layer]), middle, upstream)
        normed = layer_norm(inputs.astype(jnp.float32)).astype(jnp.bfloat16)
        source = jnp.roll(normed, rolls, (0, 1, 2)) if region_on else normed
        attn_grad = jnp.roll(middle_grad, rolls, (0, 1, 2)) if region_on else middle_grad

        def step(item_set):
            source_rows, grad_rows, bias_row, row_index = item_set
            windows, probabilities, mixed_rows = mix_rows(source_rows, bias_row, row_index, w_qkv[layer], region_on)
            proj_grad = jnp.dot(mixed_rows.reshape(-1, C).T, grad_rows.reshape(-1, C), preferred_element_type=jnp.float32)
            mixed_grad = project(grad_rows, w_proj[layer].T).astype(jnp.bfloat16)
            window_grad, score_grad = attend_back(windows, probabilities, to_windows(mixed_grad)[:, 0])
            qkv_grad = from_windows(window_grad[:, None])
            qkv_weight_grad = jnp.dot(source_rows.reshape(-1, C).T, qkv_grad.reshape(-1, 3 * C), preferred_element_type=jnp.float32)
            source_grad = project(qkv_grad, w_qkv[layer].T).astype(jnp.bfloat16)
            return (source_grad, lax.optimization_barrier(jnp.sum(score_grad, axis=1)), proj_grad, qkv_weight_grad)
        source_grad, bias_grad, proj_grad, qkv_weight_grad = lax.map(step, (split_rows(source), split_rows(attn_grad), bias_rows[layer], row_ids))
        normed_grad = join_rows(source_grad)
        if region_on:
            normed_grad = jnp.roll(normed_grad, unrolls, (0, 1, 2))
        input_grad = (middle_grad.astype(jnp.float32) + norm_back(inputs, normed_grad.astype(jnp.float32))).astype(jnp.bfloat16)
        return (input_grad, bias_grad.transpose(1, 0, 2, 3, 4), lax.optimization_barrier(jnp.sum(proj_grad, axis=0)), lax.optimization_barrier(jnp.sum(qkv_weight_grad, axis=0)))
    first_mid = block_forward(tokens, 0, False)
    hidden_one = by_rows(lambda mid_rows: mlp_forward(mid_rows, w_in[0], w_out[0]), first_mid)
    second_mid = block_forward(hidden_one, 1, True)
    grad_one, bias_one, proj_one, qkv_one = block_backward(hidden_one, second_mid, cotangent, 1, True)
    grad_zero, bias_zero, proj_zero, qkv_zero = block_backward(tokens, first_mid, grad_one, 0, False)
    bias_total = jnp.stack([bias_zero, bias_one]).reshape(2, ZWIN, LATWIN, HEADS, WIN * WIN)
    return (grad_zero, jnp.stack([qkv_zero, qkv_one]), jnp.stack([proj_zero, proj_one]), bias_total)
```

```python
import functools

import jax
import jax.numpy as jnp
import numpy as np
from jax import lax
from jax.experimental import pallas as pl
from jax.experimental.pallas import tpu as pltpu
from jax.sharding import PartitionSpec as P

F32 = jnp.float32
BF16 = jnp.bfloat16
C = 192
HEADS = 6
HD = 32
FF = 768
WIN = 144
TOK = 576
EPSILON = 1e-05
SCALE = HD ** (-0.5)
MESH = pl.DeviceIdType.MESH
E0, S0, D0, SEND = 0, 224, 304, 384
ONCE = pl.Buffered(1)
VMEM_LIMIT = 56 * 1024 * 1024


def _plain_index(level, row, col):
    window = (level // 2) * 2 + row // 6
    return window * WIN + (level % 2) * 72 + (row % 6) * 12 + col


def _matrices():
    load = np.zeros((TOK, 768), np.float32)
    own = np.zeros((TOK, TOK), np.float32)
    send = np.zeros((SEND, TOK), np.float32)
    recv = np.zeros((TOK, SEND), np.float32)
    for level in range(4):
        for row in range(12):
            for col in range(12):
                here = _plain_index(level, row, col)
                load[here, (level * 12 + row) * 16 + col] = 1
                target_row, target_col = row - 3, col - 6
                target = _plain_index((level - 1) % 4, target_row % 12, target_col % 12)
                if target_row >= 0 and target_col >= 0:
                    own[target, here] = 1
                    continue
                if target_row >= 0:
                    slot = E0 + (level * 9 + row - 3) * 6 + col
                elif target_col >= 0:
                    slot = S0 + (level * 3 + row) * 6 + col - 6
                else:
                    slot = D0 + (level * 3 + row) * 6 + col
                send[slot, here] = 1
                recv[target, slot] = 1
    return load, own, send, recv


def nn(a, b):
    return jnp.dot(a, b, preferred_element_type=F32)


def nt(a, b):
    return lax.dot_general(a, b, (((1,), (1,)), ((), ())), preferred_element_type=F32)


def eye(n):
    rows = lax.broadcasted_iota(jnp.int32, (n, n), 0)
    cols = lax.broadcasted_iota(jnp.int32, (n, n), 1)
    return jnp.where(rows == cols, 1.0, 0.0).astype(BF16)


def flip(a, n):
    return nt(eye(n), a).astype(BF16)


def normalize(x):
    center = jnp.mean(x, axis=-1, keepdims=True)
    offset = x - center
    spread = jnp.mean(offset * offset, axis=-1, keepdims=True)
    inverse = lax.rsqrt(spread + EPSILON)
    return offset * inverse, inverse


def norm_back(x, upstream):
    normed, inverse = normalize(x)
    first = jnp.mean(upstream, axis=-1, keepdims=True)
    second = jnp.mean(upstream * normed, axis=-1, keepdims=True)
    return inverse * (upstream - first - normed * second)


def cumulative(x):
    return 0.5 * (1.0 + lax.erf(x * 0.7071067811865476))


def density(x):
    return 0.3989422804014327 * jnp.exp(-0.5 * x * x)


def rows_of(window):
    return pl.ds(pl.multiple_of(window * WIN, WIN), WIN)


def spread_bias(bias_ref, window, main, rest):
    def step(group, carry):
        block = bias_ref[
            0, window // 2, window % 2, :, pl.ds(pl.multiple_of(group * 1152, 128), 1152)
        ].astype(F32)
        for r in range(8):
            at = pl.ds(pl.multiple_of(group * 64, 64) + 8 * r, 6)
            main[at, :] = block[:, WIN * r : WIN * r + 128]
            rest[at, 0:16] = block[:, WIN * r + 128 : WIN * r + WIN]
        return carry

    lax.fori_loop(0, 18, step, 0)


def head_bias(main, rest, head):
    left = main[pl.ds(head, WIN, stride=8), :]
    right = rest[pl.ds(head, WIN, stride=8), :]
    return jnp.concatenate([left, right[:, :16]], axis=1)


def attention_forward(window, qkv_ref, qkvt_ref, prob_ref, mixedt_ref, mixed_ref, bias_ref, main, rest, mask):
    qkv = qkv_ref[rows_of(window), :]
    qkvt_ref[window] = flip(qkv, 3 * C)
    spread_bias(bias_ref, window, main, rest)
    for head in range(HEADS):
        lo = head * HD
        keys = qkvt_ref[window, C + lo : C + lo + HD, :]
        values = qkvt_ref[window, 2 * C + lo : 2 * C + lo + HD, :]
        scores = nn(qkv[:, lo : lo + HD], keys) * SCALE + head_bias(main, rest, head)
        weights = jnp.exp(scores)
        if mask is not None:
            weights = weights * mask
        probs = weights / jnp.sum(weights, axis=-1, keepdims=True)
        prob_ref[window * HEADS + head] = probs
        mixedt_ref[window, lo : lo + HD, :] = nt(values, probs.astype(BF16)).astype(BF16)
    mixed_ref[rows_of(window), :] = flip(mixedt_ref[window], WIN)


def attention_backward(
    window, source_ref, qkv_ref, qkvt_ref, prob_ref, mixedt_ref, mgrad_ref, grad_ref,
    w_qkv, w_proj, gradt, sgrad_ref, wgrad, main, rest,
):
    mgrad = mgrad_ref[rows_of(window), :]
    wgrad[:, 3 * C :] += nn(mixedt_ref[window], mgrad)
    grad = grad_ref[rows_of(window), :]
    gt = nt(w_proj, mgrad).astype(BF16)
    for head in range(HEADS):
        lo = head * HD
        queries = qkvt_ref[window, lo : lo + HD, :]
        keys = qkvt_ref[window, C + lo : C + lo + HD, :]
        values = qkvt_ref[window, 2 * C + lo : 2 * C + lo + HD, :]
        probs = prob_ref[window * HEADS + head]
        pgrad = nn(grad[:, lo : lo + HD], values)
        vgrad = nn(gt[lo : lo + HD, :], probs.astype(BF16))
        delta = jnp.sum(pgrad * probs, axis=-1, keepdims=True)
        sgrad = probs * (pgrad - delta)
        at = pl.ds(window * HEADS + head, WIN, stride=24)
        main[at, :] = sgrad[:, :128]
        rest[at, :] = jnp.concatenate([sgrad[:, 128:], jnp.zeros((WIN, 112), F32)], axis=1)
        sround = sgrad.astype(BF16)
        gradt[lo : lo + HD, :] = (nt(keys, sround) * SCALE).astype(BF16)
        gradt[C + lo : C + lo + HD, :] = (nn(queries, sround) * SCALE).astype(BF16)
        gradt[2 * C + lo : 2 * C + lo + HD, :] = vgrad.astype(BF16)
    all_grad = gradt[...]
    sourcet = flip(source_ref[rows_of(window), :], C)
    wgrad[:, : 3 * C] += nt(sourcet, all_grad)
    sgradt = nn(w_qkv, all_grad).astype(BF16)
    sgrad_ref[rows_of(window), :] = flip(sgradt, WIN)


def pack_bias(main, rest, out_ref):
    def flat(first):
        parts = []
        for r in range(8):
            at = pl.ds(pl.multiple_of(first * 192, 8) + 24 * r, 24)
            parts += [main[at, :], rest[at, :][:, :16]]
        return jnp.concatenate(parts, axis=1)

    def step(group, carry):
        top = flat(group)
        bottom = flat(group + 9)
        for third in range(3):
            both = jnp.concatenate(
                [top[8 * third : 8 * third + 8], bottom[8 * third : 8 * third + 8]], axis=0
            ).astype(BF16)
            for j in range(9):
                out_ref[third * 81 + group * 9 + j] = both[:, 128 * j : 128 * j + 128]
        return carry

    lax.fori_loop(0, 9, step, 0)
    out_ref[243:256] = jnp.zeros((13, 16, 128), BF16)


def pack_weights(wgrad, out_ref):
    for i in range(12):
        block = wgrad[16 * i : 16 * i + 16, :].astype(BF16)
        for j in range(6):
            out_ref[6 * i + j] = block[:, 128 * j : 128 * j + 128]


def mlp_back(middle, upstream, slope, w_in, w_out):
    act_grad = nt(upstream, w_out)
    pre_grad = (slope * act_grad).astype(BF16)
    ngrad = nt(pre_grad, w_in)
    return (upstream.astype(F32) + norm_back(middle.astype(F32), ngrad)).astype(BF16)


def load_grid(grid_ref, pad, matrix):
    for i in range(48):
        pad[16 * i : 16 * i + 12, :] = grid_ref[i]
    return nn(matrix, pad[...]).astype(BF16)


def forward_kernel(
    tok_ref, cot_ref, load_ref, own_ref, send_ref, w_qkv, w_proj, w_in, w_out, bias_ref,
    x_out, source_out, qkv_out, qkvt_out, prob_out, mixedt_out, mid_out, slope_out, kept_out, sent_out,
    pad, mixed, main, rest,
):
    pad[...] = jnp.zeros_like(pad)
    cot = load_grid(cot_ref, pad, load_ref[...])
    kept_out[1] = nn(own_ref[...], cot).astype(BF16)
    sent_out[1] = nn(send_ref[...], cot).astype(BF16)
    x = load_grid(tok_ref, pad, load_ref[...])
    x_out[...] = x
    x = x.astype(F32)
    source = normalize(x)[0].astype(BF16)
    source_out[...] = source
    qkv_out[...] = nn(source, w_qkv[0]).astype(BF16)

    def step(window, carry):
        attention_forward(
            window, qkv_out, qkvt_out, prob_out, mixedt_out, mixed, bias_ref, main, rest, None
        )
        return carry

    lax.fori_loop(0, 4, step, 0)
    attended = nn(mixed[...], w_proj[0]).astype(BF16)
    middle = (x + attended.astype(F32)).astype(BF16)
    mid_out[...] = middle
    middle = middle.astype(F32)
    pre = nn(normalize(middle)[0].astype(BF16), w_in[0])
    phi = cumulative(pre)
    slope_out[...] = phi + pre * density(pre)
    hidden = (pre * phi).astype(BF16)
    x1 = (middle + nn(hidden, w_out[0])).astype(BF16)
    kept_out[0] = nn(own_ref[...], x1).astype(BF16)
    sent_out[0] = nn(send_ref[...], x1).astype(BF16)


def region_mask(window):
    last_lat = lax.axis_index("lat") == lax.axis_size("lat") - 1

    def region(tokens):
        level = tokens // 72
        row = tokens // 12 % 6
        upper = jnp.where(window // 2 == 1, level, 0)
        lower = jnp.where(jnp.logical_and(last_lat, window % 2 == 1), row // 3, 0)
        return upper * 2 + lower

    queries = region(lax.broadcasted_iota(jnp.int32, (WIN, WIN), 0))
    keys = region(lax.broadcasted_iota(jnp.int32, (WIN, WIN), 1))
    return jnp.where(queries == keys, 1.0, 0.0)


def middle_kernel(
    kept_ref, arrived_ref, recv_ref, send2_ref, own2_ref, w_qkv, w_proj, w_in, w_out, bias_ref,
    kept_out, sent_out, tiles_out, wtiles_out,
    source, qkv, qkvt, prob, mixedt, mixed, mgrad, grad, gradt, sgrad, wgrad, main, rest, main24, rest24,
):
    x = (kept_ref[0].astype(F32) + nn(recv_ref[...], arrived_ref[0])).astype(BF16)
    cot = (kept_ref[1].astype(F32) + nn(recv_ref[...], arrived_ref[1])).astype(BF16)
    x = x.astype(F32)
    source[...] = normalize(x)[0].astype(BF16)
    qkv[...] = nn(source[...], w_qkv[0]).astype(BF16)

    def step(window, carry):
        attention_forward(
            window, qkv, qkvt, prob, mixedt, mixed, bias_ref, main, rest, region_mask(window)
        )
        return carry

    lax.fori_loop(0, 4, step, 0)
    attended = nn(mixed[...], w_proj[0]).astype(BF16)
    middle = (x + attended.astype(F32)).astype(BF16)
    pre = nn(normalize(middle.astype(F32))[0].astype(BF16), w_in[0])
    slope = cumulative(pre) + pre * density(pre)
    mgrad[...] = mlp_back(middle, cot, slope, w_in[0], w_out[0])
    grad[...] = nt(mgrad[...], w_proj[0]).astype(BF16)
    wgrad[...] = jnp.zeros_like(wgrad)

    def back(window, carry):
        attention_backward(
            window, source, qkv, qkvt, prob, mixedt, mgrad, grad, w_qkv[0], w_proj[0], gradt, sgrad,
            wgrad, main24, rest24,
        )
        return carry

    lax.fori_loop(0, 4, back, 0)
    result = (mgrad[...].astype(F32) + norm_back(x, sgrad[...].astype(F32))).astype(BF16)
    kept_out[...] = nn(own2_ref[...], result).astype(BF16)
    sent_out[...] = nn(send2_ref[...], result).astype(BF16)
    pack_bias(main24, rest24, tiles_out)
    pack_weights(wgrad, wtiles_out)


def backward_kernel(
    kept_ref, arrived_ref, recv2_ref, loadt_ref, x_ref, source_ref, qkv_ref, qkvt_ref, prob_ref, mixedt_ref,
    mid_ref, slope_ref, w_qkv, w_proj, w_in, w_out,
    grid_out, tiles_out, wtiles_out,
    mgrad, grad, gradt, sgrad, wgrad, main24, rest24,
):
    upstream = (kept_ref[...].astype(F32) + nn(recv2_ref[...], arrived_ref[...])).astype(BF16)
    mgrad[...] = mlp_back(mid_ref[...], upstream, slope_ref[...], w_in[0], w_out[0])
    grad[...] = nt(mgrad[...], w_proj[0]).astype(BF16)
    wgrad[...] = jnp.zeros_like(wgrad)

    def back(window, carry):
        attention_backward(
            window, source_ref, qkv_ref, qkvt_ref, prob_ref, mixedt_ref, mgrad, grad, w_qkv[0], w_proj[0],
            gradt, sgrad, wgrad, main24, rest24,
        )
        return carry

    lax.fori_loop(0, 4, back, 0)
    x = x_ref[...].astype(F32)
    result = (mgrad[...].astype(F32) + norm_back(x, sgrad[...].astype(F32))).astype(BF16)
    placed = nn(loadt_ref[...], result).astype(BF16)
    for i in range(48):
        grid_out[i] = placed[16 * i : 16 * i + 12, :]
    pack_bias(main24, rest24, tiles_out)
    pack_weights(wgrad, wtiles_out)


def whole(ndim):
    return lambda *_: (0,) * ndim


def compute_call(kernel, operands, outs, scratch):
    specs, arrays = [], []
    for operand in operands:
        array, layer = operand if isinstance(operand, tuple) else (operand, None)
        arrays.append(array)
        shape = array.shape if layer is None else (1,) + array.shape[1:]
        index = (0 if layer is None else layer,) + (0,) * (array.ndim - 1)
        specs.append(pl.BlockSpec(shape, functools.partial(lambda at, _: at, index), pipeline_mode=ONCE))
    return pl.pallas_call(
        kernel,
        out_shape=[jax.ShapeDtypeStruct(shape, kind) for shape, kind in outs],
        in_specs=specs,
        out_specs=[pl.BlockSpec(shape, whole(len(shape)), pipeline_mode=ONCE) for shape, kind in outs],
        grid=(1,),
        scratch_shapes=[pltpu.VMEM(shape, kind) for shape, kind in scratch],
        compiler_params=pltpu.CompilerParams(vmem_limit_bytes=VMEM_LIMIT),
    )(*arrays)


def neighbour(lat_steps, lon_steps):
    lats, lons = lax.axis_size("lat"), lax.axis_size("lon")
    return (
        lax.rem(lax.axis_index("lat") + lat_steps + lats, lats),
        lax.rem(lax.axis_index("lon") + lon_steps + lons, lons),
    )


def exchange_kernel(sign, send_ref, out_ref, send_sems, recv_sems):
    barrier = pltpu.get_barrier_semaphore()
    steps = [(0, sign, E0, S0), (sign, 0, S0, D0), (sign, sign, D0, SEND)]
    for lat, lon, _, _ in steps:
        pl.semaphore_signal(barrier, inc=1, device_id=neighbour(-lat, -lon), device_id_type=MESH)
    pl.semaphore_wait(barrier, 3)
    copies = []
    for i, (lat, lon, start, stop) in enumerate(steps):
        piece = pl.ds(start, stop - start)
        copy = pltpu.make_async_remote_copy(
            src_ref=send_ref.at[:, piece],
            dst_ref=out_ref.at[:, piece],
            send_sem=send_sems.at[i],
            recv_sem=recv_sems.at[i],
            device_id=neighbour(lat, lon),
            device_id_type=MESH,
        )
        copy.start()
        copies.append(copy)
    for copy in copies:
        copy.wait()


def exchange(sent, sign, collective_id):
    return pl.pallas_call(
        functools.partial(exchange_kernel, sign),
        out_shape=jax.ShapeDtypeStruct(sent.shape, BF16),
        in_specs=[pl.BlockSpec(memory_space=pltpu.VMEM)],
        out_specs=pl.BlockSpec(memory_space=pltpu.VMEM),
        scratch_shapes=[pltpu.SemaphoreType.DMA((3,)), pltpu.SemaphoreType.DMA((3,))],
        compiler_params=pltpu.CompilerParams(collective_id=collective_id, has_side_effects=True),
    )(sent)


ZS = 8
CHUNK = 32


def reduce_kernel(
    tiles0, tiles1, w0, w1, out_ref, wout_ref,
    right_in, left_in, right_sum, left_sum, mine, other, wpart, wmid, wown, w_all,
    rs_send, rs_recv, ls_send, ls_recv, y_send, y_recv, ga_send, ga_recv, gb_send, gb_recv,
    wa_send, wa_recv, wb_send, wb_recv, wc_send, wc_recv, wd_send, wd_recv,
):
    lat = lax.axis_index("lat")
    lon = lax.axis_index("lon")
    z = lax.rem(lon, ZS)
    y = lon // ZS
    lats = lax.axis_size("lat")
    lons = lax.axis_size("lon")

    def along(steps):
        return (lat, y * ZS + lax.rem(z + steps + ZS, ZS))

    def copy_to(src, dst, send, recv, device):
        return pltpu.make_async_remote_copy(
            src_ref=src, dst_ref=dst, send_sem=send, recv_sem=recv, device_id=device, device_id_type=MESH
        )

    barrier = pltpu.get_barrier_semaphore()
    for k in range(1, 16):
        pl.semaphore_signal(barrier, inc=1, device_id=(lax.rem(lat + k, lats), lon), device_id_type=MESH)
        pl.semaphore_signal(barrier, inc=1, device_id=(lat, lax.rem(lon + k, lons)), device_id_type=MESH)
    pl.semaphore_wait(barrier, 30)

    def own(tiles, owner):
        return tiles[pl.ds(lax.rem(owner + 2 * ZS, ZS) * CHUNK, CHUNK)]

    for layer, w in enumerate((w0, w1)):
        w_all[pl.ds(72 * layer, 72)] = w[...]
    started = []
    for k in range(1, 16):
        to = lax.rem(lat + k, lats)
        copy = copy_to(w_all.at[pl.ds(to * 9, 9)], wpart.at[k], wa_send.at[k], wa_recv.at[k], (to, lon))
        copy.start()
        started.append(copy)

    def ring_sum(step):
        for layer, tiles in enumerate((tiles0, tiles1)):
            value = own(tiles, z + 4 - step)
            if step:
                value = (value.astype(F32) + right_in[step - 1, layer].astype(F32)).astype(BF16)
            right_sum[step, layer] = value
            if step < 3:
                value = own(tiles, z - 3 + step)
                if step:
                    value = (value.astype(F32) + left_in[step - 1, layer].astype(F32)).astype(BF16)
                left_sum[step, layer] = value

    rings = []
    for step in range(4):
        if step:
            for copy in rings[-1]:
                copy.wait_recv()
        ring_sum(step)
        now = [copy_to(right_sum.at[step], right_in.at[step], rs_send.at[step], rs_recv.at[step], along(1))]
        if step < 3:
            now.append(
                copy_to(left_sum.at[step], left_in.at[step], ls_send.at[step], ls_recv.at[step], along(-1))
            )
        for copy in now:
            copy.start()
        rings.append(now)

    total = w_all[pl.ds(lat * 9, 9)].astype(F32)
    for k, copy in enumerate(started, 1):
        copy.wait_recv()
        total = total + wpart[k].astype(F32)
    wmid[0:9] = total.astype(BF16)
    for k in range(1, 16):
        to = lax.rem(lon + k, lons)

        @pl.when(to < 9)
        def _():
            copy_to(wmid.at[to], wown.at[k], wb_send.at[k], wb_recv.at[k], (lat, to)).start()

    rings[3][0].wait_recv()
    for layer, tiles in enumerate((tiles0, tiles1)):
        mine[layer] = (
            own(tiles, z).astype(F32) + right_in[3, layer].astype(F32) + left_in[2, layer].astype(F32)
        ).astype(BF16)
    swap = copy_to(mine, other, y_send.at[0], y_recv.at[0], (lat, (1 - y) * ZS + z))
    swap.start()

    @pl.when(lon < 9)
    def _():
        value = wmid[lon].astype(F32)
        for k in range(1, 16):
            copy_to(wmid.at[0], wown.at[k], wb_send.at[k], wb_recv.at[k], (lat, lon)).wait_recv()
            value = value + wown[k].astype(F32)
        wmid[9 + lon] = value.astype(BF16)
        for k in range(1, 16):
            to = lax.rem(lon + k, lons)
            copy_to(wmid.at[9 + lon], wmid.at[9 + lon], wc_send.at[k], wc_recv.at[k], (lat, to)).start()

    swap.wait_recv()
    for layer in range(2):
        out_ref[z, layer] = (mine[layer].astype(F32) + other[layer].astype(F32)).astype(BF16)

    gathers = []
    for step in range(4):
        if step:
            for copy in gathers[-1]:
                copy.wait_recv()
        at = lax.rem(z - step + ZS, ZS)
        now = [copy_to(out_ref.at[at], out_ref.at[at], ga_send.at[step], ga_recv.at[step], along(1))]
        if step < 3:
            at = lax.rem(z + step, ZS)
            now.append(copy_to(out_ref.at[at], out_ref.at[at], gb_send.at[step], gb_recv.at[step], along(-1)))
        for copy in now:
            copy.start()
        gathers.append(now)

        if step == 0:
            for k in range(1, 16):
                source = lax.rem(lon - k + lons, lons)

                @pl.when(source < 9)
                def _():
                    copy_to(
                        wmid.at[9 + source], wmid.at[9 + source], wc_send.at[k], wc_recv.at[k], (lat, source)
                    ).wait_recv()

            wout_ref[pl.ds(lat * 9, 9)] = wmid[9:18]
            final = []
            for k in range(1, 16):
                to = lax.rem(lat + k, lats)
                piece = wout_ref.at[pl.ds(lat * 9, 9)]
                copy = copy_to(piece, piece, wd_send.at[k], wd_recv.at[k], (to, lon))
                copy.start()
                final.append(copy)

    gathers[3][0].wait_recv()
    for copy in final:
        copy.wait()
    for now in rings + gathers:
        for copy in now:
            copy.wait_send()
    for copy in started:
        copy.wait_send()
    swap.wait_send()
    for k in range(1, 16):
        to = lax.rem(lon + k, lons)

        @pl.when(to < 9)
        def _():
            copy_to(wmid.at[to], wown.at[k], wb_send.at[k], wb_recv.at[k], (lat, to)).wait_send()

    @pl.when(lon < 9)
    def _():
        for k in range(1, 16):
            to = lax.rem(lon + k, lons)
            copy_to(wmid.at[9 + lon], wmid.at[9 + lon], wc_send.at[k], wc_recv.at[k], (lat, to)).wait_send()


def reduce_all(tiles0, tiles1, w0, w1):
    dma = pltpu.SemaphoreType.DMA
    ring = (2, CHUNK, 16, 128)
    scratch = [
        pltpu.VMEM((4,) + ring, BF16),
        pltpu.VMEM((3,) + ring, BF16),
        pltpu.VMEM((4,) + ring, BF16),
        pltpu.VMEM((3,) + ring, BF16),
        pltpu.VMEM(ring, BF16),
        pltpu.VMEM(ring, BF16),
        pltpu.VMEM((16, 9, 16, 128), BF16),
        pltpu.VMEM((18, 16, 128), BF16),
        pltpu.VMEM((16, 16, 128), BF16),
        pltpu.VMEM((144, 16, 128), BF16),
    ]
    sems = [4, 4, 3, 3, 1, 1, 4, 4, 3, 3] + [16] * 8
    return pl.pallas_call(
        reduce_kernel,
        out_shape=[
            jax.ShapeDtypeStruct((ZS,) + ring, BF16),
            jax.ShapeDtypeStruct((144, 16, 128), BF16),
        ],
        in_specs=[pl.BlockSpec(memory_space=pltpu.VMEM)] * 4,
        out_specs=[pl.BlockSpec(memory_space=pltpu.VMEM)] * 2,
        scratch_shapes=scratch + [dma((n,)) for n in sems],
        compiler_params=pltpu.CompilerParams(
            collective_id=2, has_side_effects=True, vmem_limit_bytes=VMEM_LIMIT
        ),
    )(tiles0, tiles1, w0, w1)


def unpack_kernel(tiles_ref, wtiles_ref, bias_out, qkv_out, proj_out):
    for j in range(81):
        rows = []
        for third in range(3):
            at = third * 81 + j
            rows.append(tiles_ref[at // CHUNK, 0, at % CHUNK].astype(F32))
        for half in range(2):
            full = jnp.concatenate([part[8 * half : 8 * half + 8] for part in rows], axis=0)
            lanes = slice(half * 10368 + 128 * j, half * 10368 + 128 * j + 128)
            for window in range(4):
                bias_out[0, window // 2, window % 2, :, lanes] = full[6 * window : 6 * window + 6]
    for i in range(12):
        row = jnp.concatenate([wtiles_ref[6 * i + j].astype(F32) for j in range(6)], axis=1)
        qkv_out[0, 16 * i : 16 * i + 16, :] = row[:, : 3 * C]
        proj_out[0, 16 * i : 16 * i + 16, :] = row[:, 3 * C :]


def unpack(tiles, wtiles):
    lat_wins = 2
    return pl.pallas_call(
        unpack_kernel,
        grid=(2,),
        out_shape=[
            jax.ShapeDtypeStruct((2, 2, lat_wins, HEADS, WIN * WIN), F32),
            jax.ShapeDtypeStruct((2, C, 3 * C), F32),
            jax.ShapeDtypeStruct((2, C, C), F32),
        ],
        in_specs=[
            pl.BlockSpec((ZS, 1, CHUNK, 16, 128), lambda l: (0, l, 0, 0, 0)),
            pl.BlockSpec((72, 16, 128), lambda l: (l, 0, 0)),
        ],
        out_specs=[
            pl.BlockSpec((1, 2, lat_wins, HEADS, WIN * WIN), lambda l: (l, 0, 0, 0, 0)),
            pl.BlockSpec((1, C, 3 * C), lambda l: (l, 0, 0)),
            pl.BlockSpec((1, C, C), lambda l: (l, 0, 0)),
        ],
        compiler_params=pltpu.CompilerParams(vmem_limit_bytes=VMEM_LIMIT),
    )(tiles, wtiles)


def shards(tokens, cotangent, w_qkv, w_proj, w_in, w_out, earth_bias):
    load, own, send, recv = (jnp.asarray(m, BF16) for m in _matrices())
    matrices = {"loadt": load.T, "own2": own.T, "send2": recv.T, "recv2": send.T}
    params = [w_qkv, w_proj, w_in, w_out]
    flat = (48, 12, C)
    main, rest = [((WIN * 8, 128), F32)] * 2
    main24, rest24 = [((WIN * 24, 128), F32)] * 2
    tok = ((TOK, C), BF16)
    qkv = ((TOK, 3 * C), BF16)
    qkvt = ((4, 3 * C, WIN), BF16)
    prob = ((24, WIN, WIN), F32)
    mixedt = ((4, C, WIN), BF16)
    slope = ((TOK, FF), F32)
    tiles = ((256, 16, 128), BF16)
    wtiles = ((72, 16, 128), BF16)
    back_scratch = [tok, tok, ((3 * C, WIN), BF16), tok, ((C, FF), F32)]
    kept_state = [tok, tok, qkv, qkvt, prob, mixedt, tok, slope]

    *state, kept, sent = compute_call(
        forward_kernel,
        [tokens.reshape(flat), cotangent.reshape(flat), load, own, send]
        + [(p, 0) for p in params]
        + [(earth_bias, 0)],
        kept_state + [((2, TOK, C), BF16), ((2, SEND, C), BF16)],
        [((768, C), BF16), tok, main, rest],
    )
    arrived = exchange(sent, -1, 0)
    kept, sent, tiles1, w1 = compute_call(
        middle_kernel,
        [kept, arrived, recv, matrices["send2"], matrices["own2"]]
        + [(p, 1) for p in params]
        + [(earth_bias, 1)],
        [tok, ((SEND, C), BF16), tiles, wtiles],
        [tok, qkv, qkvt, prob, mixedt, tok] + back_scratch + [main, rest, main24, rest24],
    )
    arrived = exchange(sent[None], 1, 1)[0]
    grid, tiles0, w0 = compute_call(
        backward_kernel,
        [kept, arrived, matrices["recv2"], matrices["loadt"]] + state + [(p, 0) for p in params],
        [(flat, BF16), tiles, wtiles],
        back_scratch + [main24, rest24],
    )
    total, wtotal = reduce_all(tiles0, tiles1, w0, w1)
    bias_total, qkv_total, proj_total = unpack(total, wtotal)
    return grid.reshape(tokens.shape), qkv_total, proj_total, bias_total


def solution(mesh):
    return jax.shard_map(
        shards,
        mesh=mesh,
        in_specs=(
            P(None, "lat", "lon", None),
            P(None, "lat", "lon", None),
            P(),
            P(),
            P(),
            P(),
            P(None, None, "lat", None, None),
        ),
        out_specs=(P(None, "lat", "lon", None), P(), P(), P(None, None, "lat", None, None)),
        check_vma=False,
    )
```

```python
import functools

import jax
import jax.numpy as jnp
import numpy as np
from jax import lax
from jax.experimental import pallas as pl
from jax.experimental.pallas import tpu as pltpu
from jax.sharding import PartitionSpec as P

F32 = jnp.float32
BF16 = jnp.bfloat16
C = 192
HEADS = 6
HD = 32
FF = 768
WIN = 144
TOK = 576
EPSILON = 1e-05
SCALE = HD ** (-0.5)
MESH = pl.DeviceIdType.MESH
E0, S0, D0, SEND = 0, 224, 304, 384
VMEM_LIMIT = 48 * 1024 * 1024
ZS = 8
PAIRS = 12
FLAT = 3888
ROWS = 4096


def _plain_index(level, row, col):
    window = (level // 2) * 2 + row // 6
    return window * WIN + (level % 2) * 72 + (row % 6) * 12 + col


def _matrices():
    load = np.zeros((TOK, 768), np.float32)
    own = np.zeros((TOK, TOK), np.float32)
    send = np.zeros((SEND, TOK), np.float32)
    recv = np.zeros((TOK, SEND), np.float32)
    for level in range(4):
        for row in range(12):
            for col in range(12):
                here = _plain_index(level, row, col)
                load[here, (level * 12 + row) * 16 + col] = 1
                target_row, target_col = row - 3, col - 6
                target = _plain_index((level - 1) % 4, target_row % 12, target_col % 12)
                if target_row >= 0 and target_col >= 0:
                    own[target, here] = 1
                    continue
                if target_row >= 0:
                    slot = E0 + (level * 9 + row - 3) * 6 + col
                elif target_col >= 0:
                    slot = S0 + (level * 3 + row) * 6 + col - 6
                else:
                    slot = D0 + (level * 3 + row) * 6 + col
                send[slot, here] = 1
                recv[target, slot] = 1
    return load, own, send, recv


def nn(a, b):
    return jnp.dot(a, b, preferred_element_type=F32)


def nt(a, b):
    return lax.dot_general(a, b, (((1,), (1,)), ((), ())), preferred_element_type=F32)


def eye(n):
    rows = lax.broadcasted_iota(jnp.int32, (n, n), 0)
    cols = lax.broadcasted_iota(jnp.int32, (n, n), 1)
    return jnp.where(rows == cols, 1.0, 0.0).astype(BF16)


def flip(a, n):
    return nt(eye(n), a).astype(BF16)


def normalize(x):
    center = jnp.mean(x, axis=-1, keepdims=True)
    offset = x - center
    spread = jnp.mean(offset * offset, axis=-1, keepdims=True)
    inverse = lax.rsqrt(spread + EPSILON)
    return offset * inverse, inverse


def norm_back(x, upstream):
    normed, inverse = normalize(x)
    first = jnp.mean(upstream, axis=-1, keepdims=True)
    second = jnp.mean(upstream * normed, axis=-1, keepdims=True)
    return inverse * (upstream - first - normed * second)


def cumulative(x):
    return 0.5 * (1.0 + lax.erf(x * 0.7071067811865476))


def density(x):
    return 0.3989422804014327 * jnp.exp(-0.5 * x * x)


def rows_of(window):
    return pl.ds(pl.multiple_of(window * WIN, WIN), WIN)


def spread_bias(bias_ref, window, main, rest):
    def step(group, carry):
        block = bias_ref[
            0, window // 2, window % 2, :, pl.ds(pl.multiple_of(group * 1152, 128), 1152)
        ].astype(F32)
        for r in range(8):
            at = pl.ds(pl.multiple_of(group * 64, 64) + 8 * r, 6)
            main[at, :] = block[:, WIN * r : WIN * r + 128]
            rest[at, 0:16] = block[:, WIN * r + 128 : WIN * r + WIN]
        return carry

    lax.fori_loop(0, 18, step, 0)


def head_bias(main, rest, head):
    left = main[pl.ds(head, WIN, stride=8), :]
    right = rest[pl.ds(head, WIN, stride=8), :]
    return jnp.concatenate([left, right[:, :16]], axis=1)


def pack_bias(main, rest, out_ref):
    def flat(first):
        parts = []
        for r in range(8):
            at = pl.ds(pl.multiple_of(first * 192, 8) + 24 * r, 24)
            parts += [main[at, :], rest[at, :][:, :16]]
        return jnp.concatenate(parts, axis=1)

    def step(group, carry):
        top = flat(group)
        bottom = flat(group + 9)
        for third in range(3):
            both = jnp.concatenate(
                [top[8 * third : 8 * third + 8], bottom[8 * third : 8 * third + 8]], axis=0
            ).astype(BF16)
            for j in range(9):
                out_ref[third * 81 + group * 9 + j] = both[:, 128 * j : 128 * j + 128]
        return carry

    lax.fori_loop(0, 9, step, 0)
    out_ref[243:256] = jnp.zeros((13, 16, 128), BF16)


def pack_weights(wgrad, out_ref):
    for i in range(12):
        block = wgrad[16 * i : 16 * i + 16, :].astype(BF16)
        for j in range(6):
            out_ref[6 * i + j] = block[:, 128 * j : 128 * j + 128]
    out_ref[72:80] = jnp.zeros((8, 16, 128), BF16)


def attention_forward(window, qkv_ref, qkvt_ref, prob_ref, mixedt_ref, mixed_ref, biases, mask):
    bias_ref, main, rest = biases
    spread_bias(bias_ref, window, main, rest)
    qkv = qkv_ref[rows_of(window), :]
    qkvt_ref[window] = flip(qkv, 3 * C)
    for head in range(HEADS):
        lo = head * HD
        keys = qkvt_ref[window, C + lo : C + lo + HD, :]
        values = qkvt_ref[window, 2 * C + lo : 2 * C + lo + HD, :]
        scores = nn(qkv[:, lo : lo + HD], keys) * SCALE + head_bias(main, rest, head)
        weights = jnp.exp(scores)
        if mask is not None:
            weights = weights * mask
        probs = weights / jnp.sum(weights, axis=-1, keepdims=True)
        probs = probs.astype(BF16)
        prob_ref[window * HEADS + head] = probs
        mixedt_ref[window, lo : lo + HD, :] = nt(values, probs).astype(BF16)
    mixed_ref[rows_of(window), :] = flip(mixedt_ref[window], WIN)


def attention_backward(
    window, source_ref, qkvt_ref, prob_ref, mixedt_ref, mgrad_ref, grad_ref,
    w_qkv, w_proj, gradt, sgrad_ref, wgrad, table,
):
    mgrad = mgrad_ref[rows_of(window), :]
    wgrad[:, 3 * C :] += nn(mixedt_ref[window], mgrad)
    grad = grad_ref[rows_of(window), :]
    gt = nt(w_proj, mgrad).astype(BF16)
    for head in range(HEADS):
        lo = head * HD
        queries = qkvt_ref[window, lo : lo + HD, :]
        keys = qkvt_ref[window, C + lo : C + lo + HD, :]
        values = qkvt_ref[window, 2 * C + lo : 2 * C + lo + HD, :]
        probs = prob_ref[window * HEADS + head]
        pgrad = nn(grad[:, lo : lo + HD], values)
        vgrad = nn(gt[lo : lo + HD, :], probs)
        probs = probs.astype(F32)
        delta = jnp.sum(pgrad * probs, axis=-1, keepdims=True)
        sgrad = probs * (pgrad - delta)
        at = pl.ds(window * HEADS + head, WIN, stride=24)
        table[0][at, :] = sgrad[:, :128]
        table[1][at, :] = jnp.concatenate([sgrad[:, 128:], jnp.zeros((WIN, 112), F32)], axis=1)
        sround = sgrad.astype(BF16)
        gradt[lo : lo + HD, :] = (nt(keys, sround) * SCALE).astype(BF16)
        gradt[C + lo : C + lo + HD, :] = (nn(queries, sround) * SCALE).astype(BF16)
        gradt[2 * C + lo : 2 * C + lo + HD, :] = vgrad.astype(BF16)
    all_grad = gradt[...]
    sourcet = flip(source_ref[rows_of(window), :], C)
    wgrad[:, : 3 * C] += nt(sourcet, all_grad)
    sgradt = nn(w_qkv, all_grad).astype(BF16)
    sgrad_ref[rows_of(window), :] = flip(sgradt, WIN)


def mlp_back(middle, upstream, slope, w_in, w_outt):
    act_grad = nn(upstream, w_outt)
    pre_grad = (slope * act_grad).astype(BF16)
    ngrad = nt(pre_grad, w_in)
    return (upstream.astype(F32) + norm_back(middle.astype(F32), ngrad)).astype(BF16)


def region_mask(window):
    last_lat = lax.axis_index("lat") == lax.axis_size("lat") - 1

    def region(tokens):
        level = tokens // 72
        row = tokens // 12 % 6
        upper = jnp.where(window // 2 == 1, level, 0)
        lower = jnp.where(jnp.logical_and(last_lat, window % 2 == 1), row // 3, 0)
        return upper * 2 + lower

    queries = region(lax.broadcasted_iota(jnp.int32, (WIN, WIN), 0))
    keys = region(lax.broadcasted_iota(jnp.int32, (WIN, WIN), 1))
    return jnp.where(queries == keys, 1.0, 0.0)


def place():
    lat, lon = lax.axis_index("lat"), lax.axis_index("lon")
    return lat, lon, lax.rem(lon, ZS), lon // ZS


def neighbour(lat_steps, lon_steps):
    lats, lons = lax.axis_size("lat"), lax.axis_size("lon")
    lat, lon, _, _ = place()
    return lax.rem(lat + lat_steps + lats, lats), lax.rem(lon + lon_steps + lons, lons)


def remote(src, dst, send, recv, device):
    return pltpu.make_async_remote_copy(
        src_ref=src, dst_ref=dst, send_sem=send, recv_sem=recv, device_id=device, device_id_type=MESH
    )


def wait_all(copies):
    for copy in copies:
        copy.wait()


def greet():
    barrier = pltpu.get_barrier_semaphore()
    for k in range(1, 16):
        for device in (neighbour(k, 0), neighbour(0, k)):
            pl.semaphore_signal(barrier, inc=1, device_id=device, device_id_type=MESH)
    pl.semaphore_wait(barrier, 30)


def exchange_kernel(sign, send_ref, out_ref, send_sems, recv_sems):
    barrier = pltpu.get_barrier_semaphore()
    steps = [(0, sign, E0, S0), (sign, 0, S0, D0), (sign, sign, D0, SEND)]
    for lat, lon, _, _ in steps:
        pl.semaphore_signal(barrier, inc=1, device_id=neighbour(-lat, -lon), device_id_type=MESH)
    pl.semaphore_wait(barrier, 3)
    copies = []
    for i, (lat, lon, start, stop) in enumerate(steps):
        piece = pl.ds(start, stop - start)
        copy = pltpu.make_async_remote_copy(
            src_ref=send_ref.at[:, piece],
            dst_ref=out_ref.at[:, piece],
            send_sem=send_sems.at[i],
            recv_sem=recv_sems.at[i],
            device_id=neighbour(lat, lon),
            device_id_type=MESH,
        )
        copy.start()
        copies.append(copy)
    for copy in copies:
        copy.wait()


def exchange(sent, sign, collective_id):
    return pl.pallas_call(
        functools.partial(exchange_kernel, sign),
        out_shape=jax.ShapeDtypeStruct(sent.shape, BF16),
        in_specs=[pl.BlockSpec(memory_space=pltpu.VMEM)],
        out_specs=pl.BlockSpec(memory_space=pltpu.VMEM),
        scratch_shapes=[pltpu.SemaphoreType.DMA((3,)), pltpu.SemaphoreType.DMA((3,))],
        compiler_params=pltpu.CompilerParams(collective_id=collective_id, has_side_effects=True),
    )(sent)


class Ring:
    def __init__(self, rows, own, out, base, bufs, sems):
        self.rows, self.own, self.out, self.base = rows, own, out, base
        self.right_in, self.left_in, self.right_sum, self.left_sum = bufs
        self.sems = sems
        lat, lon, self.z, y = place()
        self.right = (lat, y * ZS + lax.rem(self.z + 1, ZS))
        self.left = (lat, y * ZS + lax.rem(self.z + ZS - 1, ZS))
        self.sums, self.gathers = [], []

    def chunk(self, steps):
        return pl.multiple_of(lax.rem(self.z + steps + 2 * ZS, ZS) * self.rows, self.rows)

    def send(self, kind, step, src, dst, device):
        copy = remote(src, dst, self.sems.at[kind, step], self.sems.at[kind + 1, step], device)
        copy.start()
        return copy

    def reduce(self, step):
        if step:
            for copy in self.sums[-1]:
                copy.wait_recv()
        now = []
        value = self.own(self.chunk(4 - step))
        if step:
            value = (value.astype(F32) + self.right_in[step - 1].astype(F32)).astype(BF16)
        self.right_sum[step] = value
        now.append(self.send(0, step, self.right_sum.at[step], self.right_in.at[step], self.right))
        if step < 3:
            value = self.own(self.chunk(step - 3))
            if step:
                value = (value.astype(F32) + self.left_in[step - 1].astype(F32)).astype(BF16)
            self.left_sum[step] = value
            now.append(self.send(2, step, self.left_sum.at[step], self.left_in.at[step], self.left))
        self.sums.append(now)

    def total(self):
        self.sums[3][0].wait_recv()
        return self.own(self.chunk(0)).astype(F32) + self.right_in[3].astype(F32) + self.left_in[2].astype(F32)

    def piece(self, steps):
        return self.out.at[pl.ds(pl.multiple_of(self.base + self.chunk(steps), self.rows), self.rows)]

    def gather(self, step):
        came = []
        if step:
            for copy in self.gathers[-1]:
                copy.wait_recv()
            came.append((step, self.piece(-step)))
            if step < 4:
                came.append((step + 4, self.piece(step)))
        if step < 4:
            now = [self.send(4, step, self.piece(-step), self.piece(-step), self.right)]
            if step < 3:
                now.append(self.send(6, step, self.piece(step), self.piece(step), self.left))
            self.gathers.append(now)
        return came

    def finish(self):
        for now in self.sums + self.gathers:
            for copy in now:
                copy.wait_send()


def sum_tiles(tiles, out, bufs, sems, y_sems):
    lat, lon, z, y = place()
    partner = (lat, (1 - y) * ZS + z)
    bufs_a, mine, other, bufs_b, half, half_in = bufs
    a = Ring(256, lambda at: tiles[pl.ds(at, 256)], out, 0, bufs_a, sems.at[0])
    base = 2048 + y * 1024
    b = Ring(128, lambda at: half[pl.ds(at, 128)], out, base, bufs_b, sems.at[1])
    away = pl.ds(pl.multiple_of(2048 + (1 - y) * 1024, 1024), 1024)
    here = pl.ds(pl.multiple_of(2048 + y * 1024, 1024), 1024)
    cross = remote(tiles.at[away], half_in, y_sems.at[0, 0], y_sems.at[1, 0], partner)
    cross.start()
    a.reduce(0)
    yield
    a.reduce(1)
    yield
    cross.wait_recv()
    half[...] = (tiles[here].astype(F32) + half_in[...].astype(F32)).astype(BF16)
    b.reduce(0)
    a.reduce(2)
    yield
    b.reduce(1)
    a.reduce(3)
    yield
    b.reduce(2)
    mine[...] = a.total().astype(BF16)
    swap = remote(mine, other, y_sems.at[0, 1], y_sems.at[1, 1], partner)
    swap.start()
    yield
    b.reduce(3)
    swap.wait_recv()
    a.piece(0)[...] = (mine[...].astype(F32) + other[...].astype(F32)).astype(BF16)
    a.gather(0)
    yield
    b.piece(0)[...] = b.total().astype(BF16)
    b.gather(0)
    shared = []

    def share(pieces):
        for slot, piece in pieces:
            copy = remote(piece, piece, y_sems.at[0, 2 + slot], y_sems.at[1, 2 + slot], partner)
            copy.start()
            shared.append(copy)

    share([(0, b.piece(0))])
    a.gather(1)
    yield
    share(b.gather(1))
    a.gather(2)
    yield
    share(b.gather(2))
    a.gather(3)
    yield
    share(b.gather(3))
    a.gather(4)
    yield
    share(b.gather(4))
    wait_all(shared)
    cross.wait_send()
    swap.wait_send()
    a.finish()
    b.finish()


def sum_weights(w, out, part, mid, owned, done, sems, first):
    lat, lon, _, _ = place()
    peers = range(1, 16)
    scatter = []
    for k in peers:
        to = neighbour(k, 0)
        copy = remote(w.at[pl.ds(to[0] * 5, 5)], part.at[k], sems.at[0, k], sems.at[1, k], to)
        copy.start()
        scatter.append(copy)
    yield
    total = w[pl.ds(lat * 5, 5)].astype(F32)
    for k, copy in enumerate(scatter, 1):
        copy.wait_recv()
        total = total + part[k].astype(F32)
    mid[...] = total.astype(BF16)

    def owner(index):
        return jnp.logical_and(index >= first, index < first + 5)

    def to_owner(k, device):
        tile = jnp.clip(device[1] - first, 0, 4)
        return remote(mid.at[tile], owned.at[k], sems.at[2, k], sems.at[3, k], device)

    def from_owner(k, tile, device):
        tile = jnp.clip(tile, 0, 4)
        return remote(done.at[tile], done.at[tile], sems.at[4, k], sems.at[5, k], device)

    for k in peers:
        to = neighbour(0, k)

        @pl.when(owner(to[1]))
        def _():
            to_owner(k, to).start()

    yield

    @pl.when(owner(lon))
    def _():
        mine = jnp.clip(lon - first, 0, 4)
        value = mid[mine].astype(F32)
        for k in peers:
            to_owner(k, (lat, lon)).wait_recv()
            value = value + owned[k].astype(F32)
        done[mine] = value.astype(BF16)
        for k in peers:
            from_owner(k, lon - first, neighbour(0, k)).start()

    yield
    for k in peers:
        source = neighbour(0, -k)

        @pl.when(owner(source[1]))
        def _():
            from_owner(k, source[1] - first, source).wait_recv()

    out[pl.ds(lat * 5, 5)] = done[...]
    spread = []
    for k in peers:
        piece = out.at[pl.ds(lat * 5, 5)]
        copy = remote(piece, piece, sems.at[6, k], sems.at[7, k], neighbour(k, 0))
        copy.start()
        spread.append(copy)
    yield
    wait_all(spread)
    for copy in scatter:
        copy.wait_send()
    for k in peers:
        to = neighbour(0, k)

        @pl.when(owner(to[1]))
        def _():
            to_owner(k, to).wait_send()

    @pl.when(owner(lon))
    def _():
        for k in peers:
            from_owner(k, lon - first, neighbour(0, k)).wait_send()


def advance(*streams):
    for stream in streams:
        next(stream, None)


def drain(*streams):
    live = list(streams)
    while live:
        live = [stream for stream in live if next(stream, live) is not live]


def attention_block(x, source, qkv, qkvt, prob, mixedt, mixed, w_qkv, w_proj, w_in, biases, masked):
    source[...] = normalize(x)[0].astype(BF16)
    qkv[...] = nn(source[...], w_qkv[0]).astype(BF16)

    def step(window, carry):
        attention_forward(
            window, qkv, qkvt, prob, mixedt, mixed, biases, region_mask(window) if masked else None
        )
        return carry

    lax.fori_loop(0, 4, step, 0)
    attended = nn(mixed[...], w_proj[0]).astype(BF16)
    middle = (x + attended.astype(F32)).astype(BF16)
    pre = nn(normalize(middle.astype(F32))[0].astype(BF16), w_in[0])
    phi = cumulative(pre)
    return middle, pre, phi, phi + pre * density(pre)


def load_grid(grid_ref, pad, matrix):
    for i in range(48):
        pad[16 * i : 16 * i + 12, :] = grid_ref[i]
    return nn(matrix, pad[...])


def forward_kernel(
    tok_ref, cot_ref, load_ref, own_ref, send_ref, w_qkv, w_proj, w_in, w_outt, bias_ref,
    x_out, source, qkvt, prob, mixedt, mid_out, slope_out, kept, sent,
    qkv, mixed, main, rest, pad,
):
    pad[...] = jnp.zeros_like(pad)
    cot = load_grid(cot_ref, pad, load_ref[...]).astype(BF16)
    sent[1] = nn(send_ref[...], cot).astype(BF16)
    kept[1] = nn(own_ref[...], cot).astype(BF16)
    x0 = load_grid(tok_ref, pad, load_ref[...])
    x_out[...] = x0.astype(BF16)
    middle, pre, phi, slope = attention_block(
        x0, source, qkv, qkvt, prob, mixedt, mixed, w_qkv, w_proj, w_in, (bias_ref, main, rest), False
    )
    mid_out[...] = middle
    slope_out[...] = slope.astype(BF16)
    x1 = (middle.astype(F32) + nt((pre * phi).astype(BF16), w_outt[0])).astype(BF16)
    sent[0] = nn(send_ref[...], x1).astype(BF16)
    kept[0] = nn(own_ref[...], x1).astype(BF16)


def middle_kernel(
    kept, arrived, recv_ref, ownt_ref, recvt_ref, w_qkv, w_proj, w_in, w_outt, bias_ref,
    kept_out, sent, tiles, wtiles,
    source, qkv, qkvt, prob, mixedt, mixed, mgrad, grad, gradt, sgrad, wgrad, main24, rest24, main, rest,
):
    x1 = kept[0].astype(F32) + nn(recv_ref[...], arrived[0])
    middle, _, _, slope = attention_block(
        x1, source, qkv, qkvt, prob, mixedt, mixed, w_qkv, w_proj, w_in, (bias_ref, main, rest), True
    )
    cot = (kept[1].astype(F32) + nn(recv_ref[...], arrived[1])).astype(BF16)
    mgrad[...] = mlp_back(middle, cot, slope, w_in[0], w_outt[0])
    grad[...] = nt(mgrad[...], w_proj[0]).astype(BF16)
    wgrad[...] = jnp.zeros_like(wgrad)

    def back(window, carry):
        attention_backward(
            window, source, qkvt, prob, mixedt, mgrad, grad, w_qkv[0], w_proj[0], gradt, sgrad, wgrad, (main24, rest24)
        )
        return carry

    lax.fori_loop(0, 4, back, 0)
    result = (mgrad[...].astype(F32) + norm_back(x1, sgrad[...].astype(F32))).astype(BF16)
    sent[0] = nn(recvt_ref[...], result).astype(BF16)
    kept_out[...] = nn(ownt_ref[...], result).astype(BF16)
    pack_bias(main24, rest24, tiles)
    pack_weights(wgrad, wtiles)


def backward_kernel(
    kept, arrived, sendt_ref, loadt_ref, x_ref, source, qkvt, prob, mixedt, mid, slope,
    w_qkv, w_proj, w_in, w_outt,
    grid_out, tiles, wtiles,
    mgrad, grad, gradt, sgrad, wgrad, main24, rest24,
):
    upstream = (kept[...].astype(F32) + nn(sendt_ref[...], arrived[0])).astype(BF16)
    mgrad[...] = mlp_back(mid[...], upstream, slope[...].astype(F32), w_in[0], w_outt[0])
    grad[...] = nt(mgrad[...], w_proj[0]).astype(BF16)
    wgrad[...] = jnp.zeros_like(wgrad)

    def back(window, carry):
        attention_backward(
            window, source, qkvt, prob, mixedt, mgrad, grad, w_qkv[0], w_proj[0], gradt, sgrad, wgrad, (main24, rest24)
        )
        return carry

    lax.fori_loop(0, 4, back, 0)
    result = (mgrad[...].astype(F32) + norm_back(x_ref[...].astype(F32), sgrad[...].astype(F32))).astype(BF16)
    placed = nn(loadt_ref[...], result).astype(BF16)
    for i in range(48):
        grid_out[i] = placed[16 * i : 16 * i + 12, :]
    pack_bias(main24, rest24, tiles)
    pack_weights(wgrad, wtiles)


def compute_call(kernel, operands, outs, scratch):
    specs, arrays = [], []
    once = pl.Buffered(1)
    for operand in operands:
        array, layer = operand if isinstance(operand, tuple) else (operand, None)
        arrays.append(array)
        shape = array.shape if layer is None else (1,) + array.shape[1:]
        index = (0 if layer is None else layer,) + (0,) * (array.ndim - 1)
        specs.append(pl.BlockSpec(shape, functools.partial(lambda at, _: at, index), pipeline_mode=once))
    return pl.pallas_call(
        kernel,
        out_shape=[jax.ShapeDtypeStruct(shape, kind) for shape, kind in outs],
        grid=(1,),
        in_specs=specs,
        out_specs=[
            pl.BlockSpec(shape, functools.partial(lambda at, _: at, (0,) * len(shape)), pipeline_mode=once)
            for shape, kind in outs
        ],
        scratch_shapes=[pltpu.VMEM(shape, kind) for shape, kind in scratch],
        compiler_params=pltpu.CompilerParams(vmem_limit_bytes=VMEM_LIMIT),
    )(*arrays)


def sum_kernel(
    tiles0, tiles1, wtiles0, wtiles1, bias_out, w_out,
    a_right_in, a_left_in, a_right_sum, a_left_sum, mine, other,
    b_right_in, b_left_in, b_right_sum, b_left_sum, half, half_in, ring_sems, y_sems,
    wpart, wmid, wowned, wdone, w_sems,
):
    greet()
    streams = []
    for layer, (tiles, wtiles) in enumerate(((tiles0, wtiles0), (tiles1, wtiles1))):
        bufs_a = [ref.at[layer] for ref in (a_right_in, a_left_in, a_right_sum, a_left_sum)]
        bufs_b = [ref.at[layer] for ref in (b_right_in, b_left_in, b_right_sum, b_left_sum)]
        bufs = (bufs_a, mine.at[layer], other.at[layer], bufs_b, half.at[layer], half_in.at[layer])
        streams.append(sum_tiles(tiles, bias_out.at[layer], bufs, ring_sems.at[layer], y_sems.at[layer]))
        streams.append(
            sum_weights(
                wtiles, w_out.at[layer], wpart.at[layer], wmid.at[layer], wowned.at[layer],
                wdone.at[layer], w_sems.at[layer], 8 * layer,
            )
        )
    drain(*streams)


def sum_all(tiles0, tiles1, wtiles0, wtiles1):
    vmem, dma = pltpu.VMEM, pltpu.SemaphoreType.DMA

    def ring(rows):
        return [vmem((2, n, rows, 128), BF16) for n in (4, 3, 4, 3)]

    return pl.pallas_call(
        sum_kernel,
        out_shape=[
            jax.ShapeDtypeStruct((2, ROWS, 128), BF16),
            jax.ShapeDtypeStruct((2, 80, 16, 128), BF16),
        ],
        in_specs=[pl.BlockSpec(memory_space=vmem)] * 4,
        out_specs=[pl.BlockSpec(memory_space=vmem)] * 2,
        scratch_shapes=[
            *ring(256),
            vmem((2, 256, 128), BF16),
            vmem((2, 256, 128), BF16),
            *ring(128),
            vmem((2, 1024, 128), BF16),
            vmem((2, 1024, 128), BF16),
            dma((2, 2, 8, 4)),
            dma((2, 2, 10)),
            vmem((2, 16, 5, 16, 128), BF16),
            vmem((2, 5, 16, 128), BF16),
            vmem((2, 16, 16, 128), BF16),
            vmem((2, 5, 16, 128), BF16),
            dma((2, 8, 16)),
        ],
        compiler_params=pltpu.CompilerParams(
            collective_id=2, has_side_effects=True, vmem_limit_bytes=VMEM_LIMIT
        ),
    )(tiles0, tiles1, wtiles0, wtiles1)


def unpack_kernel(tiles_ref, wtiles_ref, bias_out, qkv_out, proj_out):
    for j in range(81):
        rows = [tiles_ref[0, 16 * (third * 81 + j) : 16 * (third * 81 + j) + 16, :].astype(F32) for third in range(3)]
        for half in range(2):
            lanes = slice(half * 10368 + 128 * j, half * 10368 + 128 * j + 128)
            full = jnp.concatenate([part[8 * half : 8 * half + 8] for part in rows], axis=0)
            for window in range(4):
                bias_out[0, window // 2, window % 2, :, lanes] = full[6 * window : 6 * window + 6]
    for i in range(12):
        row = jnp.concatenate([wtiles_ref[0, 6 * i + j].astype(F32) for j in range(6)], axis=1)
        qkv_out[0, 16 * i : 16 * i + 16, :] = row[:, : 3 * C]
        proj_out[0, 16 * i : 16 * i + 16, :] = row[:, 3 * C :]


def unpack(tiles, wtiles):
    return pl.pallas_call(
        unpack_kernel,
        grid=(2,),
        out_shape=[
            jax.ShapeDtypeStruct((2, 2, 2, HEADS, WIN * WIN), F32),
            jax.ShapeDtypeStruct((2, C, 3 * C), F32),
            jax.ShapeDtypeStruct((2, C, C), F32),
        ],
        in_specs=[
            pl.BlockSpec((1, ROWS, 128), lambda l: (l, 0, 0)),
            pl.BlockSpec((1, 80, 16, 128), lambda l: (l, 0, 0, 0)),
        ],
        out_specs=[
            pl.BlockSpec((1, 2, 2, HEADS, WIN * WIN), lambda l: (l, 0, 0, 0, 0)),
            pl.BlockSpec((1, C, 3 * C), lambda l: (l, 0, 0)),
            pl.BlockSpec((1, C, C), lambda l: (l, 0, 0)),
        ],
        compiler_params=pltpu.CompilerParams(vmem_limit_bytes=VMEM_LIMIT),
    )(tiles, wtiles)


def to_cells(grid):
    return grid.reshape(48, 12, C)


def shards(tokens, cotangent, w_qkv, w_proj, w_in, w_out, earth_bias):
    load, own, send, recv = _matrices()
    loadt, ownt, recvt, sendt = (jnp.asarray(m.T, BF16) for m in (load, own, recv, send))
    load, own, send, recv = (jnp.asarray(m, BF16) for m in (load, own, send, recv))
    params = [w_qkv, w_proj, w_in, w_out.transpose(0, 2, 1)]
    tok, wide = ((TOK, C), BF16), ((TOK, 3 * C), BF16)
    qkvt, mixedt = ((4, 3 * C, WIN), BF16), ((4, C, WIN), BF16)
    prob = ((24, WIN, WIN), BF16)
    spread = [((WIN * 8, 128), F32)] * 2
    back = [tok, tok, ((3 * C, WIN), BF16), tok, ((C, FF), F32), ((WIN * 24, 128), F32), ((WIN * 24, 128), F32)]
    sums = [((256, 16, 128), BF16), ((80, 16, 128), BF16)]

    *state, kept, sent = compute_call(
        forward_kernel,
        [to_cells(tokens), to_cells(cotangent), load, own, send] + [(p, 0) for p in params + [earth_bias]],
        [tok, tok, qkvt, prob, mixedt, tok, ((TOK, FF), BF16), ((2, TOK, C), BF16), ((2, SEND, C), BF16)],
        [wide, tok] + spread + [((768, C), BF16)],
    )
    arrived = exchange(sent, -1, 0)
    kept, sent, tiles1, wtiles1 = compute_call(
        middle_kernel,
        [kept, arrived, recv, ownt, recvt] + [(p, 1) for p in params + [earth_bias]],
        [tok, ((1, SEND, C), BF16)] + sums,
        [tok, wide, qkvt, prob, mixedt, tok] + back + spread,
    )
    arrived = exchange(sent, 1, 1)
    grid, tiles0, wtiles0 = compute_call(
        backward_kernel,
        [kept, arrived, sendt, loadt] + state + [(p, 0) for p in params],
        [((48, 12, C), BF16)] + sums,
        back,
    )
    tiles, wtiles = sum_all(tiles0.reshape(ROWS, 128), tiles1.reshape(ROWS, 128), wtiles0, wtiles1)
    bias_grad, qkv_grad, proj_grad = unpack(tiles, wtiles)
    grid = grid.reshape(4, 12, 12, C)
    return grid, qkv_grad, proj_grad, bias_grad


def solution(mesh):
    return jax.shard_map(
        shards,
        mesh=mesh,
        in_specs=(
            P(None, "lat", "lon", None),
            P(None, "lat", "lon", None),
            P(),
            P(),
            P(),
            P(),
            P(None, None, "lat", None, None),
        ),
        out_specs=(P(None, "lat", "lon", None), P(), P(), P(None, None, "lat", None, None)),
        check_vma=False,
    )
```

```python
import functools

import jax
import jax.numpy as jnp
import numpy as np
from jax import lax
from jax.experimental import pallas as pl
from jax.experimental.pallas import tpu as pltpu
from jax.sharding import PartitionSpec as P

F32 = jnp.float32
BF16 = jnp.bfloat16
C = 192
HEADS = 6
HD = 32
FF = 768
WIN = 144
TOK = 576
EPSILON = 1e-05
SCALE = HD ** (-0.5)
MESH = pl.DeviceIdType.MESH
E0, S0, D0, SEND = 0, 224, 304, 384
VMEM_LIMIT = 56 * 1024 * 1024
ZS = 8
PAIRS = 12
FLAT = 3888
ROWS = 4096


def _plain_index(level, row, col):
    window = (level // 2) * 2 + row // 6
    return window * WIN + (level % 2) * 72 + (row % 6) * 12 + col


def _matrices():
    load = np.zeros((TOK, TOK), np.float32)
    own = np.zeros((TOK, TOK), np.float32)
    send = np.zeros((SEND, TOK), np.float32)
    recv = np.zeros((TOK, SEND), np.float32)
    for level in range(4):
        for row in range(12):
            for col in range(12):
                here = _plain_index(level, row, col)
                load[here, (row * 12 + col) * 4 + level] = 1
                target_row, target_col = row - 3, col - 6
                target = _plain_index((level - 1) % 4, target_row % 12, target_col % 12)
                if target_row >= 0 and target_col >= 0:
                    own[target, here] = 1
                    continue
                if target_row >= 0:
                    slot = E0 + (level * 9 + row - 3) * 6 + col
                elif target_col >= 0:
                    slot = S0 + (level * 3 + row) * 6 + col - 6
                else:
                    slot = D0 + (level * 3 + row) * 6 + col
                send[slot, here] = 1
                recv[target, slot] = 1
    return load, own, send, recv


def nn(a, b):
    return jnp.dot(a, b, preferred_element_type=F32)


def nt(a, b):
    return lax.dot_general(a, b, (((1,), (1,)), ((), ())), preferred_element_type=F32)


def eye(n):
    rows = lax.broadcasted_iota(jnp.int32, (n, n), 0)
    cols = lax.broadcasted_iota(jnp.int32, (n, n), 1)
    return jnp.where(rows == cols, 1.0, 0.0).astype(BF16)


def flip(a, n):
    return nt(eye(n), a).astype(BF16)


def normalize(x):
    center = jnp.mean(x, axis=-1, keepdims=True)
    offset = x - center
    spread = jnp.mean(offset * offset, axis=-1, keepdims=True)
    inverse = lax.rsqrt(spread + EPSILON)
    return offset * inverse, inverse


def norm_back(x, upstream):
    normed, inverse = normalize(x)
    first = jnp.mean(upstream, axis=-1, keepdims=True)
    second = jnp.mean(upstream * normed, axis=-1, keepdims=True)
    return inverse * (upstream - first - normed * second)


def cumulative(x):
    return 0.5 * (1.0 + lax.erf(x * 0.7071067811865476))


def density(x):
    return 0.3989422804014327 * jnp.exp(-0.5 * x * x)


def rows_of(window):
    return pl.ds(pl.multiple_of(window * WIN, WIN), WIN)


def spread_bias(bias_ref, window, main, rest):
    def step(group, carry):
        block = bias_ref[
            0, window // 2, window % 2, :, pl.ds(pl.multiple_of(group * 1152, 128), 1152)
        ].astype(F32)
        for r in range(8):
            at = pl.ds(pl.multiple_of(group * 64, 64) + 8 * r, 6)
            main[at, :] = block[:, WIN * r : WIN * r + 128]
            rest[at, 0:16] = block[:, WIN * r + 128 : WIN * r + WIN]
        return carry

    lax.fori_loop(0, 18, step, 0)


def head_bias(main, rest, head):
    left = main[pl.ds(head, WIN, stride=8), :]
    right = rest[pl.ds(head, WIN, stride=8), :]
    return jnp.concatenate([left, right[:, :16]], axis=1)


def pack_bias(main, rest, out_ref):
    def flat(first):
        parts = []
        for r in range(8):
            at = pl.ds(pl.multiple_of(first * 192, 8) + 24 * r, 24)
            parts += [main[at, :], rest[at, :][:, :16]]
        return jnp.concatenate(parts, axis=1)

    def step(group, carry):
        top = flat(group)
        bottom = flat(group + 9)
        for third in range(3):
            both = jnp.concatenate(
                [top[8 * third : 8 * third + 8], bottom[8 * third : 8 * third + 8]], axis=0
            ).astype(BF16)
            for j in range(9):
                out_ref[third * 81 + group * 9 + j] = both[:, 128 * j : 128 * j + 128]
        return carry

    lax.fori_loop(0, 9, step, 0)
    out_ref[243:256] = jnp.zeros((13, 16, 128), BF16)


def pack_weights(wgrad, out_ref):
    for i in range(12):
        block = wgrad[16 * i : 16 * i + 16, :].astype(BF16)
        for j in range(6):
            out_ref[6 * i + j] = block[:, 128 * j : 128 * j + 128]
    out_ref[72:80] = jnp.zeros((8, 16, 128), BF16)


def attention_forward(window, qkv_ref, qkvt_ref, prob_ref, mixedt_ref, mixed_ref, biases, mask):
    bias_ref, main, rest = biases
    spread_bias(bias_ref, window, main, rest)
    qkv = qkv_ref[rows_of(window), :]
    qkvt_ref[window] = flip(qkv, 3 * C)
    for head in range(HEADS):
        lo = head * HD
        keys = qkvt_ref[window, C + lo : C + lo + HD, :]
        values = qkvt_ref[window, 2 * C + lo : 2 * C + lo + HD, :]
        scores = nn(qkv[:, lo : lo + HD], keys) * SCALE + head_bias(main, rest, head)
        weights = jnp.exp(scores)
        if mask is not None:
            weights = weights * mask
        probs = weights / jnp.sum(weights, axis=-1, keepdims=True)
        probs = probs.astype(BF16)
        prob_ref[window * HEADS + head] = probs
        mixedt_ref[window, lo : lo + HD, :] = nt(values, probs).astype(BF16)
    mixed_ref[rows_of(window), :] = flip(mixedt_ref[window], WIN)


def attention_backward(
    window, source_ref, qkvt_ref, prob_ref, mixedt_ref, mgrad_ref, grad_ref,
    w_qkv, w_proj, gradt, sgrad_ref, wgrad, table,
):
    mgrad = mgrad_ref[rows_of(window), :]
    wgrad[:, 3 * C :] += nn(mixedt_ref[window], mgrad)
    grad = grad_ref[rows_of(window), :]
    gt = nt(w_proj, mgrad).astype(BF16)
    for head in range(HEADS):
        lo = head * HD
        queries = qkvt_ref[window, lo : lo + HD, :]
        keys = qkvt_ref[window, C + lo : C + lo + HD, :]
        values = qkvt_ref[window, 2 * C + lo : 2 * C + lo + HD, :]
        probs = prob_ref[window * HEADS + head]
        pgrad = nn(grad[:, lo : lo + HD], values)
        vgrad = nn(gt[lo : lo + HD, :], probs)
        probs = probs.astype(F32)
        delta = jnp.sum(pgrad * probs, axis=-1, keepdims=True)
        sgrad = probs * (pgrad - delta)
        at = pl.ds(window * HEADS + head, WIN, stride=24)
        table[0][at, :] = sgrad[:, :128]
        table[1][at, :] = jnp.concatenate([sgrad[:, 128:], jnp.zeros((WIN, 112), F32)], axis=1)
        sround = sgrad.astype(BF16)
        gradt[lo : lo + HD, :] = (nt(keys, sround) * SCALE).astype(BF16)
        gradt[C + lo : C + lo + HD, :] = (nn(queries, sround) * SCALE).astype(BF16)
        gradt[2 * C + lo : 2 * C + lo + HD, :] = vgrad.astype(BF16)
    all_grad = gradt[...]
    sourcet = flip(source_ref[rows_of(window), :], C)
    wgrad[:, : 3 * C] += nt(sourcet, all_grad)
    sgradt = nn(w_qkv, all_grad).astype(BF16)
    sgrad_ref[rows_of(window), :] = flip(sgradt, WIN)


def mlp_back(middle, upstream, slope, w_in, w_outt):
    act_grad = nn(upstream, w_outt)
    pre_grad = (slope * act_grad).astype(BF16)
    ngrad = nt(pre_grad, w_in)
    return (upstream.astype(F32) + norm_back(middle.astype(F32), ngrad)).astype(BF16)


def region_mask(window):
    last_lat = lax.axis_index("lat") == lax.axis_size("lat") - 1

    def region(tokens):
        level = tokens // 72
        row = tokens // 12 % 6
        upper = jnp.where(window // 2 == 1, level, 0)
        lower = jnp.where(jnp.logical_and(last_lat, window % 2 == 1), row // 3, 0)
        return upper * 2 + lower

    queries = region(lax.broadcasted_iota(jnp.int32, (WIN, WIN), 0))
    keys = region(lax.broadcasted_iota(jnp.int32, (WIN, WIN), 1))
    return jnp.where(queries == keys, 1.0, 0.0)


def place():
    lat, lon = lax.axis_index("lat"), lax.axis_index("lon")
    return lat, lon, lax.rem(lon, ZS), lon // ZS


def neighbour(lat_steps, lon_steps):
    lats, lons = lax.axis_size("lat"), lax.axis_size("lon")
    lat, lon, _, _ = place()
    return lax.rem(lat + lat_steps + lats, lats), lax.rem(lon + lon_steps + lons, lons)


def remote(src, dst, send, recv, device):
    return pltpu.make_async_remote_copy(
        src_ref=src, dst_ref=dst, send_sem=send, recv_sem=recv, device_id=device, device_id_type=MESH
    )


def wait_all(copies):
    for copy in copies:
        copy.wait()


def greet():
    barrier = pltpu.get_barrier_semaphore()
    for k in range(1, 16):
        for device in (neighbour(k, 0), neighbour(0, k)):
            pl.semaphore_signal(barrier, inc=1, device_id=device, device_id_type=MESH)
    pl.semaphore_wait(barrier, 30)


def exchange_kernel(sign, send_ref, out_ref, send_sems, recv_sems):
    barrier = pltpu.get_barrier_semaphore()
    steps = [(0, sign, E0, S0), (sign, 0, S0, D0), (sign, sign, D0, SEND)]
    for lat, lon, _, _ in steps:
        pl.semaphore_signal(barrier, inc=1, device_id=neighbour(-lat, -lon), device_id_type=MESH)
    pl.semaphore_wait(barrier, 3)
    copies = []
    for i, (lat, lon, start, stop) in enumerate(steps):
        piece = pl.ds(start, stop - start)
        copy = pltpu.make_async_remote_copy(
            src_ref=send_ref.at[:, piece],
            dst_ref=out_ref.at[:, piece],
            send_sem=send_sems.at[i],
            recv_sem=recv_sems.at[i],
            device_id=neighbour(lat, lon),
            device_id_type=MESH,
        )
        copy.start()
        copies.append(copy)
    for copy in copies:
        copy.wait()


def exchange(sent, sign, collective_id):
    return pl.pallas_call(
        functools.partial(exchange_kernel, sign),
        out_shape=jax.ShapeDtypeStruct(sent.shape, BF16),
        in_specs=[pl.BlockSpec(memory_space=pltpu.VMEM)],
        out_specs=pl.BlockSpec(memory_space=pltpu.VMEM),
        scratch_shapes=[pltpu.SemaphoreType.DMA((3,)), pltpu.SemaphoreType.DMA((3,))],
        compiler_params=pltpu.CompilerParams(collective_id=collective_id, has_side_effects=True),
    )(sent)


class Ring:
    def __init__(self, rows, own, out, base, bufs, sems):
        self.rows, self.own, self.out, self.base = rows, own, out, base
        self.right_in, self.left_in, self.right_sum, self.left_sum = bufs
        self.sems = sems
        lat, lon, self.z, y = place()
        self.right = (lat, y * ZS + lax.rem(self.z + 1, ZS))
        self.left = (lat, y * ZS + lax.rem(self.z + ZS - 1, ZS))
        self.sums, self.gathers = [], []

    def chunk(self, steps):
        return pl.multiple_of(lax.rem(self.z + steps + 2 * ZS, ZS) * self.rows, self.rows)

    def send(self, kind, step, src, dst, device):
        copy = remote(src, dst, self.sems.at[kind, step], self.sems.at[kind + 1, step], device)
        copy.start()
        return copy

    def reduce(self, step):
        if step:
            for copy in self.sums[-1]:
                copy.wait_recv()
        now = []
        value = self.own(self.chunk(4 - step))
        if step:
            value = (value.astype(F32) + self.right_in[step - 1].astype(F32)).astype(BF16)
        self.right_sum[step] = value
        now.append(self.send(0, step, self.right_sum.at[step], self.right_in.at[step], self.right))
        if step < 3:
            value = self.own(self.chunk(step - 3))
            if step:
                value = (value.astype(F32) + self.left_in[step - 1].astype(F32)).astype(BF16)
            self.left_sum[step] = value
            now.append(self.send(2, step, self.left_sum.at[step], self.left_in.at[step], self.left))
        self.sums.append(now)

    def total(self):
        self.sums[3][0].wait_recv()
        return self.own(self.chunk(0)).astype(F32) + self.right_in[3].astype(F32) + self.left_in[2].astype(F32)

    def piece(self, steps):
        return self.out.at[pl.ds(pl.multiple_of(self.base + self.chunk(steps), self.rows), self.rows)]

    def gather(self, step):
        came = []
        if step:
            for copy in self.gathers[-1]:
                copy.wait_recv()
            came.append((step, self.piece(-step)))
            if step < 4:
                came.append((step + 4, self.piece(step)))
        if step < 4:
            now = [self.send(4, step, self.piece(-step), self.piece(-step), self.right)]
            if step < 3:
                now.append(self.send(6, step, self.piece(step), self.piece(step), self.left))
            self.gathers.append(now)
        return came

    def finish(self):
        for now in self.sums + self.gathers:
            for copy in now:
                copy.wait_send()


def sum_tiles(tiles, out, bufs, sems, y_sems):
    lat, lon, z, y = place()
    partner = (lat, (1 - y) * ZS + z)
    bufs_a, mine, other, bufs_b, half, half_in = bufs
    a = Ring(256, lambda at: tiles[pl.ds(at, 256)], out, 0, bufs_a, sems.at[0])
    base = 2048 + y * 1024
    b = Ring(128, lambda at: half[pl.ds(at, 128)], out, base, bufs_b, sems.at[1])
    away = pl.ds(pl.multiple_of(2048 + (1 - y) * 1024, 1024), 1024)
    here = pl.ds(pl.multiple_of(2048 + y * 1024, 1024), 1024)
    cross = remote(tiles.at[away], half_in, y_sems.at[0, 0], y_sems.at[1, 0], partner)
    cross.start()
    a.reduce(0)
    yield
    a.reduce(1)
    yield
    cross.wait_recv()
    half[...] = (tiles[here].astype(F32) + half_in[...].astype(F32)).astype(BF16)
    b.reduce(0)
    a.reduce(2)
    yield
    b.reduce(1)
    a.reduce(3)
    yield
    b.reduce(2)
    mine[...] = a.total().astype(BF16)
    swap = remote(mine, other, y_sems.at[0, 1], y_sems.at[1, 1], partner)
    swap.start()
    yield
    b.reduce(3)
    swap.wait_recv()
    a.piece(0)[...] = (mine[...].astype(F32) + other[...].astype(F32)).astype(BF16)
    a.gather(0)
    yield
    b.piece(0)[...] = b.total().astype(BF16)
    b.gather(0)
    shared = []

    def share(pieces):
        for slot, piece in pieces:
            copy = remote(piece, piece, y_sems.at[0, 2 + slot], y_sems.at[1, 2 + slot], partner)
            copy.start()
            shared.append(copy)

    share([(0, b.piece(0))])
    a.gather(1)
    yield
    share(b.gather(1))
    a.gather(2)
    yield
    share(b.gather(2))
    a.gather(3)
    yield
    share(b.gather(3))
    a.gather(4)
    yield
    share(b.gather(4))
    wait_all(shared)
    cross.wait_send()
    swap.wait_send()
    a.finish()
    b.finish()


def sum_weights(w, out, part, mid, owned, done, sems, first):
    lat, lon, _, _ = place()
    peers = range(1, 16)
    scatter = []
    for k in peers:
        to = neighbour(k, 0)
        copy = remote(w.at[pl.ds(to[0] * 5, 5)], part.at[k], sems.at[0, k], sems.at[1, k], to)
        copy.start()
        scatter.append(copy)
    yield
    total = w[pl.ds(lat * 5, 5)].astype(F32)
    for k, copy in enumerate(scatter, 1):
        copy.wait_recv()
        total = total + part[k].astype(F32)
    mid[...] = total.astype(BF16)

    def owner(index):
        return jnp.logical_and(index >= first, index < first + 5)

    def to_owner(k, device):
        tile = jnp.clip(device[1] - first, 0, 4)
        return remote(mid.at[tile], owned.at[k], sems.at[2, k], sems.at[3, k], device)

    def from_owner(k, tile, device):
        tile = jnp.clip(tile, 0, 4)
        return remote(done.at[tile], done.at[tile], sems.at[4, k], sems.at[5, k], device)

    for k in peers:
        to = neighbour(0, k)

        @pl.when(owner(to[1]))
        def _():
            to_owner(k, to).start()

    yield

    @pl.when(owner(lon))
    def _():
        mine = jnp.clip(lon - first, 0, 4)
        value = mid[mine].astype(F32)
        for k in peers:
            to_owner(k, (lat, lon)).wait_recv()
            value = value + owned[k].astype(F32)
        done[mine] = value.astype(BF16)
        for k in peers:
            from_owner(k, lon - first, neighbour(0, k)).start()

    yield
    for k in peers:
        source = neighbour(0, -k)

        @pl.when(owner(source[1]))
        def _():
            from_owner(k, source[1] - first, source).wait_recv()

    out[pl.ds(lat * 5, 5)] = done[...]
    spread = []
    for k in peers:
        piece = out.at[pl.ds(lat * 5, 5)]
        copy = remote(piece, piece, sems.at[6, k], sems.at[7, k], neighbour(k, 0))
        copy.start()
        spread.append(copy)
    yield
    wait_all(spread)
    for copy in scatter:
        copy.wait_send()
    for k in peers:
        to = neighbour(0, k)

        @pl.when(owner(to[1]))
        def _():
            to_owner(k, to).wait_send()

    @pl.when(owner(lon))
    def _():
        for k in peers:
            from_owner(k, lon - first, neighbour(0, k)).wait_send()


def advance(*streams):
    for stream in streams:
        next(stream, None)


def drain(fast, slow, rounds):
    step = 0
    while fast:
        fast = [stream for stream in fast if next(stream, 1) is None]
        if step in rounds:
            advance(*slow)
        step += 1
    while slow:
        slow = [stream for stream in slow if next(stream, 1) is None]


def attention_block(x, source, qkv, qkvt, prob, mixedt, mixed, w_qkv, w_proj, w_in, biases, masked):
    source[...] = normalize(x)[0].astype(BF16)
    qkv[...] = nn(source[...], w_qkv[0]).astype(BF16)

    def step(window, carry):
        attention_forward(
            window, qkv, qkvt, prob, mixedt, mixed, biases, region_mask(window) if masked else None
        )
        return carry

    lax.fori_loop(0, 4, step, 0)
    attended = nn(mixed[...], w_proj[0]).astype(BF16)
    middle = (x + attended.astype(F32)).astype(BF16)
    pre = nn(normalize(middle.astype(F32))[0].astype(BF16), w_in[0])
    phi = cumulative(pre)
    return middle, pre, phi, phi + pre * density(pre)


def forward_kernel(
    tok_ref, cot_ref, load_ref, own_ref, send_ref, w_qkv, w_proj, w_in, w_outt, bias_ref,
    x_out, source, qkvt, prob, mixedt, mid_out, slope_out, kept, sent,
    qkv, mixed, main, rest,
):
    cot = nn(load_ref[...], cot_ref[...].reshape(TOK, C)).astype(BF16)
    sent[1] = nn(send_ref[...], cot).astype(BF16)
    kept[1] = nn(own_ref[...], cot).astype(BF16)
    x0 = nn(load_ref[...], tok_ref[...].reshape(TOK, C))
    x_out[...] = x0.astype(BF16)
    middle, pre, phi, slope = attention_block(
        x0, source, qkv, qkvt, prob, mixedt, mixed, w_qkv, w_proj, w_in, (bias_ref, main, rest), False
    )
    mid_out[...] = middle
    slope_out[...] = slope.astype(BF16)
    x1 = (middle.astype(F32) + nt((pre * phi).astype(BF16), w_outt[0])).astype(BF16)
    sent[0] = nn(send_ref[...], x1).astype(BF16)
    kept[0] = nn(own_ref[...], x1).astype(BF16)


def middle_kernel(
    kept, arrived, recv_ref, ownt_ref, recvt_ref, w_qkv, w_proj, w_in, w_outt, bias_ref,
    kept_out, sent, tiles, wtiles,
    source, qkv, qkvt, prob, mixedt, mixed, mgrad, grad, gradt, sgrad, wgrad, main24, rest24, main, rest,
):
    x1 = kept[0].astype(F32) + nn(recv_ref[...], arrived[0])
    middle, _, _, slope = attention_block(
        x1, source, qkv, qkvt, prob, mixedt, mixed, w_qkv, w_proj, w_in, (bias_ref, main, rest), True
    )
    cot = (kept[1].astype(F32) + nn(recv_ref[...], arrived[1])).astype(BF16)
    mgrad[...] = mlp_back(middle, cot, slope, w_in[0], w_outt[0])
    grad[...] = nt(mgrad[...], w_proj[0]).astype(BF16)
    wgrad[...] = jnp.zeros_like(wgrad)

    def back(window, carry):
        attention_backward(
            window, source, qkvt, prob, mixedt, mgrad, grad, w_qkv[0], w_proj[0], gradt, sgrad, wgrad, (main24, rest24)
        )
        return carry

    lax.fori_loop(0, 4, back, 0)
    result = (mgrad[...].astype(F32) + norm_back(x1, sgrad[...].astype(F32))).astype(BF16)
    sent[0] = nn(recvt_ref[...], result).astype(BF16)
    kept_out[...] = nn(ownt_ref[...], result).astype(BF16)
    pack_bias(main24, rest24, tiles)
    pack_weights(wgrad, wtiles)


def backward_kernel(
    kept, arrived, sendt_ref, loadt_ref, x_ref, source, qkvt, prob, mixedt, mid, slope,
    w_qkv, w_proj, w_in, w_outt,
    grid_out, tiles, wtiles,
    mgrad, grad, gradt, sgrad, wgrad, main24, rest24,
):
    upstream = (kept[...].astype(F32) + nn(sendt_ref[...], arrived[0])).astype(BF16)
    mgrad[...] = mlp_back(mid[...], upstream, slope[...].astype(F32), w_in[0], w_outt[0])
    grad[...] = nt(mgrad[...], w_proj[0]).astype(BF16)
    wgrad[...] = jnp.zeros_like(wgrad)

    def back(window, carry):
        attention_backward(
            window, source, qkvt, prob, mixedt, mgrad, grad, w_qkv[0], w_proj[0], gradt, sgrad, wgrad, (main24, rest24)
        )
        return carry

    lax.fori_loop(0, 4, back, 0)
    result = (mgrad[...].astype(F32) + norm_back(x_ref[...].astype(F32), sgrad[...].astype(F32))).astype(BF16)
    grid_out[...] = nn(loadt_ref[...], result).astype(BF16).reshape(144, 4, C)
    pack_bias(main24, rest24, tiles)
    pack_weights(wgrad, wtiles)


def compute_call(kernel, operands, outs, scratch):
    specs, arrays = [], []
    once = pl.Buffered(1)
    for operand in operands:
        array, layer = operand if isinstance(operand, tuple) else (operand, None)
        arrays.append(array)
        shape = array.shape if layer is None else (1,) + array.shape[1:]
        index = (0 if layer is None else layer,) + (0,) * (array.ndim - 1)
        specs.append(pl.BlockSpec(shape, functools.partial(lambda at, _: at, index), pipeline_mode=once))
    return pl.pallas_call(
        kernel,
        out_shape=[jax.ShapeDtypeStruct(shape, kind) for shape, kind in outs],
        grid=(1,),
        in_specs=specs,
        out_specs=[
            pl.BlockSpec(shape, functools.partial(lambda at, _: at, (0,) * len(shape)), pipeline_mode=once)
            for shape, kind in outs
        ],
        scratch_shapes=[pltpu.VMEM(shape, kind) for shape, kind in scratch],
        compiler_params=pltpu.CompilerParams(vmem_limit_bytes=VMEM_LIMIT),
    )(*arrays)


def sum_kernel(
    tiles0, tiles1, wtiles0, wtiles1, bias_out, w_out,
    a_right_in, a_left_in, a_right_sum, a_left_sum, mine, other,
    b_right_in, b_left_in, b_right_sum, b_left_sum, half, half_in, ring_sems, y_sems,
    wpart, wmid, wowned, wdone, w_sems,
):
    greet()
    streams = []
    for layer, (tiles, wtiles) in enumerate(((tiles0, wtiles0), (tiles1, wtiles1))):
        bufs_a = [ref.at[layer] for ref in (a_right_in, a_left_in, a_right_sum, a_left_sum)]
        bufs_b = [ref.at[layer] for ref in (b_right_in, b_left_in, b_right_sum, b_left_sum)]
        bufs = (bufs_a, mine.at[layer], other.at[layer], bufs_b, half.at[layer], half_in.at[layer])
        streams.append(sum_tiles(tiles, bias_out.at[layer], bufs, ring_sems.at[layer], y_sems.at[layer]))
        streams.append(
            sum_weights(
                wtiles, w_out.at[layer], wpart.at[layer], wmid.at[layer], wowned.at[layer],
                wdone.at[layer], w_sems.at[layer], 8 * layer,
            )
        )
    drain(streams[::2], streams[1::2], (0, 2, 5, 7))


def sum_all(tiles0, tiles1, wtiles0, wtiles1):
    vmem, dma = pltpu.VMEM, pltpu.SemaphoreType.DMA

    def ring(rows):
        return [vmem((2, n, rows, 128), BF16) for n in (4, 3, 4, 3)]

    return pl.pallas_call(
        sum_kernel,
        out_shape=[
            jax.ShapeDtypeStruct((2, ROWS, 128), BF16),
            jax.ShapeDtypeStruct((2, 80, 16, 128), BF16),
        ],
        in_specs=[pl.BlockSpec(memory_space=vmem)] * 4,
        out_specs=[pl.BlockSpec(memory_space=vmem)] * 2,
        scratch_shapes=[
            *ring(256),
            vmem((2, 256, 128), BF16),
            vmem((2, 256, 128), BF16),
            *ring(128),
            vmem((2, 1024, 128), BF16),
            vmem((2, 1024, 128), BF16),
            dma((2, 2, 8, 4)),
            dma((2, 2, 10)),
            vmem((2, 16, 5, 16, 128), BF16),
            vmem((2, 5, 16, 128), BF16),
            vmem((2, 16, 16, 128), BF16),
            vmem((2, 5, 16, 128), BF16),
            dma((2, 8, 16)),
        ],
        compiler_params=pltpu.CompilerParams(
            collective_id=2, has_side_effects=True, vmem_limit_bytes=VMEM_LIMIT
        ),
    )(tiles0, tiles1, wtiles0, wtiles1)


def unpack_kernel(tiles_ref, wtiles_ref, bias_out, qkv_out, proj_out):
    for j in range(81):
        rows = [tiles_ref[0, 16 * (third * 81 + j) : 16 * (third * 81 + j) + 16, :].astype(F32) for third in range(3)]
        for half in range(2):
            lanes = slice(half * 10368 + 128 * j, half * 10368 + 128 * j + 128)
            full = jnp.concatenate([part[8 * half : 8 * half + 8] for part in rows], axis=0)
            for window in range(4):
                bias_out[0, window // 2, window % 2, :, lanes] = full[6 * window : 6 * window + 6]
    for i in range(12):
        row = jnp.concatenate([wtiles_ref[0, 6 * i + j].astype(F32) for j in range(6)], axis=1)
        qkv_out[0, 16 * i : 16 * i + 16, :] = row[:, : 3 * C]
        proj_out[0, 16 * i : 16 * i + 16, :] = row[:, 3 * C :]


def unpack(tiles, wtiles):
    return pl.pallas_call(
        unpack_kernel,
        grid=(2,),
        out_shape=[
            jax.ShapeDtypeStruct((2, 2, 2, HEADS, WIN * WIN), F32),
            jax.ShapeDtypeStruct((2, C, 3 * C), F32),
            jax.ShapeDtypeStruct((2, C, C), F32),
        ],
        in_specs=[
            pl.BlockSpec((1, ROWS, 128), lambda l: (l, 0, 0)),
            pl.BlockSpec((1, 80, 16, 128), lambda l: (l, 0, 0, 0)),
        ],
        out_specs=[
            pl.BlockSpec((1, 2, 2, HEADS, WIN * WIN), lambda l: (l, 0, 0, 0, 0)),
            pl.BlockSpec((1, C, 3 * C), lambda l: (l, 0, 0)),
            pl.BlockSpec((1, C, C), lambda l: (l, 0, 0)),
        ],
        compiler_params=pltpu.CompilerParams(vmem_limit_bytes=VMEM_LIMIT),
    )(tiles, wtiles)


def to_cells(grid):
    return grid.transpose(1, 2, 0, 3).reshape(144, 4, C)


def shards(tokens, cotangent, w_qkv, w_proj, w_in, w_out, earth_bias):
    load, own, send, recv = _matrices()
    loadt, ownt, recvt, sendt = (jnp.asarray(m.T, BF16) for m in (load, own, recv, send))
    load, own, send, recv = (jnp.asarray(m, BF16) for m in (load, own, send, recv))
    params = [w_qkv, w_proj, w_in, w_out.transpose(0, 2, 1)]
    tok, wide = ((TOK, C), BF16), ((TOK, 3 * C), BF16)
    qkvt, mixedt = ((4, 3 * C, WIN), BF16), ((4, C, WIN), BF16)
    prob = ((24, WIN, WIN), BF16)
    spread = [((WIN * 8, 128), F32)] * 2
    back = [tok, tok, ((3 * C, WIN), BF16), tok, ((C, FF), F32), ((WIN * 24, 128), F32), ((WIN * 24, 128), F32)]
    sums = [((256, 16, 128), BF16), ((80, 16, 128), BF16)]

    *state, kept, sent = compute_call(
        forward_kernel,
        [to_cells(tokens), to_cells(cotangent), load, own, send] + [(p, 0) for p in params + [earth_bias]],
        [tok, tok, qkvt, prob, mixedt, tok, ((TOK, FF), BF16), ((2, TOK, C), BF16), ((2, SEND, C), BF16)],
        [wide, tok] + spread,
    )
    arrived = exchange(sent, -1, 0)
    kept, sent, tiles1, wtiles1 = compute_call(
        middle_kernel,
        [kept, arrived, recv, ownt, recvt] + [(p, 1) for p in params + [earth_bias]],
        [tok, ((1, SEND, C), BF16)] + sums,
        [tok, wide, qkvt, prob, mixedt, tok] + back + spread,
    )
    arrived = exchange(sent, 1, 1)
    grid, tiles0, wtiles0 = compute_call(
        backward_kernel,
        [kept, arrived, sendt, loadt] + state + [(p, 0) for p in params],
        [((144, 4, C), BF16)] + sums,
        back,
    )
    tiles, wtiles = sum_all(tiles0.reshape(ROWS, 128), tiles1.reshape(ROWS, 128), wtiles0, wtiles1)
    bias_grad, qkv_grad, proj_grad = unpack(tiles, wtiles)
    grid = grid.reshape(12, 12, 4, C).transpose(2, 0, 1, 3)
    return grid, qkv_grad, proj_grad, bias_grad


def solution(mesh):
    return jax.shard_map(
        shards,
        mesh=mesh,
        in_specs=(
            P(None, "lat", "lon", None),
            P(None, "lat", "lon", None),
            P(),
            P(),
            P(),
            P(),
            P(None, None, "lat", None, None),
        ),
        out_specs=(P(None, "lat", "lon", None), P(), P(), P(None, None, "lat", None, None)),
        check_vma=False,
    )
```

```python
import functools

import jax
import jax.numpy as jnp
import numpy as np
from jax import lax
from jax.experimental import pallas as pl
from jax.experimental.pallas import tpu as pltpu
from jax.sharding import PartitionSpec as P

F32 = jnp.float32
BF16 = jnp.bfloat16
C = 192
HEADS = 6
HD = 32
FF = 768
WIN = 144
TOK = 576
EPSILON = 1e-05
SCALE = HD ** (-0.5)
MESH = pl.DeviceIdType.MESH
E0, S0, D0, SEND = 0, 224, 304, 384
VMEM_LIMIT = 56 * 1024 * 1024
ZS = 8
PAIRS = 12
FLAT = 3888
ROWS = 4096


def _plain_index(level, row, col):
    window = (level // 2) * 2 + row // 6
    return window * WIN + (level % 2) * 72 + (row % 6) * 12 + col


def _matrices():
    load = np.zeros((TOK, TOK), np.float32)
    own = np.zeros((TOK, TOK), np.float32)
    send = np.zeros((SEND, TOK), np.float32)
    recv = np.zeros((TOK, SEND), np.float32)
    for level in range(4):
        for row in range(12):
            for col in range(12):
                here = _plain_index(level, row, col)
                load[here, (row * 12 + col) * 4 + level] = 1
                target_row, target_col = row - 3, col - 6
                target = _plain_index((level - 1) % 4, target_row % 12, target_col % 12)
                if target_row >= 0 and target_col >= 0:
                    own[target, here] = 1
                    continue
                if target_row >= 0:
                    slot = E0 + (level * 9 + row - 3) * 6 + col
                elif target_col >= 0:
                    slot = S0 + (level * 3 + row) * 6 + col - 6
                else:
                    slot = D0 + (level * 3 + row) * 6 + col
                send[slot, here] = 1
                recv[target, slot] = 1
    return load, own, send, recv


def nn(a, b):
    return jnp.dot(a, b, preferred_element_type=F32)


def nt(a, b):
    return lax.dot_general(a, b, (((1,), (1,)), ((), ())), preferred_element_type=F32)


def eye(n):
    rows = lax.broadcasted_iota(jnp.int32, (n, n), 0)
    cols = lax.broadcasted_iota(jnp.int32, (n, n), 1)
    return jnp.where(rows == cols, 1.0, 0.0).astype(BF16)


def flip(a, n):
    return nt(eye(n), a).astype(BF16)


def normalize(x):
    center = jnp.mean(x, axis=-1, keepdims=True)
    offset = x - center
    spread = jnp.mean(offset * offset, axis=-1, keepdims=True)
    inverse = lax.rsqrt(spread + EPSILON)
    return offset * inverse, inverse


def norm_back(x, upstream):
    normed, inverse = normalize(x)
    first = jnp.mean(upstream, axis=-1, keepdims=True)
    second = jnp.mean(upstream * normed, axis=-1, keepdims=True)
    return inverse * (upstream - first - normed * second)


def cumulative(x):
    return 0.5 * (1.0 + lax.erf(x * 0.7071067811865476))


def density(x):
    return 0.3989422804014327 * jnp.exp(-0.5 * x * x)


def rows_of(window):
    return pl.ds(pl.multiple_of(window * WIN, WIN), WIN)


def spread_bias(bias_ref, layer, lined, table):
    for window in range(4):
        for j in range(162):
            row = window * 18 + j // 9
            value = bias_ref[layer, window // 2, window % 2, :, 128 * j : 128 * j + 128]
            lined[row, j % 9 * 8 : j % 9 * 8 + HEADS, :] = value.astype(F32)
    rows = lax.broadcasted_iota(jnp.int32, (256, 256), 0)
    cols = lax.broadcasted_iota(jnp.int32, (256, 256), 1)
    for r in range(8):
        pick = jnp.where(jnp.logical_and(rows - cols == 16 * r, cols < WIN), 1.0, 0.0).astype(BF16)
        pair = [lined[:, 8 * (r + i) : 8 * (r + i) + 8, :].reshape(576, 128) for i in range(2)]
        placed = nn(jnp.concatenate(pair, axis=1).astype(BF16), pick)
        for part in range(2):
            half = placed[:, 128 * part : 128 * part + 128]
            for row in range(72):
                table[part][64 * row + 8 * r : 64 * row + 8 * r + 8, :] = half[8 * row : 8 * row + 8]


def head_bias(table, window, head):
    at = pl.ds(pl.multiple_of(window * WIN * 8, 8) + head, WIN, stride=8)
    return jnp.concatenate([table[0][at, :], table[1][at, :][:, 0:16]], axis=1)


def pack_bias(main, rest, out_ref):
    def flat(first):
        parts = []
        for r in range(8):
            at = pl.ds(pl.multiple_of(first * 192, 8) + 24 * r, 24)
            parts += [main[at, :], rest[at, :][:, :16]]
        return jnp.concatenate(parts, axis=1)

    def step(group, carry):
        top = flat(group)
        bottom = flat(group + 9)
        for third in range(3):
            both = jnp.concatenate(
                [top[8 * third : 8 * third + 8], bottom[8 * third : 8 * third + 8]], axis=0
            ).astype(BF16)
            for j in range(9):
                out_ref[third * 81 + group * 9 + j] = both[:, 128 * j : 128 * j + 128]
        return carry

    lax.fori_loop(0, 9, step, 0)
    out_ref[243:256] = jnp.zeros((13, 16, 128), BF16)


def pack_weights(wgrad, out_ref):
    for i in range(12):
        block = wgrad[16 * i : 16 * i + 16, :].astype(BF16)
        for j in range(6):
            out_ref[6 * i + j] = block[:, 128 * j : 128 * j + 128]
    out_ref[72:80] = jnp.zeros((8, 16, 128), BF16)


def attention_forward(window, qkv_ref, qkvt_ref, prob_ref, mixedt_ref, mixed_ref, biases, mask):

    qkv = qkv_ref[rows_of(window), :]
    qkvt_ref[window] = flip(qkv, 3 * C)
    for head in range(HEADS):
        lo = head * HD
        keys = qkvt_ref[window, C + lo : C + lo + HD, :]
        values = qkvt_ref[window, 2 * C + lo : 2 * C + lo + HD, :]
        scores = nn(qkv[:, lo : lo + HD], keys) * SCALE + head_bias(biases, window, head)
        weights = jnp.exp(scores)
        if mask is not None:
            weights = weights * mask
        probs = weights / jnp.sum(weights, axis=-1, keepdims=True)
        probs = probs.astype(BF16)
        prob_ref[window * HEADS + head] = probs
        mixedt_ref[window, lo : lo + HD, :] = nt(values, probs).astype(BF16)
    mixed_ref[rows_of(window), :] = flip(mixedt_ref[window], WIN)


def attention_backward(
    window, source_ref, qkvt_ref, prob_ref, mixedt_ref, mgrad_ref, grad_ref,
    w_qkv, w_proj, gradt, sgrad_ref, wgrad, table,
):
    mgrad = mgrad_ref[rows_of(window), :]
    wgrad[:, 3 * C :] += nn(mixedt_ref[window], mgrad)
    grad = grad_ref[rows_of(window), :]
    gt = nt(w_proj, mgrad).astype(BF16)
    for head in range(HEADS):
        lo = head * HD
        queries = qkvt_ref[window, lo : lo + HD, :]
        keys = qkvt_ref[window, C + lo : C + lo + HD, :]
        values = qkvt_ref[window, 2 * C + lo : 2 * C + lo + HD, :]
        probs = prob_ref[window * HEADS + head]
        pgrad = nn(grad[:, lo : lo + HD], values)
        vgrad = nn(gt[lo : lo + HD, :], probs)
        probs = probs.astype(F32)
        delta = jnp.sum(pgrad * probs, axis=-1, keepdims=True)
        sgrad = probs * (pgrad - delta)
        at = pl.ds(window * HEADS + head, WIN, stride=24)
        table[0][at, :] = sgrad[:, :128]
        table[1][at, :] = jnp.concatenate([sgrad[:, 128:], jnp.zeros((WIN, 112), F32)], axis=1)
        sround = sgrad.astype(BF16)
        gradt[lo : lo + HD, :] = (nt(keys, sround) * SCALE).astype(BF16)
        gradt[C + lo : C + lo + HD, :] = (nn(queries, sround) * SCALE).astype(BF16)
        gradt[2 * C + lo : 2 * C + lo + HD, :] = vgrad.astype(BF16)
    all_grad = gradt[...]
    sourcet = flip(source_ref[rows_of(window), :], C)
    wgrad[:, : 3 * C] += nt(sourcet, all_grad)
    sgradt = nn(w_qkv, all_grad).astype(BF16)
    sgrad_ref[rows_of(window), :] = flip(sgradt, WIN)


def mlp_back(middle, upstream, slope, w_in, w_outt):
    act_grad = nn(upstream, w_outt)
    pre_grad = (slope * act_grad).astype(BF16)
    ngrad = nt(pre_grad, w_in)
    return (upstream.astype(F32) + norm_back(middle.astype(F32), ngrad)).astype(BF16)


def region_mask(window):
    last_lat = lax.axis_index("lat") == lax.axis_size("lat") - 1

    def region(tokens):
        level = tokens // 72
        row = tokens // 12 % 6
        upper = jnp.where(window // 2 == 1, level, 0)
        lower = jnp.where(jnp.logical_and(last_lat, window % 2 == 1), row // 3, 0)
        return upper * 2 + lower

    queries = region(lax.broadcasted_iota(jnp.int32, (WIN, WIN), 0))
    keys = region(lax.broadcasted_iota(jnp.int32, (WIN, WIN), 1))
    return jnp.where(queries == keys, 1.0, 0.0)


def place():
    lat, lon = lax.axis_index("lat"), lax.axis_index("lon")
    return lat, lon, lax.rem(lon, ZS), lon // ZS


def neighbour(lat_steps, lon_steps):
    lats, lons = lax.axis_size("lat"), lax.axis_size("lon")
    lat, lon, _, _ = place()
    return lax.rem(lat + lat_steps + lats, lats), lax.rem(lon + lon_steps + lons, lons)


def remote(src, dst, send, recv, device):
    return pltpu.make_async_remote_copy(
        src_ref=src, dst_ref=dst, send_sem=send, recv_sem=recv, device_id=device, device_id_type=MESH
    )


def wait_all(copies):
    for copy in copies:
        copy.wait()


def greet():
    barrier = pltpu.get_barrier_semaphore()
    for k in range(1, 16):
        for device in (neighbour(k, 0), neighbour(0, k)):
            pl.semaphore_signal(barrier, inc=1, device_id=device, device_id_type=MESH)
    pl.semaphore_wait(barrier, 30)


def exchange_kernel(sign, send_ref, out_ref, send_sems, recv_sems):
    barrier = pltpu.get_barrier_semaphore()
    steps = [(0, sign, E0, S0), (sign, 0, S0, D0), (sign, sign, D0, SEND)]
    for lat, lon, _, _ in steps:
        pl.semaphore_signal(barrier, inc=1, device_id=neighbour(-lat, -lon), device_id_type=MESH)
    pl.semaphore_wait(barrier, 3)
    copies = []
    for i, (lat, lon, start, stop) in enumerate(steps):
        piece = pl.ds(start, stop - start)
        copy = pltpu.make_async_remote_copy(
            src_ref=send_ref.at[:, piece],
            dst_ref=out_ref.at[:, piece],
            send_sem=send_sems.at[i],
            recv_sem=recv_sems.at[i],
            device_id=neighbour(lat, lon),
            device_id_type=MESH,
        )
        copy.start()
        copies.append(copy)
    for copy in copies:
        copy.wait()


def exchange(sent, sign, collective_id):
    return pl.pallas_call(
        functools.partial(exchange_kernel, sign),
        out_shape=jax.ShapeDtypeStruct(sent.shape, BF16),
        in_specs=[pl.BlockSpec(memory_space=pltpu.VMEM)],
        out_specs=pl.BlockSpec(memory_space=pltpu.VMEM),
        scratch_shapes=[pltpu.SemaphoreType.DMA((3,)), pltpu.SemaphoreType.DMA((3,))],
        compiler_params=pltpu.CompilerParams(collective_id=collective_id, has_side_effects=True),
    )(sent)


class Ring:
    def __init__(self, rows, own, out, base, bufs, sems):
        self.rows, self.own, self.out, self.base = rows, own, out, base
        self.right_in, self.left_in, self.right_sum, self.left_sum = bufs
        self.sems = sems
        lat, lon, self.z, y = place()
        self.right = (lat, y * ZS + lax.rem(self.z + 1, ZS))
        self.left = (lat, y * ZS + lax.rem(self.z + ZS - 1, ZS))
        self.sums, self.gathers = [], []

    def chunk(self, steps):
        return pl.multiple_of(lax.rem(self.z + steps + 2 * ZS, ZS) * self.rows, self.rows)

    def send(self, kind, step, src, dst, device):
        copy = remote(src, dst, self.sems.at[kind, step], self.sems.at[kind + 1, step], device)
        copy.start()
        return copy

    def reduce(self, step):
        if step:
            for copy in self.sums[-1]:
                copy.wait_recv()
        now = []
        value = self.own(self.chunk(4 - step))
        if step:
            value = (value.astype(F32) + self.right_in[step - 1].astype(F32)).astype(BF16)
        self.right_sum[step] = value
        now.append(self.send(0, step, self.right_sum.at[step], self.right_in.at[step], self.right))
        if step < 3:
            value = self.own(self.chunk(step - 3))
            if step:
                value = (value.astype(F32) + self.left_in[step - 1].astype(F32)).astype(BF16)
            self.left_sum[step] = value
            now.append(self.send(2, step, self.left_sum.at[step], self.left_in.at[step], self.left))
        self.sums.append(now)

    def total(self):
        self.sums[3][0].wait_recv()
        return self.own(self.chunk(0)).astype(F32) + self.right_in[3].astype(F32) + self.left_in[2].astype(F32)

    def piece(self, steps):
        return self.out.at[pl.ds(pl.multiple_of(self.base + self.chunk(steps), self.rows), self.rows)]

    def gather(self, step):
        came = []
        if step:
            for copy in self.gathers[-1]:
                copy.wait_recv()
            came.append((step, self.piece(-step)))
            if step < 4:
                came.append((step + 4, self.piece(step)))
        if step < 4:
            now = [self.send(4, step, self.piece(-step), self.piece(-step), self.right)]
            if step < 3:
                now.append(self.send(6, step, self.piece(step), self.piece(step), self.left))
            self.gathers.append(now)
        return came

    def finish(self):
        for now in self.sums + self.gathers:
            for copy in now:
                copy.wait_send()


def sum_tiles(tiles, out, bufs, sems, y_sems):
    lat, lon, z, y = place()
    partner = (lat, (1 - y) * ZS + z)
    bufs_a, mine, other, bufs_b, half, half_in = bufs
    a = Ring(256, lambda at: tiles[pl.ds(at, 256)], out, 0, bufs_a, sems.at[0])
    base = 2048 + y * 1024
    b = Ring(128, lambda at: half[pl.ds(at, 128)], out, base, bufs_b, sems.at[1])
    away = pl.ds(pl.multiple_of(2048 + (1 - y) * 1024, 1024), 1024)
    here = pl.ds(pl.multiple_of(2048 + y * 1024, 1024), 1024)
    cross = remote(tiles.at[away], half_in, y_sems.at[0, 0], y_sems.at[1, 0], partner)
    cross.start()
    a.reduce(0)
    yield
    a.reduce(1)
    yield
    cross.wait_recv()
    half[...] = (tiles[here].astype(F32) + half_in[...].astype(F32)).astype(BF16)
    b.reduce(0)
    a.reduce(2)
    yield
    b.reduce(1)
    a.reduce(3)
    yield
    b.reduce(2)
    mine[...] = a.total().astype(BF16)
    swap = remote(mine, other, y_sems.at[0, 1], y_sems.at[1, 1], partner)
    swap.start()
    yield
    b.reduce(3)
    swap.wait_recv()
    a.piece(0)[...] = (mine[...].astype(F32) + other[...].astype(F32)).astype(BF16)
    a.gather(0)
    yield
    b.piece(0)[...] = b.total().astype(BF16)
    b.gather(0)
    shared = []

    def share(pieces):
        for slot, piece in pieces:
            copy = remote(piece, piece, y_sems.at[0, 2 + slot], y_sems.at[1, 2 + slot], partner)
            copy.start()
            shared.append(copy)

    share([(0, b.piece(0))])
    a.gather(1)
    yield
    share(b.gather(1))
    a.gather(2)
    yield
    share(b.gather(2))
    a.gather(3)
    yield
    share(b.gather(3))
    a.gather(4)
    yield
    share(b.gather(4))
    wait_all(shared)
    cross.wait_send()
    swap.wait_send()
    a.finish()
    b.finish()


def sum_weights(w, out, part, mid, owned, done, sems, first):
    lat, lon, _, _ = place()
    peers = range(1, 16)
    scatter = []
    for k in peers:
        to = neighbour(k, 0)
        copy = remote(w.at[pl.ds(to[0] * 5, 5)], part.at[k], sems.at[0, k], sems.at[1, k], to)
        copy.start()
        scatter.append(copy)
    yield
    total = w[pl.ds(lat * 5, 5)].astype(F32)
    for k, copy in enumerate(scatter, 1):
        copy.wait_recv()
        total = total + part[k].astype(F32)
    mid[...] = total.astype(BF16)

    def owner(index):
        return jnp.logical_and(index >= first, index < first + 5)

    def to_owner(k, device):
        tile = jnp.clip(device[1] - first, 0, 4)
        return remote(mid.at[tile], owned.at[k], sems.at[2, k], sems.at[3, k], device)

    def from_owner(k, tile, device):
        tile = jnp.clip(tile, 0, 4)
        return remote(done.at[tile], done.at[tile], sems.at[4, k], sems.at[5, k], device)

    for k in peers:
        to = neighbour(0, k)

        @pl.when(owner(to[1]))
        def _():
            to_owner(k, to).start()

    yield

    @pl.when(owner(lon))
    def _():
        mine = jnp.clip(lon - first, 0, 4)
        value = mid[mine].astype(F32)
        for k in peers:
            to_owner(k, (lat, lon)).wait_recv()
            value = value + owned[k].astype(F32)
        done[mine] = value.astype(BF16)
        for k in peers:
            from_owner(k, lon - first, neighbour(0, k)).start()

    yield
    for k in peers:
        source = neighbour(0, -k)

        @pl.when(owner(source[1]))
        def _():
            from_owner(k, source[1] - first, source).wait_recv()

    out[pl.ds(lat * 5, 5)] = done[...]
    spread = []
    for k in peers:
        piece = out.at[pl.ds(lat * 5, 5)]
        copy = remote(piece, piece, sems.at[6, k], sems.at[7, k], neighbour(k, 0))
        copy.start()
        spread.append(copy)
    yield
    wait_all(spread)
    for copy in scatter:
        copy.wait_send()
    for k in peers:
        to = neighbour(0, k)

        @pl.when(owner(to[1]))
        def _():
            to_owner(k, to).wait_send()

    @pl.when(owner(lon))
    def _():
        for k in peers:
            from_owner(k, lon - first, neighbour(0, k)).wait_send()


def advance(*streams):
    for stream in streams:
        next(stream, None)


def drain(fast, slow, rounds):
    step = 0
    while fast:
        fast = [stream for stream in fast if next(stream, 1) is None]
        if step in rounds:
            advance(*slow)
        step += 1
    while slow:
        slow = [stream for stream in slow if next(stream, 1) is None]


def attention_block(x, source, qkv, qkvt, prob, mixedt, mixed, w_qkv, w_proj, w_in, biases, masked):
    source[...] = normalize(x)[0].astype(BF16)
    qkv[...] = nn(source[...], w_qkv[0]).astype(BF16)

    def step(window, carry):
        attention_forward(
            window, qkv, qkvt, prob, mixedt, mixed, biases, region_mask(window) if masked else None
        )
        return carry

    lax.fori_loop(0, 4, step, 0)
    attended = nn(mixed[...], w_proj[0]).astype(BF16)
    middle = (x + attended.astype(F32)).astype(BF16)
    pre = nn(normalize(middle.astype(F32))[0].astype(BF16), w_in[0])
    phi = cumulative(pre)
    return middle, pre, phi, phi + pre * density(pre)


def forward_kernel(
    tok_ref, cot_ref, load_ref, own_ref, send_ref, w_qkv, w_proj, w_in, w_outt, bias_ref,
    x_out, source, qkvt, prob, mixedt, mid_out, slope_out, kept, sent,
    qkv, mixed, main, rest, lined,
):
    cot = nn(load_ref[...], cot_ref[...].reshape(TOK, C)).astype(BF16)
    sent[1] = nn(send_ref[...], cot).astype(BF16)
    kept[1] = nn(own_ref[...], cot).astype(BF16)
    x0 = nn(load_ref[...], tok_ref[...].reshape(TOK, C))
    x_out[...] = x0.astype(BF16)
    lined[...] = jnp.zeros_like(lined)
    spread_bias(bias_ref, 0, lined, (main, rest))
    middle, pre, phi, slope = attention_block(
        x0, source, qkv, qkvt, prob, mixedt, mixed, w_qkv, w_proj, w_in, (main, rest), False
    )
    mid_out[...] = middle
    slope_out[...] = slope.astype(BF16)
    x1 = (middle.astype(F32) + nt((pre * phi).astype(BF16), w_outt[0])).astype(BF16)
    sent[0] = nn(send_ref[...], x1).astype(BF16)
    kept[0] = nn(own_ref[...], x1).astype(BF16)


def middle_kernel(
    kept, arrived, recv_ref, ownt_ref, recvt_ref, w_qkv, w_proj, w_in, w_outt, bias_ref,
    kept_out, sent, tiles, wtiles,
    source, qkv, qkvt, prob, mixedt, mixed, mgrad, grad, gradt, sgrad, wgrad, main24, rest24, main, rest, lined,
):
    x1 = kept[0].astype(F32) + nn(recv_ref[...], arrived[0])
    lined[...] = jnp.zeros_like(lined)
    spread_bias(bias_ref, 0, lined, (main, rest))
    middle, _, _, slope = attention_block(
        x1, source, qkv, qkvt, prob, mixedt, mixed, w_qkv, w_proj, w_in, (main, rest), True
    )
    cot = (kept[1].astype(F32) + nn(recv_ref[...], arrived[1])).astype(BF16)
    mgrad[...] = mlp_back(middle, cot, slope, w_in[0], w_outt[0])
    grad[...] = nt(mgrad[...], w_proj[0]).astype(BF16)
    wgrad[...] = jnp.zeros_like(wgrad)

    def back(window, carry):
        attention_backward(
            window, source, qkvt, prob, mixedt, mgrad, grad, w_qkv[0], w_proj[0], gradt, sgrad, wgrad, (main24, rest24)
        )
        return carry

    lax.fori_loop(0, 4, back, 0)
    result = (mgrad[...].astype(F32) + norm_back(x1, sgrad[...].astype(F32))).astype(BF16)
    sent[0] = nn(recvt_ref[...], result).astype(BF16)
    kept_out[...] = nn(ownt_ref[...], result).astype(BF16)
    pack_bias(main24, rest24, tiles)
    pack_weights(wgrad, wtiles)


def backward_kernel(
    kept, arrived, sendt_ref, loadt_ref, x_ref, source, qkvt, prob, mixedt, mid, slope,
    w_qkv, w_proj, w_in, w_outt,
    grid_out, tiles, wtiles,
    mgrad, grad, gradt, sgrad, wgrad, main24, rest24,
):
    upstream = (kept[...].astype(F32) + nn(sendt_ref[...], arrived[0])).astype(BF16)
    mgrad[...] = mlp_back(mid[...], upstream, slope[...].astype(F32), w_in[0], w_outt[0])
    grad[...] = nt(mgrad[...], w_proj[0]).astype(BF16)
    wgrad[...] = jnp.zeros_like(wgrad)

    def back(window, carry):
        attention_backward(
            window, source, qkvt, prob, mixedt, mgrad, grad, w_qkv[0], w_proj[0], gradt, sgrad, wgrad, (main24, rest24)
        )
        return carry

    lax.fori_loop(0, 4, back, 0)
    result = (mgrad[...].astype(F32) + norm_back(x_ref[...].astype(F32), sgrad[...].astype(F32))).astype(BF16)
    grid_out[...] = nn(loadt_ref[...], result).astype(BF16).reshape(144, 4, C)
    pack_bias(main24, rest24, tiles)
    pack_weights(wgrad, wtiles)


def compute_call(kernel, operands, outs, scratch):
    specs, arrays = [], []
    once = pl.Buffered(1)
    for operand in operands:
        array, layer = operand if isinstance(operand, tuple) else (operand, None)
        arrays.append(array)
        shape = array.shape if layer is None else (1,) + array.shape[1:]
        index = (0 if layer is None else layer,) + (0,) * (array.ndim - 1)
        specs.append(pl.BlockSpec(shape, functools.partial(lambda at, _: at, index), pipeline_mode=once))
    return pl.pallas_call(
        kernel,
        out_shape=[jax.ShapeDtypeStruct(shape, kind) for shape, kind in outs],
        grid=(1,),
        in_specs=specs,
        out_specs=[
            pl.BlockSpec(shape, functools.partial(lambda at, _: at, (0,) * len(shape)), pipeline_mode=once)
            for shape, kind in outs
        ],
        scratch_shapes=[pltpu.VMEM(shape, kind) for shape, kind in scratch],
        compiler_params=pltpu.CompilerParams(vmem_limit_bytes=VMEM_LIMIT),
    )(*arrays)


def sum_kernel(
    tiles0, tiles1, wtiles0, wtiles1, bias_out, w_out,
    a_right_in, a_left_in, a_right_sum, a_left_sum, mine, other,
    b_right_in, b_left_in, b_right_sum, b_left_sum, half, half_in, ring_sems, y_sems,
    wpart, wmid, wowned, wdone, w_sems,
):
    greet()
    streams = []
    for layer, (tiles, wtiles) in enumerate(((tiles0, wtiles0), (tiles1, wtiles1))):
        bufs_a = [ref.at[layer] for ref in (a_right_in, a_left_in, a_right_sum, a_left_sum)]
        bufs_b = [ref.at[layer] for ref in (b_right_in, b_left_in, b_right_sum, b_left_sum)]
        bufs = (bufs_a, mine.at[layer], other.at[layer], bufs_b, half.at[layer], half_in.at[layer])
        streams.append(sum_tiles(tiles, bias_out.at[layer], bufs, ring_sems.at[layer], y_sems.at[layer]))
        streams.append(
            sum_weights(
                wtiles, w_out.at[layer], wpart.at[layer], wmid.at[layer], wowned.at[layer],
                wdone.at[layer], w_sems.at[layer], 8 * layer,
            )
        )
    drain(streams[::2], streams[1::2], (0, 2, 5, 7))


def sum_all(tiles0, tiles1, wtiles0, wtiles1):
    vmem, dma = pltpu.VMEM, pltpu.SemaphoreType.DMA

    def ring(rows):
        return [vmem((2, n, rows, 128), BF16) for n in (4, 3, 4, 3)]

    return pl.pallas_call(
        sum_kernel,
        out_shape=[
            jax.ShapeDtypeStruct((2, ROWS, 128), BF16),
            jax.ShapeDtypeStruct((2, 80, 16, 128), BF16),
        ],
        in_specs=[pl.BlockSpec(memory_space=vmem)] * 4,
        out_specs=[pl.BlockSpec(memory_space=vmem)] * 2,
        scratch_shapes=[
            *ring(256),
            vmem((2, 256, 128), BF16),
            vmem((2, 256, 128), BF16),
            *ring(128),
            vmem((2, 1024, 128), BF16),
            vmem((2, 1024, 128), BF16),
            dma((2, 2, 8, 4)),
            dma((2, 2, 10)),
            vmem((2, 16, 5, 16, 128), BF16),
            vmem((2, 5, 16, 128), BF16),
            vmem((2, 16, 16, 128), BF16),
            vmem((2, 5, 16, 128), BF16),
            dma((2, 8, 16)),
        ],
        compiler_params=pltpu.CompilerParams(
            collective_id=2, has_side_effects=True, vmem_limit_bytes=VMEM_LIMIT
        ),
    )(tiles0, tiles1, wtiles0, wtiles1)


def unpack_kernel(tiles_ref, wtiles_ref, bias_out, qkv_out, proj_out):
    for j in range(81):
        rows = [tiles_ref[0, 16 * (third * 81 + j) : 16 * (third * 81 + j) + 16, :].astype(F32) for third in range(3)]
        for half in range(2):
            lanes = slice(half * 10368 + 128 * j, half * 10368 + 128 * j + 128)
            full = jnp.concatenate([part[8 * half : 8 * half + 8] for part in rows], axis=0)
            for window in range(4):
                bias_out[0, window // 2, window % 2, :, lanes] = full[6 * window : 6 * window + 6]
    for i in range(12):
        row = jnp.concatenate([wtiles_ref[0, 6 * i + j].astype(F32) for j in range(6)], axis=1)
        qkv_out[0, 16 * i : 16 * i + 16, :] = row[:, : 3 * C]
        proj_out[0, 16 * i : 16 * i + 16, :] = row[:, 3 * C :]


def unpack(tiles, wtiles):
    return pl.pallas_call(
        unpack_kernel,
        grid=(2,),
        out_shape=[
            jax.ShapeDtypeStruct((2, 2, 2, HEADS, WIN * WIN), F32),
            jax.ShapeDtypeStruct((2, C, 3 * C), F32),
            jax.ShapeDtypeStruct((2, C, C), F32),
        ],
        in_specs=[
            pl.BlockSpec((1, ROWS, 128), lambda l: (l, 0, 0)),
            pl.BlockSpec((1, 80, 16, 128), lambda l: (l, 0, 0, 0)),
        ],
        out_specs=[
            pl.BlockSpec((1, 2, 2, HEADS, WIN * WIN), lambda l: (l, 0, 0, 0, 0)),
            pl.BlockSpec((1, C, 3 * C), lambda l: (l, 0, 0)),
            pl.BlockSpec((1, C, C), lambda l: (l, 0, 0)),
        ],
        compiler_params=pltpu.CompilerParams(vmem_limit_bytes=VMEM_LIMIT),
    )(tiles, wtiles)


def to_cells(grid):
    return grid.transpose(1, 2, 0, 3).reshape(144, 4, C)


def shards(tokens, cotangent, w_qkv, w_proj, w_in, w_out, earth_bias):
    load, own, send, recv = _matrices()
    loadt, ownt, recvt, sendt = (jnp.asarray(m.T, BF16) for m in (load, own, recv, send))
    load, own, send, recv = (jnp.asarray(m, BF16) for m in (load, own, send, recv))
    params = [w_qkv, w_proj, w_in, w_out.transpose(0, 2, 1)]
    tok, wide = ((TOK, C), BF16), ((TOK, 3 * C), BF16)
    qkvt, mixedt = ((4, 3 * C, WIN), BF16), ((4, C, WIN), BF16)
    prob = ((24, WIN, WIN), BF16)
    spread = [((4 * WIN * 8 + 8, 128), F32)] * 2 + [((72, 72, 128), F32)]
    back = [tok, tok, ((3 * C, WIN), BF16), tok, ((C, FF), F32), ((WIN * 24, 128), F32), ((WIN * 24, 128), F32)]
    sums = [((256, 16, 128), BF16), ((80, 16, 128), BF16)]

    *state, kept, sent = compute_call(
        forward_kernel,
        [to_cells(tokens), to_cells(cotangent), load, own, send] + [(p, 0) for p in params + [earth_bias]],
        [tok, tok, qkvt, prob, mixedt, tok, ((TOK, FF), BF16), ((2, TOK, C), BF16), ((2, SEND, C), BF16)],
        [wide, tok] + spread,
    )
    arrived = exchange(sent, -1, 0)
    kept, sent, tiles1, wtiles1 = compute_call(
        middle_kernel,
        [kept, arrived, recv, ownt, recvt] + [(p, 1) for p in params + [earth_bias]],
        [tok, ((1, SEND, C), BF16)] + sums,
        [tok, wide, qkvt, prob, mixedt, tok] + back + spread,
    )
    arrived = exchange(sent, 1, 1)
    grid, tiles0, wtiles0 = compute_call(
        backward_kernel,
        [kept, arrived, sendt, loadt] + state + [(p, 0) for p in params],
        [((144, 4, C), BF16)] + sums,
        back,
    )
    tiles, wtiles = sum_all(tiles0.reshape(ROWS, 128), tiles1.reshape(ROWS, 128), wtiles0, wtiles1)
    bias_grad, qkv_grad, proj_grad = unpack(tiles, wtiles)
    grid = grid.reshape(12, 12, 4, C).transpose(2, 0, 1, 3)
    return grid, qkv_grad, proj_grad, bias_grad


def solution(mesh):
    return jax.shard_map(
        shards,
        mesh=mesh,
        in_specs=(
            P(None, "lat", "lon", None),
            P(None, "lat", "lon", None),
            P(),
            P(),
            P(),
            P(),
            P(None, None, "lat", None, None),
        ),
        out_specs=(P(None, "lat", "lon", None), P(), P(), P(None, None, "lat", None, None)),
        check_vma=False,
    )
```

```python
import functools

import jax
import jax.numpy as jnp
import numpy as np
from jax import lax
from jax.experimental import pallas as pl
from jax.experimental.pallas import tpu as pltpu
from jax.sharding import PartitionSpec as P

F32 = jnp.float32
BF16 = jnp.bfloat16
C = 192
HEADS = 6
HD = 32
FF = 768
WIN = 144
TOK = 576
EPSILON = 1e-05
SCALE = HD ** (-0.5)
MESH = pl.DeviceIdType.MESH
E0, S0, D0, SEND = 0, 224, 304, 384
VMEM_LIMIT = 56 * 1024 * 1024
ZS = 8
PAIRS = 12
FLAT = 3888
ROWS = 4096


def _plain_index(level, row, col):
    window = (level // 2) * 2 + row // 6
    return window * WIN + (level % 2) * 72 + (row % 6) * 12 + col


def _matrices():
    load = np.zeros((TOK, TOK), np.float32)
    own = np.zeros((TOK, TOK), np.float32)
    send = np.zeros((SEND, TOK), np.float32)
    recv = np.zeros((TOK, SEND), np.float32)
    for level in range(4):
        for row in range(12):
            for col in range(12):
                here = _plain_index(level, row, col)
                load[here, (row * 12 + col) * 4 + level] = 1
                target_row, target_col = row - 3, col - 6
                target = _plain_index((level - 1) % 4, target_row % 12, target_col % 12)
                if target_row >= 0 and target_col >= 0:
                    own[target, here] = 1
                    continue
                if target_row >= 0:
                    slot = E0 + (level * 9 + row - 3) * 6 + col
                elif target_col >= 0:
                    slot = S0 + (level * 3 + row) * 6 + col - 6
                else:
                    slot = D0 + (level * 3 + row) * 6 + col
                send[slot, here] = 1
                recv[target, slot] = 1
    return load, own, send, recv


def nn(a, b):
    return jnp.dot(a, b, preferred_element_type=F32)


def nt(a, b):
    return lax.dot_general(a, b, (((1,), (1,)), ((), ())), preferred_element_type=F32)


def eye(n):
    rows = lax.broadcasted_iota(jnp.int32, (n, n), 0)
    cols = lax.broadcasted_iota(jnp.int32, (n, n), 1)
    return jnp.where(rows == cols, 1.0, 0.0).astype(BF16)


def flip(a, n):
    return nt(eye(n), a).astype(BF16)


def normalize(x):
    center = jnp.mean(x, axis=-1, keepdims=True)
    offset = x - center
    spread = jnp.mean(offset * offset, axis=-1, keepdims=True)
    inverse = lax.rsqrt(spread + EPSILON)
    return offset * inverse, inverse


def norm_back(x, upstream):
    normed, inverse = normalize(x)
    first = jnp.mean(upstream, axis=-1, keepdims=True)
    second = jnp.mean(upstream * normed, axis=-1, keepdims=True)
    return inverse * (upstream - first - normed * second)


def cumulative(x):
    return 0.5 * (1.0 + lax.erf(x * 0.7071067811865476))


def density(x):
    return 0.3989422804014327 * jnp.exp(-0.5 * x * x)


def rows_of(window):
    return pl.ds(pl.multiple_of(window * WIN, WIN), WIN)


def spread_bias(bias_ref, layer, lined, table):
    for window in range(4):
        for j in range(162):
            row = window * 18 + j // 9
            value = bias_ref[layer, window // 2, window % 2, :, 128 * j : 128 * j + 128]
            lined[row, j % 9 * 8 : j % 9 * 8 + HEADS, :] = value.astype(F32)
    rows = lax.broadcasted_iota(jnp.int32, (256, 256), 0)
    cols = lax.broadcasted_iota(jnp.int32, (256, 256), 1)
    for r in range(8):
        pick = jnp.where(jnp.logical_and(rows - cols == 16 * r, cols < WIN), 1.0, 0.0).astype(BF16)
        pair = [lined[:, 8 * (r + i) : 8 * (r + i) + 8, :].reshape(576, 128) for i in range(2)]
        placed = nn(jnp.concatenate(pair, axis=1).astype(BF16), pick)
        for part in range(2):
            half = placed[:, 128 * part : 128 * part + 128]
            for row in range(72):
                table[part][64 * row + 8 * r : 64 * row + 8 * r + 8, :] = half[8 * row : 8 * row + 8]


def head_bias(table, window, head):
    at = pl.ds(pl.multiple_of(window * WIN * 8, 8) + head, WIN, stride=8)
    return jnp.concatenate([table[0][at, :], table[1][at, :][:, 0:16]], axis=1)


def pack_bias(main, rest, out_ref):
    def flat(first):
        parts = []
        for r in range(8):
            at = pl.ds(pl.multiple_of(first * 192, 8) + 24 * r, 24)
            parts += [main[at, :], rest[at, :][:, :16]]
        return jnp.concatenate(parts, axis=1)

    def step(group, carry):
        top = flat(group)
        bottom = flat(group + 9)
        for third in range(3):
            both = jnp.concatenate(
                [top[8 * third : 8 * third + 8], bottom[8 * third : 8 * third + 8]], axis=0
            ).astype(BF16)
            for j in range(9):
                at = pl.multiple_of((third * 81 + group * 9 + j) * 16, 16)
                out_ref[pl.ds(at, 16), :] = both[:, 128 * j : 128 * j + 128]
        return carry

    lax.fori_loop(0, 9, step, 0)
    out_ref[FLAT:ROWS, :] = jnp.zeros((ROWS - FLAT, 128), BF16)


def pack_weights(wgrad, out_ref):
    for i in range(12):
        block = wgrad[16 * i : 16 * i + 16, :].astype(BF16)
        for j in range(6):
            out_ref[6 * i + j] = block[:, 128 * j : 128 * j + 128]
    out_ref[72:80] = jnp.zeros((8, 16, 128), BF16)


def attention_forward(window, qkv_ref, qkvt_ref, prob_ref, mixedt_ref, mixed_ref, biases, mask):

    qkv = qkv_ref[rows_of(window), :]
    qkvt_ref[window] = flip(qkv, 3 * C)
    for head in range(HEADS):
        lo = head * HD
        keys = qkvt_ref[window, C + lo : C + lo + HD, :]
        values = qkvt_ref[window, 2 * C + lo : 2 * C + lo + HD, :]
        scores = nn(qkv[:, lo : lo + HD], keys) * SCALE + head_bias(biases, window, head)
        weights = jnp.exp(scores)
        if mask is not None:
            weights = weights * mask
        probs = weights / jnp.sum(weights, axis=-1, keepdims=True)
        probs = probs.astype(BF16)
        prob_ref[window * HEADS + head] = probs
        mixedt_ref[window, lo : lo + HD, :] = nt(values, probs).astype(BF16)
    mixed_ref[rows_of(window), :] = flip(mixedt_ref[window], WIN)


def attention_backward(
    window, source_ref, qkvt_ref, prob_ref, mixedt_ref, mgrad_ref, grad_ref,
    w_qkv, w_proj, gradt, sgrad_ref, wgrad, table,
):
    mgrad = mgrad_ref[rows_of(window), :]
    wgrad[:, 3 * C :] += nn(mixedt_ref[window], mgrad)
    grad = grad_ref[rows_of(window), :]
    gt = nt(w_proj, mgrad).astype(BF16)
    for head in range(HEADS):
        lo = head * HD
        queries = qkvt_ref[window, lo : lo + HD, :]
        keys = qkvt_ref[window, C + lo : C + lo + HD, :]
        values = qkvt_ref[window, 2 * C + lo : 2 * C + lo + HD, :]
        probs = prob_ref[window * HEADS + head]
        pgrad = nn(grad[:, lo : lo + HD], values)
        vgrad = nn(gt[lo : lo + HD, :], probs)
        probs = probs.astype(F32)
        delta = jnp.sum(pgrad * probs, axis=-1, keepdims=True)
        sgrad = probs * (pgrad - delta)
        at = pl.ds(window * HEADS + head, WIN, stride=24)
        table[0][at, :] = sgrad[:, :128]
        table[1][at, :] = jnp.concatenate([sgrad[:, 128:], jnp.zeros((WIN, 112), F32)], axis=1)
        sround = sgrad.astype(BF16)
        gradt[lo : lo + HD, :] = (nt(keys, sround) * SCALE).astype(BF16)
        gradt[C + lo : C + lo + HD, :] = (nn(queries, sround) * SCALE).astype(BF16)
        gradt[2 * C + lo : 2 * C + lo + HD, :] = vgrad.astype(BF16)
    all_grad = gradt[...]
    sourcet = flip(source_ref[rows_of(window), :], C)
    wgrad[:, : 3 * C] += nt(sourcet, all_grad)
    sgradt = nn(w_qkv, all_grad).astype(BF16)
    sgrad_ref[rows_of(window), :] = flip(sgradt, WIN)


def mlp_back(middle, upstream, slope, w_in, w_outt):
    act_grad = nn(upstream, w_outt)
    pre_grad = (slope * act_grad).astype(BF16)
    ngrad = nt(pre_grad, w_in)
    return (upstream.astype(F32) + norm_back(middle.astype(F32), ngrad)).astype(BF16)


def region_mask(window):
    last_lat = lax.axis_index("lat") == lax.axis_size("lat") - 1

    def region(tokens):
        level = tokens // 72
        row = tokens // 12 % 6
        upper = jnp.where(window // 2 == 1, level, 0)
        lower = jnp.where(jnp.logical_and(last_lat, window % 2 == 1), row // 3, 0)
        return upper * 2 + lower

    queries = region(lax.broadcasted_iota(jnp.int32, (WIN, WIN), 0))
    keys = region(lax.broadcasted_iota(jnp.int32, (WIN, WIN), 1))
    return jnp.where(queries == keys, 1.0, 0.0)


def place():
    lat, lon = lax.axis_index("lat"), lax.axis_index("lon")
    return lat, lon, lax.rem(lon, ZS), lon // ZS


def neighbour(lat_steps, lon_steps):
    lats, lons = lax.axis_size("lat"), lax.axis_size("lon")
    lat, lon, _, _ = place()
    return lax.rem(lat + lat_steps + lats, lats), lax.rem(lon + lon_steps + lons, lons)


def remote(src, dst, send, recv, device):
    return pltpu.make_async_remote_copy(
        src_ref=src, dst_ref=dst, send_sem=send, recv_sem=recv, device_id=device, device_id_type=MESH
    )


def greet():
    barrier = pltpu.get_barrier_semaphore()
    for k in range(1, 16):
        for device in (neighbour(k, 0), neighbour(0, k)):
            pl.semaphore_signal(barrier, inc=1, device_id=device, device_id_type=MESH)
    for k in (-1, 1):
        pl.semaphore_signal(barrier, inc=1, device_id=neighbour(k, k), device_id_type=MESH)
    return barrier


def halo(src, dst, sign, send, recv):
    steps = [(0, sign, E0, S0), (sign, 0, S0, D0), (sign, sign, D0, SEND)]
    copies = []
    for i, (lat, lon, start, stop) in enumerate(steps):
        piece = pl.ds(start, stop - start)
        copy = remote(src.at[piece], dst.at[piece], send.at[i], recv.at[i], neighbour(lat, lon))
        copy.start()
        copies.append(copy)
    return copies


def wait_all(copies):
    for copy in copies:
        copy.wait()


class Ring:
    def __init__(self, rows, own, out, base, bufs, sems):
        self.rows, self.own, self.out, self.base = rows, own, out, base
        self.right_in, self.left_in, self.right_sum, self.left_sum = bufs
        self.sems = sems
        lat, lon, self.z, y = place()
        self.right = (lat, y * ZS + lax.rem(self.z + 1, ZS))
        self.left = (lat, y * ZS + lax.rem(self.z + ZS - 1, ZS))
        self.sums, self.gathers = [], []

    def chunk(self, steps):
        return pl.multiple_of(lax.rem(self.z + steps + 2 * ZS, ZS) * self.rows, self.rows)

    def send(self, kind, step, src, dst, device):
        copy = remote(src, dst, self.sems.at[kind, step], self.sems.at[kind + 1, step], device)
        copy.start()
        return copy

    def reduce(self, step):
        if step:
            for copy in self.sums[-1]:
                copy.wait_recv()
        now = []
        value = self.own(self.chunk(4 - step))
        if step:
            value = (value.astype(F32) + self.right_in[step - 1].astype(F32)).astype(BF16)
        self.right_sum[step] = value
        now.append(self.send(0, step, self.right_sum.at[step], self.right_in.at[step], self.right))
        if step < 3:
            value = self.own(self.chunk(step - 3))
            if step:
                value = (value.astype(F32) + self.left_in[step - 1].astype(F32)).astype(BF16)
            self.left_sum[step] = value
            now.append(self.send(2, step, self.left_sum.at[step], self.left_in.at[step], self.left))
        self.sums.append(now)

    def total(self):
        self.sums[3][0].wait_recv()
        return self.own(self.chunk(0)).astype(F32) + self.right_in[3].astype(F32) + self.left_in[2].astype(F32)

    def piece(self, steps):
        return self.out.at[pl.ds(pl.multiple_of(self.base + self.chunk(steps), self.rows), self.rows)]

    def gather(self, step):
        came = []
        if step:
            for copy in self.gathers[-1]:
                copy.wait_recv()
            came.append((step, self.piece(-step)))
            if step < 4:
                came.append((step + 4, self.piece(step)))
        if step < 4:
            now = [self.send(4, step, self.piece(-step), self.piece(-step), self.right)]
            if step < 3:
                now.append(self.send(6, step, self.piece(step), self.piece(step), self.left))
            self.gathers.append(now)
        return came

    def finish(self):
        for now in self.sums + self.gathers:
            for copy in now:
                copy.wait_send()


def sum_tiles(tiles, out, bufs, sems, y_sems):
    lat, lon, z, y = place()
    partner = (lat, (1 - y) * ZS + z)
    bufs_a, mine, other, bufs_b, half, half_in = bufs
    a = Ring(256, lambda at: tiles[pl.ds(at, 256)], out, 0, bufs_a, sems.at[0])
    base = 2048 + y * 1024
    b = Ring(128, lambda at: half[pl.ds(at, 128)], out, base, bufs_b, sems.at[1])
    away = pl.ds(pl.multiple_of(2048 + (1 - y) * 1024, 1024), 1024)
    here = pl.ds(pl.multiple_of(2048 + y * 1024, 1024), 1024)
    cross = remote(tiles.at[away], half_in, y_sems.at[0, 0], y_sems.at[1, 0], partner)
    cross.start()
    a.reduce(0)
    yield
    a.reduce(1)
    yield
    cross.wait_recv()
    half[...] = (tiles[here].astype(F32) + half_in[...].astype(F32)).astype(BF16)
    b.reduce(0)
    a.reduce(2)
    yield
    b.reduce(1)
    a.reduce(3)
    yield
    b.reduce(2)
    mine[...] = a.total().astype(BF16)
    swap = remote(mine, other, y_sems.at[0, 1], y_sems.at[1, 1], partner)
    swap.start()
    yield
    b.reduce(3)
    swap.wait_recv()
    a.piece(0)[...] = (mine[...].astype(F32) + other[...].astype(F32)).astype(BF16)
    a.gather(0)
    yield
    b.piece(0)[...] = b.total().astype(BF16)
    b.gather(0)
    shared = []

    def share(pieces):
        for slot, piece in pieces:
            copy = remote(piece, piece, y_sems.at[0, 2 + slot], y_sems.at[1, 2 + slot], partner)
            copy.start()
            shared.append(copy)

    share([(0, b.piece(0))])
    a.gather(1)
    yield
    share(b.gather(1))
    a.gather(2)
    yield
    share(b.gather(2))
    a.gather(3)
    yield
    share(b.gather(3))
    a.gather(4)
    yield
    share(b.gather(4))
    wait_all(shared)
    cross.wait_send()
    swap.wait_send()
    a.finish()
    b.finish()


def sum_weights(w, out, part, mid, owned, done, sems, first):
    lat, lon, _, _ = place()
    peers = range(1, 16)
    scatter = []
    for k in peers:
        to = neighbour(k, 0)
        copy = remote(w.at[pl.ds(to[0] * 5, 5)], part.at[k], sems.at[0, k], sems.at[1, k], to)
        copy.start()
        scatter.append(copy)
    yield
    total = w[pl.ds(lat * 5, 5)].astype(F32)
    for k, copy in enumerate(scatter, 1):
        copy.wait_recv()
        total = total + part[k].astype(F32)
    mid[...] = total.astype(BF16)

    def owner(index):
        return jnp.logical_and(index >= first, index < first + 5)

    def to_owner(k, device):
        tile = jnp.clip(device[1] - first, 0, 4)
        return remote(mid.at[tile], owned.at[k], sems.at[2, k], sems.at[3, k], device)

    def from_owner(k, tile, device):
        tile = jnp.clip(tile, 0, 4)
        return remote(done.at[tile], done.at[tile], sems.at[4, k], sems.at[5, k], device)

    for k in peers:
        to = neighbour(0, k)

        @pl.when(owner(to[1]))
        def _():
            to_owner(k, to).start()

    yield

    @pl.when(owner(lon))
    def _():
        mine = jnp.clip(lon - first, 0, 4)
        value = mid[mine].astype(F32)
        for k in peers:
            to_owner(k, (lat, lon)).wait_recv()
            value = value + owned[k].astype(F32)
        done[mine] = value.astype(BF16)
        for k in peers:
            from_owner(k, lon - first, neighbour(0, k)).start()

    yield
    for k in peers:
        source = neighbour(0, -k)

        @pl.when(owner(source[1]))
        def _():
            from_owner(k, source[1] - first, source).wait_recv()

    out[pl.ds(lat * 5, 5)] = done[...]
    spread = []
    for k in peers:
        piece = out.at[pl.ds(lat * 5, 5)]
        copy = remote(piece, piece, sems.at[6, k], sems.at[7, k], neighbour(k, 0))
        copy.start()
        spread.append(copy)
    yield
    wait_all(spread)
    for copy in scatter:
        copy.wait_send()
    for k in peers:
        to = neighbour(0, k)

        @pl.when(owner(to[1]))
        def _():
            to_owner(k, to).wait_send()

    @pl.when(owner(lon))
    def _():
        for k in peers:
            from_owner(k, lon - first, neighbour(0, k)).wait_send()


def advance(*streams):
    for stream in streams:
        next(stream, None)


def drain(fast, slow, rounds):
    step = 0
    while fast:
        fast = [stream for stream in fast if next(stream, 1) is None]
        if step in rounds:
            advance(*slow)
        step += 1
    while slow:
        slow = [stream for stream in slow if next(stream, 1) is None]


def kernel(
    tok_ref, cot_ref, load_ref, own_ref, send_ref, recv_ref, loadt_ref, ownt_ref, recvt_ref, sendt_ref,
    w_qkv, w_proj, w_in, w_outt, bias_ref,
    grid_out, bias_out, w_out,
    x0_s, source, qkv, qkvt, prob, mixedt, mixed, mid_s, slope_s, mgrad, grad, gradt, sgrad, wgrad,
    main24, rest24, lined, main, rest, tiles, wtiles, sent, arrived,
    halo_sems, a_right_in, a_left_in, a_right_sum, a_left_sum, mine, other,
    b_right_in, b_left_in, b_right_sum, b_left_sum, half, half_in, ring_sems, y_sems,
    wpart, wmid, wowned, wdone, w_sems,
):
    barrier = greet()
    lined[...] = jnp.zeros_like(lined)

    def forward(x, layer, masked):
        source[layer] = normalize(x)[0].astype(BF16)
        qkv[...] = nn(source[layer], w_qkv[layer]).astype(BF16)
        spread_bias(bias_ref, layer, lined, (main, rest))

        def step(window, carry):
            attention_forward(
                window, qkv, qkvt.at[layer], prob.at[layer], mixedt.at[layer], mixed, (main, rest),
                region_mask(window) if masked else None,
            )
            return carry

        lax.fori_loop(0, 4, step, 0)
        attended = nn(mixed[...], w_proj[layer]).astype(BF16)
        middle = (x + attended.astype(F32)).astype(BF16)
        pre = nn(normalize(middle.astype(F32))[0].astype(BF16), w_in[layer])
        phi = cumulative(pre)
        return middle, pre, phi, phi + pre * density(pre)

    def backward(window, layer):
        attention_backward(
            window, source.at[layer], qkvt.at[layer], prob.at[layer], mixedt.at[layer], mgrad, grad,
            w_qkv[layer], w_proj[layer], gradt, sgrad, wgrad, (main24, rest24),
        )

    def streams(layer):
        bufs_a = [ref.at[layer] for ref in (a_right_in, a_left_in, a_right_sum, a_left_sum)]
        bufs_b = [ref.at[layer] for ref in (b_right_in, b_left_in, b_right_sum, b_left_sum)]
        bufs = (bufs_a, mine.at[layer], other.at[layer], bufs_b, half.at[layer], half_in.at[layer])
        bias_sum = sum_tiles(tiles.at[layer], bias_out.at[layer], bufs, ring_sems.at[layer], y_sems.at[layer])
        weight_sum = sum_weights(
            wtiles.at[layer], w_out.at[layer], wpart.at[layer], wmid.at[layer], wowned.at[layer],
            wdone.at[layer], w_sems.at[layer], 8 * layer,
        )
        return bias_sum, weight_sum

    cot = nn(load_ref[...], cot_ref[...].reshape(TOK, C)).astype(BF16)
    sent[0] = nn(send_ref[...], cot).astype(BF16)
    pl.semaphore_wait(barrier, 32)
    cot_copies = halo(sent.at[0], arrived.at[0], -1, halo_sems.at[0, 0], halo_sems.at[0, 1])
    cot = nn(own_ref[...], cot)

    x0 = nn(load_ref[...], tok_ref[...].reshape(TOK, C))
    x0_s[...] = x0.astype(BF16)
    middle, pre, phi, slope = forward(x0, 0, False)
    mid_s[...] = middle
    slope_s[...] = slope
    x1 = (middle.astype(F32) + nt((pre * phi).astype(BF16), w_outt[0])).astype(BF16)
    sent[1] = nn(send_ref[...], x1).astype(BF16)
    x1_copies = halo(sent.at[1], arrived.at[1], -1, halo_sems.at[1, 0], halo_sems.at[1, 1])
    x1 = nn(own_ref[...], x1)

    wait_all(x1_copies)
    x1 = x1 + nn(recv_ref[...], arrived[1])
    middle, pre, phi, slope = forward(x1, 1, True)
    wait_all(cot_copies)
    cot = (cot + nn(recv_ref[...], arrived[0])).astype(BF16)
    mgrad[...] = mlp_back(middle, cot, slope, w_in[1], w_outt[1])
    grad[...] = nt(mgrad[...], w_proj[1]).astype(BF16)
    wgrad[...] = jnp.zeros_like(wgrad)

    def back(window, carry):
        backward(window, 1)
        return carry

    lax.fori_loop(0, 4, back, 0)
    result = (mgrad[...].astype(F32) + norm_back(x1, sgrad[...].astype(F32))).astype(BF16)
    sent[2] = nn(recvt_ref[...], result).astype(BF16)
    back_copies = halo(sent.at[2], arrived.at[2], 1, halo_sems.at[2, 0], halo_sems.at[2, 1])
    upstream = nn(ownt_ref[...], result)
    pack_bias(main24, rest24, tiles.at[1])
    pack_weights(wgrad, wtiles.at[1])
    bias1, weight1 = streams(1)
    advance(bias1, weight1)

    wait_all(back_copies)
    upstream = (upstream + nn(sendt_ref[...], arrived[2])).astype(BF16)
    mgrad[...] = mlp_back(mid_s[...], upstream, slope_s[...], w_in[0], w_outt[0])
    advance(bias1, weight1)
    grad[...] = nt(mgrad[...], w_proj[0]).astype(BF16)
    wgrad[...] = jnp.zeros_like(wgrad)
    for window in range(4):
        backward(window, 0)
        advance(bias1, weight1)
    pack_bias(main24, rest24, tiles.at[0])
    pack_weights(wgrad, wtiles.at[0])
    bias0, weight0 = streams(0)
    advance(bias0, weight0, bias1)
    result = (mgrad[...].astype(F32) + norm_back(x0_s[...].astype(F32), sgrad[...].astype(F32))).astype(BF16)
    grid_out[...] = nn(loadt_ref[...], result).astype(BF16).reshape(144, 4, C)
    drain([bias1, bias0], [weight1, weight0], (0, 2, 5, 7))


def run(tokens, cotangent, matrices, params, bias):
    vmem, dma = pltpu.VMEM, pltpu.SemaphoreType.DMA

    def ring(rows):
        return [vmem((2, n, rows, 128), BF16) for n in (4, 3, 4, 3)]

    tok = vmem((TOK, C), BF16)
    scratch = [
        tok,
        vmem((2, TOK, C), BF16),
        vmem((TOK, 3 * C), BF16),
        vmem((2, 4, 3 * C, WIN), BF16),
        vmem((2, 24, WIN, WIN), BF16),
        vmem((2, 4, C, WIN), BF16),
        tok,
        tok,
        vmem((TOK, FF), F32),
        tok,
        tok,
        vmem((3 * C, WIN), BF16),
        tok,
        vmem((C, FF), F32),
        vmem((WIN * 24, 128), F32),
        vmem((WIN * 24, 128), F32),
        vmem((72, 72, 128), F32),
        vmem((4 * WIN * 8 + 8, 128), F32),
        vmem((4 * WIN * 8 + 8, 128), F32),
        vmem((2, ROWS, 128), BF16),
        vmem((2, 80, 16, 128), BF16),
        vmem((3, SEND, C), BF16),
        vmem((3, SEND, C), BF16),
        dma((3, 2, 3)),
        *ring(256),
        vmem((2, 256, 128), BF16),
        vmem((2, 256, 128), BF16),
        *ring(128),
        vmem((2, 1024, 128), BF16),
        vmem((2, 1024, 128), BF16),
        dma((2, 2, 8, 4)),
        dma((2, 2, 10)),
        vmem((2, 16, 5, 16, 128), BF16),
        vmem((2, 5, 16, 128), BF16),
        vmem((2, 16, 16, 128), BF16),
        vmem((2, 5, 16, 128), BF16),
        dma((2, 8, 16)),
    ]
    operands = [tokens, cotangent, *matrices, *params, bias]
    return pl.pallas_call(
        kernel,
        out_shape=[
            jax.ShapeDtypeStruct((144, 4, C), BF16),
            jax.ShapeDtypeStruct((2, ROWS, 128), BF16),
            jax.ShapeDtypeStruct((2, 80, 16, 128), BF16),
        ],
        in_specs=[pl.BlockSpec(memory_space=vmem)] * len(operands),
        out_specs=[pl.BlockSpec(memory_space=vmem)] * 3,
        scratch_shapes=scratch,
        compiler_params=pltpu.CompilerParams(
            collective_id=0, has_side_effects=True, vmem_limit_bytes=VMEM_LIMIT
        ),
    )(*operands)


def unpack_kernel(tiles_ref, wtiles_ref, bias_out, qkv_out, proj_out):
    for j in range(81):
        rows = [tiles_ref[0, 16 * (third * 81 + j) : 16 * (third * 81 + j) + 16, :].astype(F32) for third in range(3)]
        for half in range(2):
            lanes = slice(half * 10368 + 128 * j, half * 10368 + 128 * j + 128)
            full = jnp.concatenate([part[8 * half : 8 * half + 8] for part in rows], axis=0)
            for window in range(4):
                bias_out[0, window // 2, window % 2, :, lanes] = full[6 * window : 6 * window + 6]
    for i in range(12):
        row = jnp.concatenate([wtiles_ref[0, 6 * i + j].astype(F32) for j in range(6)], axis=1)
        qkv_out[0, 16 * i : 16 * i + 16, :] = row[:, : 3 * C]
        proj_out[0, 16 * i : 16 * i + 16, :] = row[:, 3 * C :]


def unpack(tiles, wtiles):
    return pl.pallas_call(
        unpack_kernel,
        grid=(2,),
        out_shape=[
            jax.ShapeDtypeStruct((2, 2, 2, HEADS, WIN * WIN), F32),
            jax.ShapeDtypeStruct((2, C, 3 * C), F32),
            jax.ShapeDtypeStruct((2, C, C), F32),
        ],
        in_specs=[
            pl.BlockSpec((1, ROWS, 128), lambda l: (l, 0, 0)),
            pl.BlockSpec((1, 80, 16, 128), lambda l: (l, 0, 0, 0)),
        ],
        out_specs=[
            pl.BlockSpec((1, 2, 2, HEADS, WIN * WIN), lambda l: (l, 0, 0, 0, 0)),
            pl.BlockSpec((1, C, 3 * C), lambda l: (l, 0, 0)),
            pl.BlockSpec((1, C, C), lambda l: (l, 0, 0)),
        ],
        compiler_params=pltpu.CompilerParams(vmem_limit_bytes=VMEM_LIMIT),
    )(tiles, wtiles)


def to_cells(grid):
    return grid.transpose(1, 2, 0, 3).reshape(144, 4, C)


def shards(tokens, cotangent, w_qkv, w_proj, w_in, w_out, earth_bias):
    load, own, send, recv = _matrices()
    matrices = [jnp.asarray(m, BF16) for m in (load, own, send, recv, load.T, own.T, recv.T, send.T)]
    params = [w_qkv, w_proj, w_in, w_out.transpose(0, 2, 1)]
    grid, tiles, wtiles = run(to_cells(tokens), to_cells(cotangent), matrices, params, earth_bias)
    bias_grad, qkv_grad, proj_grad = unpack(tiles, wtiles)
    grid = grid.reshape(12, 12, 4, C).transpose(2, 0, 1, 3)
    return grid, qkv_grad, proj_grad, bias_grad


def solution(mesh):
    return jax.shard_map(
        shards,
        mesh=mesh,
        in_specs=(
            P(None, "lat", "lon", None),
            P(None, "lat", "lon", None),
            P(),
            P(),
            P(),
            P(),
            P(None, None, "lat", None, None),
        ),
        out_specs=(P(None, "lat", "lon", None), P(), P(), P(None, None, "lat", None, None)),
        check_vma=False,
    )
```

```python
import functools

import jax
import jax.numpy as jnp
import numpy as np
from jax import lax
from jax.experimental import pallas as pl
from jax.experimental.pallas import tpu as pltpu
from jax.sharding import PartitionSpec as P

F32 = jnp.float32
BF16 = jnp.bfloat16
C = 192
HEADS = 6
HD = 32
FF = 768
WIN = 144
TOK = 576
EPSILON = 1e-05
SCALE = HD ** (-0.5)
MESH = pl.DeviceIdType.MESH
E0, S0, D0, SEND = 0, 224, 304, 384
VMEM_LIMIT = 56 * 1024 * 1024
ZS = 8
PAIRS = 12
FLAT = 3888
ROWS = 4096


def _plain_index(level, row, col):
    window = (level // 2) * 2 + row // 6
    return window * WIN + (level % 2) * 72 + (row % 6) * 12 + col


def _matrices():
    load = np.zeros((TOK, TOK), np.float32)
    own = np.zeros((TOK, TOK), np.float32)
    send = np.zeros((SEND, TOK), np.float32)
    recv = np.zeros((TOK, SEND), np.float32)
    for level in range(4):
        for row in range(12):
            for col in range(12):
                here = _plain_index(level, row, col)
                load[here, (row * 12 + col) * 4 + level] = 1
                target_row, target_col = row - 3, col - 6
                target = _plain_index((level - 1) % 4, target_row % 12, target_col % 12)
                if target_row >= 0 and target_col >= 0:
                    own[target, here] = 1
                    continue
                if target_row >= 0:
                    slot = E0 + (level * 9 + row - 3) * 6 + col
                elif target_col >= 0:
                    slot = S0 + (level * 3 + row) * 6 + col - 6
                else:
                    slot = D0 + (level * 3 + row) * 6 + col
                send[slot, here] = 1
                recv[target, slot] = 1
    return load, own, send, recv


def nn(a, b):
    return jnp.dot(a, b, preferred_element_type=F32)


def nt(a, b):
    return lax.dot_general(a, b, (((1,), (1,)), ((), ())), preferred_element_type=F32)


def eye(n):
    rows = lax.broadcasted_iota(jnp.int32, (n, n), 0)
    cols = lax.broadcasted_iota(jnp.int32, (n, n), 1)
    return jnp.where(rows == cols, 1.0, 0.0).astype(BF16)


def flip(a, n):
    return nt(eye(n), a).astype(BF16)


def normalize(x):
    center = jnp.mean(x, axis=-1, keepdims=True)
    offset = x - center
    spread = jnp.mean(offset * offset, axis=-1, keepdims=True)
    inverse = lax.rsqrt(spread + EPSILON)
    return offset * inverse, inverse


def norm_back(x, upstream):
    normed, inverse = normalize(x)
    first = jnp.mean(upstream, axis=-1, keepdims=True)
    second = jnp.mean(upstream * normed, axis=-1, keepdims=True)
    return inverse * (upstream - first - normed * second)


def cumulative(x):
    return 0.5 * (1.0 + lax.erf(x * 0.7071067811865476))


def density(x):
    return 0.3989422804014327 * jnp.exp(-0.5 * x * x)


def rows_of(window):
    return pl.ds(pl.multiple_of(window * WIN, WIN), WIN)


def spread_bias(bias_ref, layer, lined, table):
    for window in range(4):
        for j in range(162):
            row = window * 18 + j // 9
            value = bias_ref[layer, window // 2, window % 2, :, 128 * j : 128 * j + 128]
            lined[row, j % 9 * 8 : j % 9 * 8 + HEADS, :] = value.astype(F32)
    rows = lax.broadcasted_iota(jnp.int32, (256, 256), 0)
    cols = lax.broadcasted_iota(jnp.int32, (256, 256), 1)
    for r in range(8):
        pick = jnp.where(jnp.logical_and(rows - cols == 16 * r, cols < WIN), 1.0, 0.0).astype(BF16)
        pair = [lined[:, 8 * (r + i) : 8 * (r + i) + 8, :].reshape(576, 128) for i in range(2)]
        placed = nn(jnp.concatenate(pair, axis=1).astype(BF16), pick)
        for part in range(2):
            half = placed[:, 128 * part : 128 * part + 128]
            for row in range(72):
                table[part][64 * row + 8 * r : 64 * row + 8 * r + 8, :] = half[8 * row : 8 * row + 8]


def head_bias(table, window, head):
    at = pl.ds(pl.multiple_of(window * WIN * 8, 8) + head, WIN, stride=8)
    return jnp.concatenate([table[0][at, :], table[1][at, :][:, 0:16]], axis=1)


def pack_bias(main, rest, out_ref):
    def flat(first):
        parts = []
        for r in range(8):
            at = pl.ds(pl.multiple_of(first * 192, 8) + 24 * r, 24)
            parts += [main[at, :], rest[at, :][:, :16]]
        return jnp.concatenate(parts, axis=1)

    def step(group, carry):
        top = flat(group)
        bottom = flat(group + 9)
        for third in range(3):
            both = jnp.concatenate(
                [top[8 * third : 8 * third + 8], bottom[8 * third : 8 * third + 8]], axis=0
            ).astype(BF16)
            for j in range(9):
                at = pl.multiple_of((third * 81 + group * 9 + j) * 16, 16)
                out_ref[pl.ds(at, 16), :] = both[:, 128 * j : 128 * j + 128]
        return carry

    lax.fori_loop(0, 9, step, 0)
    out_ref[FLAT:ROWS, :] = jnp.zeros((ROWS - FLAT, 128), BF16)


def pack_weights(wgrad, out_ref):
    for i in range(12):
        block = wgrad[16 * i : 16 * i + 16, :].astype(BF16)
        for j in range(6):
            out_ref[6 * i + j] = block[:, 128 * j : 128 * j + 128]
    out_ref[72:80] = jnp.zeros((8, 16, 128), BF16)


def attention_forward(window, qkv_ref, qkvt_ref, prob_ref, mixedt_ref, mixed_ref, biases, mask):

    qkv = qkv_ref[rows_of(window), :]
    qkvt_ref[window] = flip(qkv, 3 * C)
    for head in range(HEADS):
        lo = head * HD
        keys = qkvt_ref[window, C + lo : C + lo + HD, :]
        values = qkvt_ref[window, 2 * C + lo : 2 * C + lo + HD, :]
        scores = nn(qkv[:, lo : lo + HD], keys) * SCALE + head_bias(biases, window, head)
        weights = jnp.exp(scores)
        if mask is not None:
            weights = weights * mask
        probs = weights / jnp.sum(weights, axis=-1, keepdims=True)
        probs = probs.astype(BF16)
        prob_ref[window * HEADS + head] = probs
        mixedt_ref[window, lo : lo + HD, :] = nt(values, probs).astype(BF16)
    mixed_ref[rows_of(window), :] = flip(mixedt_ref[window], WIN)


def attention_backward(
    window, source_ref, qkvt_ref, prob_ref, mixedt_ref, mgrad_ref, grad_ref,
    w_qkv, w_proj, gradt, sgrad_ref, wgrad, table,
):
    mgrad = mgrad_ref[rows_of(window), :]
    wgrad[:, 3 * C :] += nn(mixedt_ref[window], mgrad)
    grad = grad_ref[rows_of(window), :]
    gt = nt(w_proj, mgrad).astype(BF16)
    for head in range(HEADS):
        lo = head * HD
        queries = qkvt_ref[window, lo : lo + HD, :]
        keys = qkvt_ref[window, C + lo : C + lo + HD, :]
        values = qkvt_ref[window, 2 * C + lo : 2 * C + lo + HD, :]
        probs = prob_ref[window * HEADS + head]
        pgrad = nn(grad[:, lo : lo + HD], values)
        vgrad = nn(gt[lo : lo + HD, :], probs)
        probs = probs.astype(F32)
        delta = jnp.sum(pgrad * probs, axis=-1, keepdims=True)
        sgrad = probs * (pgrad - delta)
        at = pl.ds(window * HEADS + head, WIN, stride=24)
        table[0][at, :] = sgrad[:, :128]
        table[1][at, :] = jnp.concatenate([sgrad[:, 128:], jnp.zeros((WIN, 112), F32)], axis=1)
        sround = sgrad.astype(BF16)
        gradt[lo : lo + HD, :] = (nt(keys, sround) * SCALE).astype(BF16)
        gradt[C + lo : C + lo + HD, :] = (nn(queries, sround) * SCALE).astype(BF16)
        gradt[2 * C + lo : 2 * C + lo + HD, :] = vgrad.astype(BF16)
    all_grad = gradt[...]
    sourcet = flip(source_ref[rows_of(window), :], C)
    wgrad[:, : 3 * C] += nt(sourcet, all_grad)
    sgradt = nn(w_qkv, all_grad).astype(BF16)
    sgrad_ref[rows_of(window), :] = flip(sgradt, WIN)


def mlp_back(middle, upstream, slope, w_in, w_outt):
    act_grad = nn(upstream, w_outt)
    pre_grad = (slope * act_grad).astype(BF16)
    ngrad = nt(pre_grad, w_in)
    return (upstream.astype(F32) + norm_back(middle.astype(F32), ngrad)).astype(BF16)


def region_mask(window):
    last_lat = lax.axis_index("lat") == lax.axis_size("lat") - 1

    def region(tokens):
        level = tokens // 72
        row = tokens // 12 % 6
        upper = jnp.where(window // 2 == 1, level, 0)
        lower = jnp.where(jnp.logical_and(last_lat, window % 2 == 1), row // 3, 0)
        return upper * 2 + lower

    queries = region(lax.broadcasted_iota(jnp.int32, (WIN, WIN), 0))
    keys = region(lax.broadcasted_iota(jnp.int32, (WIN, WIN), 1))
    return jnp.where(queries == keys, 1.0, 0.0)


def place():
    lat, lon = lax.axis_index("lat"), lax.axis_index("lon")
    return lat, lon, lax.rem(lon, ZS), lon // ZS


def neighbour(lat_steps, lon_steps):
    lats, lons = lax.axis_size("lat"), lax.axis_size("lon")
    lat, lon, _, _ = place()
    return lax.rem(lat + lat_steps + lats, lats), lax.rem(lon + lon_steps + lons, lons)


def remote(src, dst, send, recv, device):
    return pltpu.make_async_remote_copy(
        src_ref=src, dst_ref=dst, send_sem=send, recv_sem=recv, device_id=device, device_id_type=MESH
    )


def greet():
    barrier = pltpu.get_barrier_semaphore()
    for k in range(1, 16):
        for device in (neighbour(k, 0), neighbour(0, k)):
            pl.semaphore_signal(barrier, inc=1, device_id=device, device_id_type=MESH)
    for k in (-1, 1):
        pl.semaphore_signal(barrier, inc=1, device_id=neighbour(k, k), device_id_type=MESH)
    return barrier


def halo(src, dst, sign, send, recv):
    steps = [(0, sign, E0, S0), (sign, 0, S0, D0), (sign, sign, D0, SEND)]
    copies = []
    for i, (lat, lon, start, stop) in enumerate(steps):
        piece = pl.ds(start, stop - start)
        copy = remote(src.at[piece], dst.at[piece], send.at[i], recv.at[i], neighbour(lat, lon))
        copy.start()
        copies.append(copy)
    return copies


def wait_all(copies):
    for copy in copies:
        copy.wait()


class Ring:
    def __init__(self, rows, own, out, base, bufs, sems):
        self.rows, self.own, self.out, self.base = rows, own, out, base
        self.right_in, self.left_in, self.right_sum, self.left_sum = bufs
        self.sems = sems
        lat, lon, self.z, y = place()
        self.right = (lat, y * ZS + lax.rem(self.z + 1, ZS))
        self.left = (lat, y * ZS + lax.rem(self.z + ZS - 1, ZS))
        self.sums, self.gathers = [], []

    def chunk(self, steps):
        return pl.multiple_of(lax.rem(self.z + steps + 2 * ZS, ZS) * self.rows, self.rows)

    def send(self, kind, step, src, dst, device):
        copy = remote(src, dst, self.sems.at[kind, step], self.sems.at[kind + 1, step], device)
        copy.start()
        return copy

    def reduce(self, step):
        if step:
            for copy in self.sums[-1]:
                copy.wait_recv()
        now = []
        value = self.own(self.chunk(4 - step))
        if step:
            value = (value.astype(F32) + self.right_in[step - 1].astype(F32)).astype(BF16)
        self.right_sum[step] = value
        now.append(self.send(0, step, self.right_sum.at[step], self.right_in.at[step], self.right))
        if step < 3:
            value = self.own(self.chunk(step - 3))
            if step:
                value = (value.astype(F32) + self.left_in[step - 1].astype(F32)).astype(BF16)
            self.left_sum[step] = value
            now.append(self.send(2, step, self.left_sum.at[step], self.left_in.at[step], self.left))
        self.sums.append(now)

    def total(self):
        self.sums[3][0].wait_recv()
        return self.own(self.chunk(0)).astype(F32) + self.right_in[3].astype(F32) + self.left_in[2].astype(F32)

    def piece(self, steps):
        return self.out.at[pl.ds(pl.multiple_of(self.base + self.chunk(steps), self.rows), self.rows)]

    def gather(self, step):
        came = []
        if step:
            for copy in self.gathers[-1]:
                copy.wait_recv()
            came.append((step, self.piece(-step)))
            if step < 4:
                came.append((step + 4, self.piece(step)))
        if step < 4:
            now = [self.send(4, step, self.piece(-step), self.piece(-step), self.right)]
            if step < 3:
                now.append(self.send(6, step, self.piece(step), self.piece(step), self.left))
            self.gathers.append(now)
        return came

    def finish(self):
        for now in self.sums + self.gathers:
            for copy in now:
                copy.wait_send()


def sum_tiles(tiles, out, bufs, sems, y_sems):
    lat, lon, z, y = place()
    partner = (lat, (1 - y) * ZS + z)
    bufs_a, mine, other, bufs_b, half, half_in = bufs
    a = Ring(256, lambda at: tiles[pl.ds(at, 256)], out, 0, bufs_a, sems.at[0])
    base = 2048 + y * 1024
    b = Ring(128, lambda at: half[pl.ds(at, 128)], out, base, bufs_b, sems.at[1])
    away = pl.ds(pl.multiple_of(2048 + (1 - y) * 1024, 1024), 1024)
    here = pl.ds(pl.multiple_of(2048 + y * 1024, 1024), 1024)
    cross = remote(tiles.at[away], half_in, y_sems.at[0, 0], y_sems.at[1, 0], partner)
    cross.start()
    a.reduce(0)
    yield
    a.reduce(1)
    yield
    cross.wait_recv()
    half[...] = (tiles[here].astype(F32) + half_in[...].astype(F32)).astype(BF16)
    b.reduce(0)
    a.reduce(2)
    yield
    b.reduce(1)
    a.reduce(3)
    yield
    b.reduce(2)
    mine[...] = a.total().astype(BF16)
    swap = remote(mine, other, y_sems.at[0, 1], y_sems.at[1, 1], partner)
    swap.start()
    yield
    b.reduce(3)
    swap.wait_recv()
    a.piece(0)[...] = (mine[...].astype(F32) + other[...].astype(F32)).astype(BF16)
    a.gather(0)
    yield
    b.piece(0)[...] = b.total().astype(BF16)
    b.gather(0)
    shared = []

    def share(pieces):
        for slot, piece in pieces:
            copy = remote(piece, piece, y_sems.at[0, 2 + slot], y_sems.at[1, 2 + slot], partner)
            copy.start()
            shared.append(copy)

    share([(0, b.piece(0))])
    a.gather(1)
    yield
    share(b.gather(1))
    a.gather(2)
    yield
    share(b.gather(2))
    a.gather(3)
    yield
    share(b.gather(3))
    a.gather(4)
    yield
    share(b.gather(4))
    wait_all(shared)
    cross.wait_send()
    swap.wait_send()
    a.finish()
    b.finish()


def sum_weights(w, out, part, mid, owned, done, sems, first):
    lat, lon, _, _ = place()
    peers = range(1, 16)
    scatter = []
    for k in peers:
        to = neighbour(k, 0)
        copy = remote(w.at[pl.ds(to[0] * 5, 5)], part.at[k], sems.at[0, k], sems.at[1, k], to)
        copy.start()
        scatter.append(copy)
    yield
    total = w[pl.ds(lat * 5, 5)].astype(F32)
    for k, copy in enumerate(scatter, 1):
        copy.wait_recv()
        total = total + part[k].astype(F32)
    mid[...] = total.astype(BF16)

    def owner(index):
        return jnp.logical_and(index >= first, index < first + 5)

    def to_owner(k, device):
        tile = jnp.clip(device[1] - first, 0, 4)
        return remote(mid.at[tile], owned.at[k], sems.at[2, k], sems.at[3, k], device)

    def from_owner(k, tile, device):
        tile = jnp.clip(tile, 0, 4)
        return remote(done.at[tile], done.at[tile], sems.at[4, k], sems.at[5, k], device)

    for k in peers:
        to = neighbour(0, k)

        @pl.when(owner(to[1]))
        def _():
            to_owner(k, to).start()

    yield

    @pl.when(owner(lon))
    def _():
        mine = jnp.clip(lon - first, 0, 4)
        value = mid[mine].astype(F32)
        for k in peers:
            to_owner(k, (lat, lon)).wait_recv()
            value = value + owned[k].astype(F32)
        done[mine] = value.astype(BF16)
        for k in peers:
            from_owner(k, lon - first, neighbour(0, k)).start()

    yield
    for k in peers:
        source = neighbour(0, -k)

        @pl.when(owner(source[1]))
        def _():
            from_owner(k, source[1] - first, source).wait_recv()

    out[pl.ds(lat * 5, 5)] = done[...]
    spread = []
    for k in peers:
        piece = out.at[pl.ds(lat * 5, 5)]
        copy = remote(piece, piece, sems.at[6, k], sems.at[7, k], neighbour(k, 0))
        copy.start()
        spread.append(copy)
    yield
    wait_all(spread)
    for copy in scatter:
        copy.wait_send()
    for k in peers:
        to = neighbour(0, k)

        @pl.when(owner(to[1]))
        def _():
            to_owner(k, to).wait_send()

    @pl.when(owner(lon))
    def _():
        for k in peers:
            from_owner(k, lon - first, neighbour(0, k)).wait_send()


def advance(*streams):
    for stream in streams:
        next(stream, None)


def drain(fast, slow, rounds):
    step = 0
    while fast:
        fast = [stream for stream in fast if next(stream, 1) is None]
        if step in rounds:
            advance(*slow)
        step += 1
    while slow:
        slow = [stream for stream in slow if next(stream, 1) is None]


def kernel(
    tok_ref, cot_ref, load_ref, own_ref, send_ref, recv_ref, loadt_ref, ownt_ref, recvt_ref, sendt_ref,
    w_qkv, w_proj, w_in, w_outt, bias_ref,
    grid_out, bias_out, w_out,
    x0_s, source, qkv, qkvt, prob, mixedt, mixed, mid_s, slope_s, mgrad, grad, gradt, sgrad, wgrad,
    main24, rest24, lined, main, rest, tiles, wtiles, sent, arrived,
    halo_sems, a_right_in, a_left_in, a_right_sum, a_left_sum, mine, other,
    b_right_in, b_left_in, b_right_sum, b_left_sum, half, half_in, ring_sems, y_sems,
    wpart, wmid, wowned, wdone, w_sems,
):
    barrier = greet()
    lined[...] = jnp.zeros_like(lined)

    def forward(x, layer, masked):
        source[layer] = normalize(x)[0].astype(BF16)
        qkv[...] = nn(source[layer], w_qkv[layer]).astype(BF16)
        spread_bias(bias_ref, layer, lined, (main, rest))

        def step(window, carry):
            attention_forward(
                window, qkv, qkvt.at[layer], prob.at[layer], mixedt.at[layer], mixed, (main, rest),
                region_mask(window) if masked else None,
            )
            return carry

        lax.fori_loop(0, 4, step, 0)
        attended = nn(mixed[...], w_proj[layer]).astype(BF16)
        middle = (x + attended.astype(F32)).astype(BF16)
        pre = nn(normalize(middle.astype(F32))[0].astype(BF16), w_in[layer])
        phi = cumulative(pre)
        return middle, pre, phi, phi + pre * density(pre)

    def backward(window, layer):
        attention_backward(
            window, source.at[layer], qkvt.at[layer], prob.at[layer], mixedt.at[layer], mgrad, grad,
            w_qkv[layer], w_proj[layer], gradt, sgrad, wgrad, (main24, rest24),
        )

    def streams(layer):
        bufs_a = [ref.at[layer] for ref in (a_right_in, a_left_in, a_right_sum, a_left_sum)]
        bufs_b = [ref.at[layer] for ref in (b_right_in, b_left_in, b_right_sum, b_left_sum)]
        bufs = (bufs_a, mine.at[layer], other.at[layer], bufs_b, half.at[layer], half_in.at[layer])
        bias_sum = sum_tiles(tiles.at[layer], bias_out.at[layer], bufs, ring_sems.at[layer], y_sems.at[layer])
        weight_sum = sum_weights(
            wtiles.at[layer], w_out.at[layer], wpart.at[layer], wmid.at[layer], wowned.at[layer],
            wdone.at[layer], w_sems.at[layer], 8 * layer,
        )
        return bias_sum, weight_sum

    cot = nn(load_ref[...], cot_ref[...].reshape(TOK, C)).astype(BF16)
    sent[0] = nn(send_ref[...], cot).astype(BF16)
    pl.semaphore_wait(barrier, 32)
    cot_copies = halo(sent.at[0], arrived.at[0], -1, halo_sems.at[0, 0], halo_sems.at[0, 1])
    cot = nn(own_ref[...], cot)

    x0 = nn(load_ref[...], tok_ref[...].reshape(TOK, C))
    x0_s[...] = x0.astype(BF16)
    middle, pre, phi, slope = forward(x0, 0, False)
    mid_s[...] = middle
    slope_s[...] = slope
    x1 = (middle.astype(F32) + nt((pre * phi).astype(BF16), w_outt[0])).astype(BF16)
    sent[1] = nn(send_ref[...], x1).astype(BF16)
    x1_copies = halo(sent.at[1], arrived.at[1], -1, halo_sems.at[1, 0], halo_sems.at[1, 1])
    x1 = nn(own_ref[...], x1)

    wait_all(x1_copies)
    x1 = x1 + nn(recv_ref[...], arrived[1])
    middle, pre, phi, slope = forward(x1, 1, True)
    wait_all(cot_copies)
    cot = (cot + nn(recv_ref[...], arrived[0])).astype(BF16)
    mgrad[...] = mlp_back(middle, cot, slope, w_in[1], w_outt[1])
    grad[...] = nt(mgrad[...], w_proj[1]).astype(BF16)
    wgrad[...] = jnp.zeros_like(wgrad)

    def back(window, carry):
        backward(window, 1)
        return carry

    lax.fori_loop(0, 4, back, 0)
    result = (mgrad[...].astype(F32) + norm_back(x1, sgrad[...].astype(F32))).astype(BF16)
    sent[2] = nn(recvt_ref[...], result).astype(BF16)
    back_copies = halo(sent.at[2], arrived.at[2], 1, halo_sems.at[2, 0], halo_sems.at[2, 1])
    upstream = nn(ownt_ref[...], result)
    pack_bias(main24, rest24, tiles.at[1])
    pack_weights(wgrad, wtiles.at[1])
    bias1, weight1 = streams(1)
    advance(bias1, weight1)

    wait_all(back_copies)
    upstream = (upstream + nn(sendt_ref[...], arrived[2])).astype(BF16)
    mgrad[...] = mlp_back(mid_s[...], upstream, slope_s[...], w_in[0], w_outt[0])
    grad[...] = nt(mgrad[...], w_proj[0]).astype(BF16)
    wgrad[...] = jnp.zeros_like(wgrad)
    for window in range(4):
        backward(window, 0)
        if window % 2 == 0:
            advance(bias1)
    advance(weight1)
    pack_bias(main24, rest24, tiles.at[0])
    pack_weights(wgrad, wtiles.at[0])
    bias0, weight0 = streams(0)
    advance(bias0, weight0, bias1)
    result = (mgrad[...].astype(F32) + norm_back(x0_s[...].astype(F32), sgrad[...].astype(F32))).astype(BF16)
    grid_out[...] = nn(loadt_ref[...], result).astype(BF16).reshape(144, 4, C)
    drain([bias1, bias0], [weight1, weight0], (0, 2, 5, 7))


def run(tokens, cotangent, matrices, params, bias):
    vmem, dma = pltpu.VMEM, pltpu.SemaphoreType.DMA

    def ring(rows):
        return [vmem((2, n, rows, 128), BF16) for n in (4, 3, 4, 3)]

    tok = vmem((TOK, C), BF16)
    scratch = [
        tok,
        vmem((2, TOK, C), BF16),
        vmem((TOK, 3 * C), BF16),
        vmem((2, 4, 3 * C, WIN), BF16),
        vmem((2, 24, WIN, WIN), BF16),
        vmem((2, 4, C, WIN), BF16),
        tok,
        tok,
        vmem((TOK, FF), F32),
        tok,
        tok,
        vmem((3 * C, WIN), BF16),
        tok,
        vmem((C, FF), F32),
        vmem((WIN * 24, 128), F32),
        vmem((WIN * 24, 128), F32),
        vmem((72, 72, 128), F32),
        vmem((4 * WIN * 8 + 8, 128), F32),
        vmem((4 * WIN * 8 + 8, 128), F32),
        vmem((2, ROWS, 128), BF16),
        vmem((2, 80, 16, 128), BF16),
        vmem((3, SEND, C), BF16),
        vmem((3, SEND, C), BF16),
        dma((3, 2, 3)),
        *ring(256),
        vmem((2, 256, 128), BF16),
        vmem((2, 256, 128), BF16),
        *ring(128),
        vmem((2, 1024, 128), BF16),
        vmem((2, 1024, 128), BF16),
        dma((2, 2, 8, 4)),
        dma((2, 2, 10)),
        vmem((2, 16, 5, 16, 128), BF16),
        vmem((2, 5, 16, 128), BF16),
        vmem((2, 16, 16, 128), BF16),
        vmem((2, 5, 16, 128), BF16),
        dma((2, 8, 16)),
    ]
    operands = [tokens, cotangent, *matrices, *params, bias]
    return pl.pallas_call(
        kernel,
        out_shape=[
            jax.ShapeDtypeStruct((144, 4, C), BF16),
            jax.ShapeDtypeStruct((2, ROWS, 128), BF16),
            jax.ShapeDtypeStruct((2, 80, 16, 128), BF16),
        ],
        in_specs=[pl.BlockSpec(memory_space=vmem)] * len(operands),
        out_specs=[pl.BlockSpec(memory_space=vmem)] * 3,
        scratch_shapes=scratch,
        compiler_params=pltpu.CompilerParams(
            collective_id=0, has_side_effects=True, vmem_limit_bytes=VMEM_LIMIT
        ),
    )(*operands)


def unpack_kernel(tiles_ref, wtiles_ref, bias_out, qkv_out, proj_out):
    for j in range(81):
        rows = [tiles_ref[0, 16 * (third * 81 + j) : 16 * (third * 81 + j) + 16, :].astype(F32) for third in range(3)]
        for half in range(2):
            lanes = slice(half * 10368 + 128 * j, half * 10368 + 128 * j + 128)
            full = jnp.concatenate([part[8 * half : 8 * half + 8] for part in rows], axis=0)
            for window in range(4):
                bias_out[0, window // 2, window % 2, :, lanes] = full[6 * window : 6 * window + 6]
    for i in range(12):
        row = jnp.concatenate([wtiles_ref[0, 6 * i + j].astype(F32) for j in range(6)], axis=1)
        qkv_out[0, 16 * i : 16 * i + 16, :] = row[:, : 3 * C]
        proj_out[0, 16 * i : 16 * i + 16, :] = row[:, 3 * C :]


def unpack(tiles, wtiles):
    return pl.pallas_call(
        unpack_kernel,
        grid=(2,),
        out_shape=[
            jax.ShapeDtypeStruct((2, 2, 2, HEADS, WIN * WIN), F32),
            jax.ShapeDtypeStruct((2, C, 3 * C), F32),
            jax.ShapeDtypeStruct((2, C, C), F32),
        ],
        in_specs=[
            pl.BlockSpec((1, ROWS, 128), lambda l: (l, 0, 0)),
            pl.BlockSpec((1, 80, 16, 128), lambda l: (l, 0, 0, 0)),
        ],
        out_specs=[
            pl.BlockSpec((1, 2, 2, HEADS, WIN * WIN), lambda l: (l, 0, 0, 0, 0)),
            pl.BlockSpec((1, C, 3 * C), lambda l: (l, 0, 0)),
            pl.BlockSpec((1, C, C), lambda l: (l, 0, 0)),
        ],
        compiler_params=pltpu.CompilerParams(vmem_limit_bytes=VMEM_LIMIT),
    )(tiles, wtiles)


def to_cells(grid):
    return grid.transpose(1, 2, 0, 3).reshape(144, 4, C)


def shards(tokens, cotangent, w_qkv, w_proj, w_in, w_out, earth_bias):
    load, own, send, recv = _matrices()
    matrices = [jnp.asarray(m, BF16) for m in (load, own, send, recv, load.T, own.T, recv.T, send.T)]
    params = [w_qkv, w_proj, w_in, w_out.transpose(0, 2, 1)]
    grid, tiles, wtiles = run(to_cells(tokens), to_cells(cotangent), matrices, params, earth_bias)
    bias_grad, qkv_grad, proj_grad = unpack(tiles, wtiles)
    grid = grid.reshape(12, 12, 4, C).transpose(2, 0, 1, 3)
    return grid, qkv_grad, proj_grad, bias_grad


def solution(mesh):
    return jax.shard_map(
        shards,
        mesh=mesh,
        in_specs=(
            P(None, "lat", "lon", None),
            P(None, "lat", "lon", None),
            P(),
            P(),
            P(),
            P(),
            P(None, None, "lat", None, None),
        ),
        out_specs=(P(None, "lat", "lon", None), P(), P(), P(None, None, "lat", None, None)),
        check_vma=False,
    )
```

```python
import functools

import jax
import jax.numpy as jnp
import numpy as np
from jax import lax
from jax.experimental import pallas as pl
from jax.experimental.pallas import tpu as pltpu
from jax.sharding import PartitionSpec as P

F32 = jnp.float32
BF16 = jnp.bfloat16
C = 192
HEADS = 6
HD = 32
FF = 768
WIN = 144
TOK = 576
EPSILON = 1e-05
SCALE = HD ** (-0.5)
MESH = pl.DeviceIdType.MESH
E0, S0, D0, SEND = 0, 224, 304, 384
VMEM_LIMIT = 56 * 1024 * 1024
ZS = 8
PAIRS = 12
FLAT = 3888
ROWS = 4096


def _plain_index(level, row, col):
    window = (level // 2) * 2 + row // 6
    return window * WIN + (level % 2) * 72 + (row % 6) * 12 + col


def _matrices():
    load = np.zeros((TOK, TOK), np.float32)
    own = np.zeros((TOK, TOK), np.float32)
    send = np.zeros((SEND, TOK), np.float32)
    recv = np.zeros((TOK, SEND), np.float32)
    for level in range(4):
        for row in range(12):
            for col in range(12):
                here = _plain_index(level, row, col)
                load[here, (row * 12 + col) * 4 + level] = 1
                target_row, target_col = row - 3, col - 6
                target = _plain_index((level - 1) % 4, target_row % 12, target_col % 12)
                if target_row >= 0 and target_col >= 0:
                    own[target, here] = 1
                    continue
                if target_row >= 0:
                    slot = E0 + (level * 9 + row - 3) * 6 + col
                elif target_col >= 0:
                    slot = S0 + (level * 3 + row) * 6 + col - 6
                else:
                    slot = D0 + (level * 3 + row) * 6 + col
                send[slot, here] = 1
                recv[target, slot] = 1
    return load, own, send, recv


def nn(a, b):
    return jnp.dot(a, b, preferred_element_type=F32)


def nt(a, b):
    return lax.dot_general(a, b, (((1,), (1,)), ((), ())), preferred_element_type=F32)


def eye(n):
    rows = lax.broadcasted_iota(jnp.int32, (n, n), 0)
    cols = lax.broadcasted_iota(jnp.int32, (n, n), 1)
    return jnp.where(rows == cols, 1.0, 0.0).astype(BF16)


def flip(a, n):
    return nt(eye(n), a).astype(BF16)


def normalize(x):
    center = jnp.mean(x, axis=-1, keepdims=True)
    offset = x - center
    spread = jnp.mean(offset * offset, axis=-1, keepdims=True)
    inverse = lax.rsqrt(spread + EPSILON)
    return offset * inverse, inverse


def norm_back(x, upstream):
    normed, inverse = normalize(x)
    first = jnp.mean(upstream, axis=-1, keepdims=True)
    second = jnp.mean(upstream * normed, axis=-1, keepdims=True)
    return inverse * (upstream - first - normed * second)


def cumulative(x):
    return 0.5 * (1.0 + lax.erf(x * 0.7071067811865476))


def density(x):
    return 0.3989422804014327 * jnp.exp(-0.5 * x * x)


def rows_of(window):
    return pl.ds(pl.multiple_of(window * WIN, WIN), WIN)


def spread_bias(bias_ref, layer, lined, table):
    for window in range(4):
        for j in range(162):
            row = window * 18 + j // 9
            value = bias_ref[layer, window // 2, window % 2, :, 128 * j : 128 * j + 128]
            lined[row, j % 9 * 8 : j % 9 * 8 + HEADS, :] = value.astype(F32)
    rows = lax.broadcasted_iota(jnp.int32, (256, 256), 0)
    cols = lax.broadcasted_iota(jnp.int32, (256, 256), 1)
    for r in range(8):
        pick = jnp.where(jnp.logical_and(rows - cols == 16 * r, cols < WIN), 1.0, 0.0).astype(BF16)
        pair = [lined[:, 8 * (r + i) : 8 * (r + i) + 8, :].reshape(576, 128) for i in range(2)]
        placed = nn(jnp.concatenate(pair, axis=1).astype(BF16), pick)
        for part in range(2):
            half = placed[:, 128 * part : 128 * part + 128]
            for row in range(72):
                table[part][64 * row + 8 * r : 64 * row + 8 * r + 8, :] = half[8 * row : 8 * row + 8]


def head_bias(table, window, head):
    at = pl.ds(pl.multiple_of(window * WIN * 8, 8) + head, WIN, stride=8)
    return jnp.concatenate([table[0][at, :], table[1][at, :][:, 0:16]], axis=1)


def pack_bias(main, rest, out_ref):
    def flat(first):
        parts = []
        for r in range(8):
            at = pl.ds(pl.multiple_of(first * 192, 8) + 24 * r, 24)
            parts += [main[at, :], rest[at, :][:, :16]]
        return jnp.concatenate(parts, axis=1)

    def step(group, carry):
        top = flat(group)
        bottom = flat(group + 9)
        for third in range(3):
            both = jnp.concatenate(
                [top[8 * third : 8 * third + 8], bottom[8 * third : 8 * third + 8]], axis=0
            ).astype(BF16)
            for j in range(9):
                at = pl.multiple_of((third * 81 + group * 9 + j) * 16, 16)
                out_ref[pl.ds(at, 16), :] = both[:, 128 * j : 128 * j + 128]
        return carry

    lax.fori_loop(0, 9, step, 0)
    out_ref[FLAT:ROWS, :] = jnp.zeros((ROWS - FLAT, 128), BF16)


def pack_weights(wgrad, out_ref):
    for i in range(12):
        block = wgrad[16 * i : 16 * i + 16, :].astype(BF16)
        for j in range(6):
            out_ref[6 * i + j] = block[:, 128 * j : 128 * j + 128]
    out_ref[72:80] = jnp.zeros((8, 16, 128), BF16)


def attention_forward(window, qkv_ref, qkvt_ref, prob_ref, mixedt_ref, mixed_ref, biases, mask):

    qkv = qkv_ref[rows_of(window), :]
    qkvt_ref[window] = flip(qkv, 3 * C)
    for head in range(HEADS):
        lo = head * HD
        keys = qkvt_ref[window, C + lo : C + lo + HD, :]
        values = qkvt_ref[window, 2 * C + lo : 2 * C + lo + HD, :]
        scores = nn(qkv[:, lo : lo + HD], keys) * SCALE + head_bias(biases, window, head)
        weights = jnp.exp(scores)
        if mask is not None:
            weights = weights * mask
        probs = weights / jnp.sum(weights, axis=-1, keepdims=True)
        probs = probs.astype(BF16)
        prob_ref[window * HEADS + head] = probs
        mixedt_ref[window, lo : lo + HD, :] = nt(values, probs).astype(BF16)
    mixed_ref[rows_of(window), :] = flip(mixedt_ref[window], WIN)


def attention_backward(
    window, source_ref, qkvt_ref, prob_ref, mixedt_ref, mgrad_ref, grad_ref,
    w_qkv, w_proj, gradt, sgrad_ref, wgrad, table,
):
    mgrad = mgrad_ref[rows_of(window), :]
    wgrad[:, 3 * C :] += nn(mixedt_ref[window], mgrad)
    grad = grad_ref[rows_of(window), :]
    gt = nt(w_proj, mgrad).astype(BF16)
    for head in range(HEADS):
        lo = head * HD
        queries = qkvt_ref[window, lo : lo + HD, :]
        keys = qkvt_ref[window, C + lo : C + lo + HD, :]
        values = qkvt_ref[window, 2 * C + lo : 2 * C + lo + HD, :]
        probs = prob_ref[window * HEADS + head]
        pgrad = nn(grad[:, lo : lo + HD], values)
        vgrad = nn(gt[lo : lo + HD, :], probs)
        probs = probs.astype(F32)
        delta = jnp.sum(pgrad * probs, axis=-1, keepdims=True)
        sgrad = probs * (pgrad - delta)
        at = pl.ds(window * HEADS + head, WIN, stride=24)
        table[0][at, :] = sgrad[:, :128]
        table[1][at, :] = jnp.concatenate([sgrad[:, 128:], jnp.zeros((WIN, 112), F32)], axis=1)
        sround = sgrad.astype(BF16)
        gradt[lo : lo + HD, :] = (nt(keys, sround) * SCALE).astype(BF16)
        gradt[C + lo : C + lo + HD, :] = (nn(queries, sround) * SCALE).astype(BF16)
        gradt[2 * C + lo : 2 * C + lo + HD, :] = vgrad.astype(BF16)
    all_grad = gradt[...]
    sourcet = flip(source_ref[rows_of(window), :], C)
    wgrad[:, : 3 * C] += nt(sourcet, all_grad)
    sgradt = nn(w_qkv, all_grad).astype(BF16)
    sgrad_ref[rows_of(window), :] = flip(sgradt, WIN)


def mlp_back(middle, upstream, slope, w_in, w_outt):
    act_grad = nn(upstream, w_outt)
    pre_grad = (slope * act_grad).astype(BF16)
    ngrad = nt(pre_grad, w_in)
    return (upstream.astype(F32) + norm_back(middle.astype(F32), ngrad)).astype(BF16)


def region_mask(window):
    last_lat = lax.axis_index("lat") == lax.axis_size("lat") - 1

    def region(tokens):
        level = tokens // 72
        row = tokens // 12 % 6
        upper = jnp.where(window // 2 == 1, level, 0)
        lower = jnp.where(jnp.logical_and(last_lat, window % 2 == 1), row // 3, 0)
        return upper * 2 + lower

    queries = region(lax.broadcasted_iota(jnp.int32, (WIN, WIN), 0))
    keys = region(lax.broadcasted_iota(jnp.int32, (WIN, WIN), 1))
    return jnp.where(queries == keys, 1.0, 0.0)


def place():
    lat, lon = lax.axis_index("lat"), lax.axis_index("lon")
    return lat, lon, lax.rem(lon, ZS), lon // ZS


def neighbour(lat_steps, lon_steps):
    lats, lons = lax.axis_size("lat"), lax.axis_size("lon")
    lat, lon, _, _ = place()
    return lax.rem(lat + lat_steps + lats, lats), lax.rem(lon + lon_steps + lons, lons)


def remote(src, dst, send, recv, device):
    return pltpu.make_async_remote_copy(
        src_ref=src, dst_ref=dst, send_sem=send, recv_sem=recv, device_id=device, device_id_type=MESH
    )


def greet():
    barrier = pltpu.get_barrier_semaphore()
    for k in range(1, 16):
        for device in (neighbour(k, 0), neighbour(0, k)):
            pl.semaphore_signal(barrier, inc=1, device_id=device, device_id_type=MESH)
    for k in (-1, 1):
        pl.semaphore_signal(barrier, inc=1, device_id=neighbour(k, k), device_id_type=MESH)
    return barrier


def halo(src, dst, sign, send, recv):
    steps = [(0, sign, E0, S0), (sign, 0, S0, D0), (sign, sign, D0, SEND)]
    copies = []
    for i, (lat, lon, start, stop) in enumerate(steps):
        piece = pl.ds(start, stop - start)
        copy = remote(src.at[piece], dst.at[piece], send.at[i], recv.at[i], neighbour(lat, lon))
        copy.start()
        copies.append(copy)
    return copies


def wait_all(copies):
    for copy in copies:
        copy.wait()


class Ring:
    def __init__(self, rows, own, out, base, bufs, sems):
        self.rows, self.own, self.out, self.base = rows, own, out, base
        self.right_in, self.left_in, self.right_sum, self.left_sum = bufs
        self.sems = sems
        lat, lon, self.z, y = place()
        self.right = (lat, y * ZS + lax.rem(self.z + 1, ZS))
        self.left = (lat, y * ZS + lax.rem(self.z + ZS - 1, ZS))
        self.sums, self.gathers = [], []

    def chunk(self, steps):
        return pl.multiple_of(lax.rem(self.z + steps + 2 * ZS, ZS) * self.rows, self.rows)

    def send(self, kind, step, src, dst, device):
        copy = remote(src, dst, self.sems.at[kind, step], self.sems.at[kind + 1, step], device)
        copy.start()
        return copy

    def reduce(self, step):
        if step:
            for copy in self.sums[-1]:
                copy.wait_recv()
        now = []
        value = self.own(self.chunk(4 - step))
        if step:
            value = (value.astype(F32) + self.right_in[step - 1].astype(F32)).astype(BF16)
        self.right_sum[step] = value
        now.append(self.send(0, step, self.right_sum.at[step], self.right_in.at[step], self.right))
        if step < 3:
            value = self.own(self.chunk(step - 3))
            if step:
                value = (value.astype(F32) + self.left_in[step - 1].astype(F32)).astype(BF16)
            self.left_sum[step] = value
            now.append(self.send(2, step, self.left_sum.at[step], self.left_in.at[step], self.left))
        self.sums.append(now)

    def total(self):
        self.sums[3][0].wait_recv()
        return self.own(self.chunk(0)).astype(F32) + self.right_in[3].astype(F32) + self.left_in[2].astype(F32)

    def piece(self, steps):
        return self.out.at[pl.ds(pl.multiple_of(self.base + self.chunk(steps), self.rows), self.rows)]

    def gather(self, step):
        came = []
        if step:
            for copy in self.gathers[-1]:
                copy.wait_recv()
            came.append((step, self.piece(-step)))
            if step < 4:
                came.append((step + 4, self.piece(step)))
        if step < 4:
            now = [self.send(4, step, self.piece(-step), self.piece(-step), self.right)]
            if step < 3:
                now.append(self.send(6, step, self.piece(step), self.piece(step), self.left))
            self.gathers.append(now)
        return came

    def finish(self):
        for now in self.sums + self.gathers:
            for copy in now:
                copy.wait_send()


def sum_tiles(tiles, out, bufs, sems, y_sems):
    lat, lon, z, y = place()
    partner = (lat, (1 - y) * ZS + z)
    bufs_a, mine, other, bufs_b, half, half_in = bufs
    a = Ring(256, lambda at: tiles[pl.ds(at, 256)], out, 0, bufs_a, sems.at[0])
    base = 2048 + y * 1024
    b = Ring(128, lambda at: half[pl.ds(at, 128)], out, base, bufs_b, sems.at[1])
    away = pl.ds(pl.multiple_of(2048 + (1 - y) * 1024, 1024), 1024)
    here = pl.ds(pl.multiple_of(2048 + y * 1024, 1024), 1024)
    cross = remote(tiles.at[away], half_in, y_sems.at[0, 0], y_sems.at[1, 0], partner)
    cross.start()
    a.reduce(0)
    yield
    a.reduce(1)
    yield
    cross.wait_recv()
    half[...] = (tiles[here].astype(F32) + half_in[...].astype(F32)).astype(BF16)
    b.reduce(0)
    a.reduce(2)
    yield
    b.reduce(1)
    a.reduce(3)
    yield
    b.reduce(2)
    mine[...] = a.total().astype(BF16)
    swap = remote(mine, other, y_sems.at[0, 1], y_sems.at[1, 1], partner)
    swap.start()
    yield
    b.reduce(3)
    swap.wait_recv()
    a.piece(0)[...] = (mine[...].astype(F32) + other[...].astype(F32)).astype(BF16)
    a.gather(0)
    yield
    b.piece(0)[...] = b.total().astype(BF16)
    b.gather(0)
    shared = []

    def share(pieces):
        for slot, piece in pieces:
            copy = remote(piece, piece, y_sems.at[0, 2 + slot], y_sems.at[1, 2 + slot], partner)
            copy.start()
            shared.append(copy)

    share([(0, b.piece(0))])
    a.gather(1)
    yield
    share(b.gather(1))
    a.gather(2)
    yield
    share(b.gather(2))
    a.gather(3)
    yield
    share(b.gather(3))
    a.gather(4)
    yield
    share(b.gather(4))
    wait_all(shared)
    cross.wait_send()
    swap.wait_send()
    a.finish()
    b.finish()


def sum_weights(w, out, part, mid, owned, done, sems, first):
    lat, lon, _, _ = place()
    peers = range(1, 16)
    scatter = []
    for k in peers:
        to = neighbour(k, 0)
        copy = remote(w.at[pl.ds(to[0] * 5, 5)], part.at[k], sems.at[0, k], sems.at[1, k], to)
        copy.start()
        scatter.append(copy)
    yield
    total = w[pl.ds(lat * 5, 5)].astype(F32)
    for k, copy in enumerate(scatter, 1):
        copy.wait_recv()
        total = total + part[k].astype(F32)
    mid[...] = total.astype(BF16)

    def owner(index):
        return jnp.logical_and(index >= first, index < first + 5)

    def to_owner(k, device):
        tile = jnp.clip(device[1] - first, 0, 4)
        return remote(mid.at[tile], owned.at[k], sems.at[2, k], sems.at[3, k], device)

    def from_owner(k, tile, device):
        tile = jnp.clip(tile, 0, 4)
        return remote(done.at[tile], done.at[tile], sems.at[4, k], sems.at[5, k], device)

    for k in peers:
        to = neighbour(0, k)

        @pl.when(owner(to[1]))
        def _():
            to_owner(k, to).start()

    yield

    @pl.when(owner(lon))
    def _():
        mine = jnp.clip(lon - first, 0, 4)
        value = mid[mine].astype(F32)
        for k in peers:
            to_owner(k, (lat, lon)).wait_recv()
            value = value + owned[k].astype(F32)
        done[mine] = value.astype(BF16)
        for k in peers:
            from_owner(k, lon - first, neighbour(0, k)).start()

    yield
    for k in peers:
        source = neighbour(0, -k)

        @pl.when(owner(source[1]))
        def _():
            from_owner(k, source[1] - first, source).wait_recv()

    out[pl.ds(lat * 5, 5)] = done[...]
    spread = []
    for k in peers:
        piece = out.at[pl.ds(lat * 5, 5)]
        copy = remote(piece, piece, sems.at[6, k], sems.at[7, k], neighbour(k, 0))
        copy.start()
        spread.append(copy)
    yield
    wait_all(spread)
    for copy in scatter:
        copy.wait_send()
    for k in peers:
        to = neighbour(0, k)

        @pl.when(owner(to[1]))
        def _():
            to_owner(k, to).wait_send()

    @pl.when(owner(lon))
    def _():
        for k in peers:
            from_owner(k, lon - first, neighbour(0, k)).wait_send()


def advance(*streams):
    for stream in streams:
        next(stream, None)


def drain(fast, slow, rounds):
    step = 0
    while fast:
        fast = [stream for stream in fast if next(stream, 1) is None]
        if step in rounds:
            advance(*slow)
        step += 1
    while slow:
        slow = [stream for stream in slow if next(stream, 1) is None]


def kernel(
    tok_ref, cot_ref, load_ref, own_ref, send_ref, recv_ref, loadt_ref, ownt_ref, recvt_ref, sendt_ref,
    w_qkv, w_proj, w_in, w_outt, bias_ref,
    grid_out, bias_out, w_out,
    x0_s, source, qkv, qkvt, prob, mixedt, mixed, mid_s, slope_s, mgrad, grad, gradt, sgrad, wgrad,
    main24, rest24, lined, main, rest, tiles, wtiles, sent, arrived,
    halo_sems, a_right_in, a_left_in, a_right_sum, a_left_sum, mine, other,
    b_right_in, b_left_in, b_right_sum, b_left_sum, half, half_in, ring_sems, y_sems,
    wpart, wmid, wowned, wdone, w_sems,
):
    barrier = greet()
    lined[...] = jnp.zeros_like(lined)

    def forward(x, layer, masked):
        source[layer] = normalize(x)[0].astype(BF16)
        qkv[...] = nn(source[layer], w_qkv[layer]).astype(BF16)

        def step(window, carry):
            attention_forward(
                window, qkv, qkvt.at[layer], prob.at[layer], mixedt.at[layer], mixed, (main, rest),
                region_mask(window) if masked else None,
            )
            return carry

        lax.fori_loop(0, 4, step, 0)
        attended = nn(mixed[...], w_proj[layer]).astype(BF16)
        middle = (x + attended.astype(F32)).astype(BF16)
        pre = nn(normalize(middle.astype(F32))[0].astype(BF16), w_in[layer])
        phi = cumulative(pre)
        return middle, pre, phi, phi + pre * density(pre)

    def backward(window, layer):
        attention_backward(
            window, source.at[layer], qkvt.at[layer], prob.at[layer], mixedt.at[layer], mgrad, grad,
            w_qkv[layer], w_proj[layer], gradt, sgrad, wgrad, (main24, rest24),
        )

    def streams(layer):
        bufs_a = [ref.at[layer] for ref in (a_right_in, a_left_in, a_right_sum, a_left_sum)]
        bufs_b = [ref.at[layer] for ref in (b_right_in, b_left_in, b_right_sum, b_left_sum)]
        bufs = (bufs_a, mine.at[layer], other.at[layer], bufs_b, half.at[layer], half_in.at[layer])
        bias_sum = sum_tiles(tiles.at[layer], bias_out.at[layer], bufs, ring_sems.at[layer], y_sems.at[layer])
        weight_sum = sum_weights(
            wtiles.at[layer], w_out.at[layer], wpart.at[layer], wmid.at[layer], wowned.at[layer],
            wdone.at[layer], w_sems.at[layer], 8 * layer,
        )
        return bias_sum, weight_sum

    cot = nn(load_ref[...], cot_ref[...].reshape(TOK, C)).astype(BF16)
    sent[0] = nn(send_ref[...], cot).astype(BF16)
    pl.semaphore_wait(barrier, 32)
    cot_copies = halo(sent.at[0], arrived.at[0], -1, halo_sems.at[0, 0], halo_sems.at[0, 1])
    cot = nn(own_ref[...], cot)

    x0 = nn(load_ref[...], tok_ref[...].reshape(TOK, C))
    x0_s[...] = x0.astype(BF16)
    spread_bias(bias_ref, 0, lined, (main, rest))
    middle, pre, phi, slope = forward(x0, 0, False)
    mid_s[...] = middle
    slope_s[...] = slope
    x1 = (middle.astype(F32) + nt((pre * phi).astype(BF16), w_outt[0])).astype(BF16)
    sent[1] = nn(send_ref[...], x1).astype(BF16)
    x1_copies = halo(sent.at[1], arrived.at[1], -1, halo_sems.at[1, 0], halo_sems.at[1, 1])
    x1 = nn(own_ref[...], x1)
    spread_bias(bias_ref, 1, lined, (main, rest))
    wait_all(cot_copies)
    cot = (cot + nn(recv_ref[...], arrived[0])).astype(BF16)

    wait_all(x1_copies)
    x1 = x1 + nn(recv_ref[...], arrived[1])
    middle, pre, phi, slope = forward(x1, 1, True)
    mgrad[...] = mlp_back(middle, cot, slope, w_in[1], w_outt[1])
    grad[...] = nt(mgrad[...], w_proj[1]).astype(BF16)
    wgrad[...] = jnp.zeros_like(wgrad)

    def back(window, carry):
        backward(window, 1)
        return carry

    lax.fori_loop(0, 4, back, 0)
    result = (mgrad[...].astype(F32) + norm_back(x1, sgrad[...].astype(F32))).astype(BF16)
    sent[2] = nn(recvt_ref[...], result).astype(BF16)
    back_copies = halo(sent.at[2], arrived.at[2], 1, halo_sems.at[2, 0], halo_sems.at[2, 1])
    upstream = nn(ownt_ref[...], result)
    pack_bias(main24, rest24, tiles.at[1])
    pack_weights(wgrad, wtiles.at[1])
    bias1, weight1 = streams(1)
    advance(bias1, weight1)

    advance(bias1)
    advance(bias1)
    wait_all(back_copies)
    upstream = (upstream + nn(sendt_ref[...], arrived[2])).astype(BF16)
    mgrad[...] = mlp_back(mid_s[...], upstream, slope_s[...], w_in[0], w_outt[0])
    grad[...] = nt(mgrad[...], w_proj[0]).astype(BF16)
    wgrad[...] = jnp.zeros_like(wgrad)
    for window in range(4):
        backward(window, 0)
        advance(bias1 if window % 2 == 0 else weight1)
    pack_bias(main24, rest24, tiles.at[0])
    pack_weights(wgrad, wtiles.at[0])
    bias0, weight0 = streams(0)
    advance(bias0, weight0, bias1)
    result = (mgrad[...].astype(F32) + norm_back(x0_s[...].astype(F32), sgrad[...].astype(F32))).astype(BF16)
    grid_out[...] = nn(loadt_ref[...], result).astype(BF16).reshape(144, 4, C)
    drain([bias1, bias0], [weight1, weight0], (0, 2, 5, 7))


def run(tokens, cotangent, matrices, params, bias):
    vmem, dma = pltpu.VMEM, pltpu.SemaphoreType.DMA

    def ring(rows):
        return [vmem((2, n, rows, 128), BF16) for n in (4, 3, 4, 3)]

    tok = vmem((TOK, C), BF16)
    scratch = [
        tok,
        vmem((2, TOK, C), BF16),
        vmem((TOK, 3 * C), BF16),
        vmem((2, 4, 3 * C, WIN), BF16),
        vmem((2, 24, WIN, WIN), BF16),
        vmem((2, 4, C, WIN), BF16),
        tok,
        tok,
        vmem((TOK, FF), F32),
        tok,
        tok,
        vmem((3 * C, WIN), BF16),
        tok,
        vmem((C, FF), F32),
        vmem((WIN * 24, 128), F32),
        vmem((WIN * 24, 128), F32),
        vmem((72, 72, 128), F32),
        vmem((4 * WIN * 8 + 8, 128), F32),
        vmem((4 * WIN * 8 + 8, 128), F32),
        vmem((2, ROWS, 128), BF16),
        vmem((2, 80, 16, 128), BF16),
        vmem((3, SEND, C), BF16),
        vmem((3, SEND, C), BF16),
        dma((3, 2, 3)),
        *ring(256),
        vmem((2, 256, 128), BF16),
        vmem((2, 256, 128), BF16),
        *ring(128),
        vmem((2, 1024, 128), BF16),
        vmem((2, 1024, 128), BF16),
        dma((2, 2, 8, 4)),
        dma((2, 2, 10)),
        vmem((2, 16, 5, 16, 128), BF16),
        vmem((2, 5, 16, 128), BF16),
        vmem((2, 16, 16, 128), BF16),
        vmem((2, 5, 16, 128), BF16),
        dma((2, 8, 16)),
    ]
    operands = [tokens, cotangent, *matrices, *params, bias]
    return pl.pallas_call(
        kernel,
        out_shape=[
            jax.ShapeDtypeStruct((144, 4, C), BF16),
            jax.ShapeDtypeStruct((2, ROWS, 128), BF16),
            jax.ShapeDtypeStruct((2, 80, 16, 128), BF16),
        ],
        in_specs=[pl.BlockSpec(memory_space=vmem)] * len(operands),
        out_specs=[pl.BlockSpec(memory_space=vmem)] * 3,
        scratch_shapes=scratch,
        compiler_params=pltpu.CompilerParams(
            collective_id=0, has_side_effects=True, vmem_limit_bytes=VMEM_LIMIT
        ),
    )(*operands)


def unpack_kernel(tiles_ref, wtiles_ref, bias_out, qkv_out, proj_out):
    for j in range(81):
        rows = [tiles_ref[0, 16 * (third * 81 + j) : 16 * (third * 81 + j) + 16, :].astype(F32) for third in range(3)]
        for half in range(2):
            lanes = slice(half * 10368 + 128 * j, half * 10368 + 128 * j + 128)
            full = jnp.concatenate([part[8 * half : 8 * half + 8] for part in rows], axis=0)
            for window in range(4):
                bias_out[0, window // 2, window % 2, :, lanes] = full[6 * window : 6 * window + 6]
    for i in range(12):
        row = jnp.concatenate([wtiles_ref[0, 6 * i + j].astype(F32) for j in range(6)], axis=1)
        qkv_out[0, 16 * i : 16 * i + 16, :] = row[:, : 3 * C]
        proj_out[0, 16 * i : 16 * i + 16, :] = row[:, 3 * C :]


def unpack(tiles, wtiles):
    return pl.pallas_call(
        unpack_kernel,
        grid=(2,),
        out_shape=[
            jax.ShapeDtypeStruct((2, 2, 2, HEADS, WIN * WIN), F32),
            jax.ShapeDtypeStruct((2, C, 3 * C), F32),
            jax.ShapeDtypeStruct((2, C, C), F32),
        ],
        in_specs=[
            pl.BlockSpec((1, ROWS, 128), lambda l: (l, 0, 0)),
            pl.BlockSpec((1, 80, 16, 128), lambda l: (l, 0, 0, 0)),
        ],
        out_specs=[
            pl.BlockSpec((1, 2, 2, HEADS, WIN * WIN), lambda l: (l, 0, 0, 0, 0)),
            pl.BlockSpec((1, C, 3 * C), lambda l: (l, 0, 0)),
            pl.BlockSpec((1, C, C), lambda l: (l, 0, 0)),
        ],
        compiler_params=pltpu.CompilerParams(vmem_limit_bytes=VMEM_LIMIT),
    )(tiles, wtiles)


def to_cells(grid):
    return grid.transpose(1, 2, 0, 3).reshape(144, 4, C)


def shards(tokens, cotangent, w_qkv, w_proj, w_in, w_out, earth_bias):
    load, own, send, recv = _matrices()
    matrices = [jnp.asarray(m, BF16) for m in (load, own, send, recv, load.T, own.T, recv.T, send.T)]
    params = [w_qkv, w_proj, w_in, w_out.transpose(0, 2, 1)]
    grid, tiles, wtiles = run(to_cells(tokens), to_cells(cotangent), matrices, params, earth_bias)
    bias_grad, qkv_grad, proj_grad = unpack(tiles, wtiles)
    grid = grid.reshape(12, 12, 4, C).transpose(2, 0, 1, 3)
    return grid, qkv_grad, proj_grad, bias_grad


def solution(mesh):
    return jax.shard_map(
        shards,
        mesh=mesh,
        in_specs=(
            P(None, "lat", "lon", None),
            P(None, "lat", "lon", None),
            P(),
            P(),
            P(),
            P(),
            P(None, None, "lat", None, None),
        ),
        out_specs=(P(None, "lat", "lon", None), P(), P(), P(None, None, "lat", None, None)),
        check_vma=False,
    )
```
